256 devices in a mesh: lon: 16 (over y, x), lat: 8 (over z), lev: 2 (over core).
Axes of the slice: x: 4, y: 4, z: 8, core: 2. Of those that a mesh axis runs over, the one named last changes fastest.
Arguments:
- prognostic: float32 [3, 32, 256, 4096], P(None, 'lev', 'lat', 'lon'), may hold values from -6 to 6
- half_width: int32 [256], P('lat'), may hold values from 1 to 16, as said below
- filter_mask: int32 [256], P('lat'), may hold values from 0 to 1, as said below
- column_inverse: float32 [256, 32, 32], P('lat'), as said below
Outputs:
- new_state: float32 [3, 32, 256, 4096], P(None, 'lev', 'lat', 'lon')
The draws below stay inside these ranges and needn't reach their ends.
Inputs may be any that keep to these rules, and one draw needn't show every extreme that they name: half_width rises with a row's distance from the equator: it is 1 on the two rows beside the equator and 16 on the two polar rows; on every other row it lies within one of 1 + (15) times the row's distance from the equator in rows, divided by 256/2 - 1 and rounded down. `filter_mask`: 1 on every row whose distance from the equator in rows is at least a cut drawn between 64 and 3 * 256/8 (rounded down); each other row is 1 with one chance in eight. `column_inverse`: one matrix for each latitude row, applied to each column of winds: diagonal entries from 0.5 to 1.5, every other entry of magnitude at most 0.9 / sqrt(32).
All inputs are finite; a program needn't handle non-finite values.
Results may differ from the reference program's by a relative error of at most 0.000059.
Values sent between devices are 32-bit elements; how exact they have to be, the bound alone decides.
No kernel may reach another device: no remote copies, remote signals or barrier semaphores. Data moves between devices by JAX's collectives and lax.ppermute only.
A program may use at most 192 MiB of HBM per device.

```python
import jax
import jax.numpy as jnp
from jax import lax

NLON = 4096
LON_DEV = 256
NLAT = 256
NLEV = 32
HMAX = 16


def distance_rows():
    row_index = jnp.arange(NLAT)
    half_rows = NLAT // 2
    from_equator = jnp.where(row_index < half_rows, half_rows - 1 - row_index, row_index - half_rows)
    return (from_equator, half_rows)


def draw_half_width(key, part):
    key = jax.random.fold_in(key, 11)
    from_equator, half_rows = distance_rows()
    baseline = 1 + (HMAX - 1) * from_equator // max(half_rows - 1, 1)
    jitter = jax.random.randint(key, (NLAT,), -1, 2)
    widths = jnp.clip(baseline + jitter, 1, HMAX)
    widths = jnp.where(from_equator == half_rows - 1, HMAX, widths)
    widths = jnp.where(from_equator == 0, 1, widths)
    return widths.astype(jnp.int32)


def draw_filter_mask(key, part):
    key = jax.random.fold_in(key, 12)
    first, second = jax.random.split(key)
    from_equator, half_rows = distance_rows()
    cut_row = jax.random.randint(first, (), half_rows // 2, 3 * half_rows // 4 + 1)
    scattered = jax.random.randint(second, (NLAT,), 0, 8) == 0
    return jnp.where((from_equator >= cut_row) | scattered, 1, 0).astype(jnp.int32)


def draw_column_inverse(key, part):
    key = jax.random.fold_in(key, 13)
    first, second = jax.random.split(key)
    off_diagonal = jnp.clip(0.45 * jax.random.normal(first, (NLAT, NLEV, NLEV), jnp.float32), -0.9, 0.9)
    diagonal = jax.random.uniform(second, (NLAT, NLEV), jnp.float32, 0.5, 1.5)
    identity = jnp.eye(NLEV, dtype=jnp.float32)
    return identity * diagonal[:, :, None] + (1.0 - identity) * off_diagonal * NLEV ** (-0.5)


def block_levels(own_key, dims, pieces, smallest, largest):
    factor_of = 1.0
    for dim, parts in pieces:
        heights = jax.random.uniform(jax.random.fold_in(jax.random.fold_in(own_key, 6), dim), (parts,), jnp.float32, smallest / len(pieces), largest / len(pieces))
        factor_of = factor_of * jnp.repeat(jnp.exp(heights), dims[dim] // parts).reshape((-1,) + (1,) * (len(dims) - 1 - dim))
    return factor_of


def noise(rng, extent, width, bound, pieces=(), held_as=jnp.bfloat16):
    level = block_levels(rng, extent, pieces, -0.22, 0.18) if pieces else 1.0
    values = jax.random.normal(rng, extent, jnp.float32) * width * level
    return jnp.minimum(jnp.maximum(values, -bound), bound).astype(held_as)


def setup_inputs(seed: int = 0) -> dict:
    streams_of = jax.random.split(jax.random.key(seed), 5)
    return {
        "prognostic": noise(streams_of[0], (3, NLEV, NLAT, NLON), 1.0, 6.0, ((1, 2), (2, 8), (3, 16)), jnp.float32),
        "half_width": draw_half_width(jax.random.fold_in(streams_of[4], 71), 0),
        "filter_mask": draw_filter_mask(jax.random.fold_in(streams_of[4], 71), 0),
        "column_inverse": draw_column_inverse(jax.random.fold_in(streams_of[4], 71), 0),
    }


TIME_STEP = 0.5
VISCOSITY = 0.05
MERIDIONAL = 0.25


def latitudes(global_rows, row_total):
    latitude_angle = -0.5 * jnp.pi + (global_rows + 0.5) * jnp.pi / row_total
    return jnp.cos(latitude_angle), jnp.sin(latitude_angle)


def tendency(padded, cosine, sine):
    centre = padded[:, :, 1:-1, 1:-1]
    eastward = padded[:, :, 1:-1, 2:]
    westward = padded[:, :, 1:-1, :-2]
    northward = padded[:, :, 2:, 1:-1]
    southward = padded[:, :, :-2, 1:-1]
    zonal_factor = (0.25 / (cosine + 0.05))[:, None]
    coriolis = (0.5 * sine)[:, None]
    zonal_diff = eastward - westward
    merid_diff = northward - southward
    laplace_sum = eastward + westward + northward + southward - 4.0 * centre
    wind_east = -zonal_factor * zonal_diff[2] + coriolis * centre[1] + VISCOSITY * laplace_sum[0]
    wind_north = -MERIDIONAL * merid_diff[2] - coriolis * centre[0] + VISCOSITY * laplace_sum[1]
    height_tend = -zonal_factor * zonal_diff[0] - MERIDIONAL * merid_diff[1]
    return jnp.stack([wind_east, wind_north, height_tend])


def filter_weight(distance, half_cells, block_width):
    reach_cells = (half_cells * block_width).astype(jnp.float32)
    return jnp.where(2.0 * distance <= reach_cells, 1.0, 0.0)


def reference(prognostic, half_width, filter_mask, column_inverse):
    cosine, sine = latitudes(jnp.arange(NLAT).astype(jnp.float32), NLAT)
    padded = jnp.pad(prognostic, ((0, 0), (0, 0), (1, 1), (0, 0)))
    padded = jnp.concatenate([padded[..., -1:], padded, padded[..., :1]], axis=3)
    tendencies = tendency(padded, cosine, sine)
    offsets = jnp.arange(NLON)
    cycle_distance = jnp.minimum(offsets, NLON - offsets).astype(jnp.float32)
    kernel = filter_weight(cycle_distance[None, :], half_width[:, None], LON_DEV)
    kernel = kernel / jnp.sum(kernel, axis=1, keepdims=True)
    spectrum = jnp.fft.rfft(tendencies, axis=3) * jnp.fft.rfft(kernel, axis=1)[None, None]
    smooth = jnp.fft.irfft(spectrum, n=NLON, axis=3).astype(jnp.float32)
    chosen = jnp.where((filter_mask == 1)[None, None, :, None], smooth, tendencies)
    updated = prognostic + TIME_STEP * chosen
    blended = jnp.einsum("jlm,fmjx->fljx", column_inverse, updated[:2], precision=lax.Precision.HIGHEST)
    return jnp.concatenate([blended, updated[2:]], axis=0)
```

```python
import functools

import jax
import jax.numpy as jnp
from jax import lax
from jax.experimental import pallas as pl
from jax.experimental.pallas import tpu as pltpu
from jax.sharding import PartitionSpec as P

TIME_STEP = 0.5
VISCOSITY = 0.05
MERIDIONAL = 0.25
HALF = 128
VMEM_LIMIT = 32 * 1024 * 1024


def latitudes(global_rows, row_total):
    latitude_angle = -0.5 * jnp.pi + (global_rows + 0.5) * jnp.pi / row_total
    return (jnp.cos(latitude_angle), jnp.sin(latitude_angle))


def tendency_kernel(prog, zonal, coriolis, south, north, west, east, out, turn):
    _, levels, rows, width = prog.shape
    row_id = lax.broadcasted_iota(jnp.int32, (rows, width), 0)
    col_id = lax.broadcasted_iota(jnp.int32, (rows, width), 1)
    first_row, last_row = row_id == 0, row_id == rows - 1
    first_col, last_col = col_id == 0, col_id == width - 1
    zon, cor = zonal[...], coriolis[...]
    for l in range(levels):
        centre, dx, dy, sx, sy = [], [], [], [], []
        for f in range(3):
            c = f * levels + l
            here = prog[f, l]
            e = jnp.where(last_col, east[:, c : c + 1], pltpu.roll(here, width - 1, 1))
            w = jnp.where(first_col, west[:, c : c + 1], pltpu.roll(here, 1, 1))
            n = jnp.where(last_row, north[c : c + 1, :], pltpu.roll(here, rows - 1, 0))
            s = jnp.where(first_row, south[c : c + 1, :], pltpu.roll(here, 1, 0))
            centre.append(here)
            dx.append(e - w)
            dy.append(n - s)
            sx.append(e + w + n + s - 4.0 * here)
        tends = (
            -zon * dx[2] + cor * centre[1] + VISCOSITY * sx[0],
            -MERIDIONAL * dy[2] - cor * centre[0] + VISCOSITY * sx[1],
            -zon * dx[0] - MERIDIONAL * dy[1],
        )
        for f in range(3):
            for half in range(2):
                turn[f, half, l * rows : (l + 1) * rows, :] = tends[f][:, half * HALF : (half + 1) * HALF]
    for j in range(rows):
        for f in range(3):
            for half in range(2):
                out[j, f * levels : (f + 1) * levels, half * HALF : (half + 1) * HALF] = turn[
                    f, half, pl.ds(j, levels, stride=rows), :
                ]


def split3(x):
    hi = x.astype(jnp.bfloat16)
    rest = x - hi.astype(jnp.float32)
    mid = rest.astype(jnp.bfloat16)
    return hi, mid, (rest - mid.astype(jnp.float32)).astype(jnp.bfloat16)


def split2(x):
    hi = x.astype(jnp.bfloat16)
    return hi, (x - hi.astype(jnp.float32)).astype(jnp.bfloat16)


def mix_operand(matrix):
    hi, lo = split2(matrix)
    return jnp.concatenate([hi, hi, lo], axis=1)


def filter_kernel(
    own_row, half_width, filter_mask, tend, matrix, out, halves, parts
):
    blocks, lev_parts, chans, _ = tend.shape
    levels = chans // 3
    count = 2 * blocks
    both = lev_parts * chans
    row = own_row[0]
    reach = half_width[row]
    whole = reach == count // 2
    norm = jnp.where(whole, count * HALF, 2 * HALF * reach + 1).astype(jnp.float32)
    filtered = filter_mask[row] == 1
    edge_gain = jnp.where(whole, 0.0, 1.0).astype(jnp.float32)

    for g in range(count):
        b, half = divmod(g, 2)
        for part in range(lev_parts):
            halves[g, part * chans : (part + 1) * chans, :] = tend[b, part, :, half * HALF : (half + 1) * HALF]

    def add_half(i, total):
        return total + halves[lax.rem(i + count - reach, count)]

    window = lax.fori_loop(0, 2 * reach, add_half, jnp.zeros((both, HALF), jnp.float32))
    for g in range(count):
        ahead = halves[lax.rem(g + reach, count)]
        behind = halves[lax.rem(g + count - reach, count)]
        change = ahead - behind
        for k, (a, b) in enumerate(zip(split3(change), split3(window))):
            parts[k, g * both : (g + 1) * both, :HALF] = a
            parts[k, g * both : (g + 1) * both, HALF:] = b
        window = window + change

    src = lax.broadcasted_iota(jnp.int32, (2 * HALF, HALF), 0)
    dst = lax.broadcasted_iota(jnp.int32, (2 * HALF, HALF), 1)
    sums = jnp.where((src <= dst) | (src >= HALF), 1.0, 0.0).astype(jnp.bfloat16)
    mixer = mix_operand(matrix[0])
    group = 4
    scale = TIME_STEP / norm
    for g0 in range(0, count, group):
        lo, hi = g0 * both, (g0 + group) * both
        box = (
            jnp.dot(parts[2, lo:hi, :], sums, preferred_element_type=jnp.float32)
            + jnp.dot(parts[1, lo:hi, :], sums, preferred_element_type=jnp.float32)
            + jnp.dot(parts[0, lo:hi, :], sums, preferred_element_type=jnp.float32)
        )
        for pair in range(group // 2):
            b = g0 // 2 + pair
            steps = []
            for half in range(2):
                g = 2 * b + half
                at = (g - g0) * both
                behind = halves[lax.rem(g + count - reach, count)]
                smooth = (box[at : at + both] + edge_gain * behind) * scale
                steps.append(jnp.where(filtered, smooth, TIME_STEP * halves[g]))
            step = jnp.concatenate(steps, axis=1)
            for f in range(2):
                wind = jnp.concatenate(
                    [step[p * chans + f * levels : p * chans + (f + 1) * levels] for p in range(lev_parts)], axis=0
                )
                wind_hi, wind_lo = split2(wind)
                mixed = jnp.dot(
                    mixer,
                    jnp.concatenate([wind_hi, wind_lo, wind_hi], axis=0),
                    preferred_element_type=jnp.float32,
                )
                for p in range(lev_parts):
                    out[b, p, f * levels : (f + 1) * levels, :] = mixed[p * levels : (p + 1) * levels]
            for p in range(lev_parts):
                out[b, p, 2 * levels :, :] = step[p * chans + 2 * levels : (p + 1) * chans]


def mix_kernel(own_part, own, other, matrix, out):
    _, levels, rows, width = own.shape
    mine = own.reshape(2, levels * rows, width)
    theirs = other.reshape(2, levels * rows, width)
    lower = own_part[0] == 0
    for j in range(rows):
        mixer = mix_operand(matrix[j])
        winds = []
        for f in range(2):
            a = mine[f, pl.ds(j, levels, stride=rows), :]
            b = theirs[f, pl.ds(j, levels, stride=rows), :]
            winds.append(jnp.concatenate([jnp.where(lower, a, b), jnp.where(lower, b, a)], axis=0))
        wind_hi, wind_lo = split2(jnp.concatenate(winds, axis=1))
        mixed = jnp.dot(
            mixer, jnp.concatenate([wind_hi, wind_lo, wind_hi], axis=0), preferred_element_type=jnp.float32
        )
        kept = jnp.where(lower, mixed[:levels], mixed[levels:])
        for f in range(2):
            out[j, f * levels : (f + 1) * levels, :] = kept[:, f * width : (f + 1) * width]


def finish_kernel(step, mixed, height, out):
    _, levels, rows, width = out.shape
    flat = out.reshape(3, levels * rows, width)
    for j in range(rows):
        for f in range(2):
            at = slice(f * levels, (f + 1) * levels)
            flat[f, pl.ds(j, levels, stride=rows), :] = step[j, at, :] + mixed[j, at, :]
        flat[2, pl.ds(j, levels, stride=rows), :] = step[j, 2 * levels :, :]
    out[2] = out[2] + height[0]


def per_device(prognostic, half_width, filter_mask, column_inverse):
    fields, levels, rows, width = prognostic.shape
    lon_devices, lat_devices, lev_devices = (lax.axis_size(a) for a in ("lon", "lat", "lev"))
    lon_index, lat_index, lev_index = (lax.axis_index(a) for a in ("lon", "lat", "lev"))
    chans = fields * levels
    params = pltpu.CompilerParams(vmem_limit_bytes=VMEM_LIMIT)

    east_edge = prognostic[:, :, :, width - 1].reshape(chans, rows).T
    west_edge = prognostic[:, :, :, 0].reshape(chans, rows).T
    west = lax.ppermute(east_edge, "lon", [(i, (i + 1) % lon_devices) for i in range(lon_devices)])
    east = lax.ppermute(west_edge, "lon", [((i + 1) % lon_devices, i) for i in range(lon_devices)])
    south = lax.ppermute(
        prognostic[:, :, rows - 1, :].reshape(chans, width), "lat", [(i, i + 1) for i in range(lat_devices - 1)]
    )
    north = lax.ppermute(
        prognostic[:, :, 0, :].reshape(chans, width), "lat", [(i + 1, i) for i in range(lat_devices - 1)]
    )
    other = lax.ppermute(prognostic[:2], "lev", [(0, 1), (1, 0)])

    global_rows = (lat_index * rows + jnp.arange(rows)).astype(jnp.float32)
    cosine, sine = latitudes(global_rows, rows * lat_devices)
    zonal = jnp.broadcast_to((0.25 / (cosine + 0.05))[:, None], (rows, width))
    coriolis = jnp.broadcast_to((0.5 * sine)[:, None], (rows, width))

    with jax.named_scope("tendencies"):
        tend = pl.pallas_call(
            tendency_kernel,
            out_shape=jax.ShapeDtypeStruct((rows, chans, width), jnp.float32),
            scratch_shapes=[pltpu.VMEM((fields, 2, levels * rows, HALF), jnp.float32)],
            compiler_params=params,
        )(prognostic, zonal, coriolis, south, north, west, east)

    whole_rows = lax.all_to_all(tend, ("lon", "lev"), 0, 0, tiled=True)

    own_row = (lon_index * lev_devices + lev_index).astype(jnp.int32).reshape(1)
    blocked = (lon_devices, lev_devices, chans, width)
    count = 2 * lon_devices
    both = lev_devices * chans
    with jax.named_scope("row_filter"):
        stepped = pl.pallas_call(
            filter_kernel,
            out_shape=jax.ShapeDtypeStruct(blocked, jnp.float32),
            grid_spec=pltpu.PrefetchScalarGridSpec(
                num_scalar_prefetch=3,
                grid=(1,),
                in_specs=[
                    pl.BlockSpec(blocked, lambda i, *_: (0, 0, 0, 0)),
                    pl.BlockSpec(
                        (1,) + column_inverse.shape[1:], lambda i, own_row, *_: (own_row[0], 0, 0)
                    ),
                ],
                out_specs=pl.BlockSpec(blocked, lambda i, *_: (0, 0, 0, 0)),
                scratch_shapes=[
                    pltpu.VMEM((count, both, HALF), jnp.float32),
                    pltpu.VMEM((3, count * both, 2 * HALF), jnp.bfloat16),
                ],
            ),
            compiler_params=params,
        )(own_row, half_width, filter_mask, whole_rows.reshape(blocked), column_inverse)

    returned = lax.all_to_all(
        stepped.reshape(rows, chans, width), ("lon", "lev"), 0, 0, tiled=True
    )

    tile = (levels, rows, HALF)
    with jax.named_scope("wind_mix"):
        mixed = pl.pallas_call(
            mix_kernel,
            out_shape=jax.ShapeDtypeStruct((rows, 2 * levels, width), jnp.float32),
            grid_spec=pltpu.PrefetchScalarGridSpec(
                num_scalar_prefetch=1,
                grid=(width // HALF,),
                in_specs=[
                    pl.BlockSpec((2,) + tile, lambda i, *_: (0, 0, 0, i)),
                    pl.BlockSpec((2,) + tile, lambda i, *_: (0, 0, 0, i)),
                    pl.BlockSpec(column_inverse.shape, lambda i, *_: (0, 0, 0)),
                ],
                out_specs=pl.BlockSpec((rows, 2 * levels, HALF), lambda i, *_: (0, 0, i)),
            ),
            compiler_params=params,
        )(lev_index.astype(jnp.int32).reshape(1), prognostic, other, column_inverse)

    with jax.named_scope("finish"):
        return pl.pallas_call(
            finish_kernel,
            out_shape=jax.ShapeDtypeStruct(prognostic.shape, jnp.float32),
            grid=(width // HALF,),
            in_specs=[
                pl.BlockSpec((rows, chans, HALF), lambda i: (0, 0, i)),
                pl.BlockSpec((rows, 2 * levels, HALF), lambda i: (0, 0, i)),
                pl.BlockSpec((1,) + tile, lambda i: (2, 0, 0, i)),
            ],
            out_specs=pl.BlockSpec((fields,) + tile, lambda i: (0, 0, 0, i)),
            compiler_params=params,
        )(returned, mixed, prognostic)


def solution(mesh):
    placed = (P(None, "lev", "lat", "lon"), P("lat"), P("lat"), P("lat", None, None))
    return jax.shard_map(
        per_device,
        mesh=mesh,
        in_specs=placed,
        out_specs=P(None, "lev", "lat", "lon"),
        check_vma=False,
    )
```

```python
import jax
import jax.numpy as jnp
from jax import lax
from jax.experimental import pallas as pl
from jax.experimental.pallas import tpu as pltpu
from jax.sharding import PartitionSpec as P

TIME_STEP = 0.5
VISCOSITY = 0.05
MERIDIONAL = 0.25
HALF = 128
SUBLANES = 8
VMEM_LIMIT = 32 * 1024 * 1024
CHUNKS = 4
GROUP = 4


def latitudes(global_rows, row_total):
    latitude_angle = -0.5 * jnp.pi + (global_rows + 0.5) * jnp.pi / row_total
    return (jnp.cos(latitude_angle), jnp.sin(latitude_angle))


def tendency_kernel(prog, zonal, coriolis, out, ends, tile, turn, edges, stage, in_sems, out_sems):
    _, levels, rows, width = prog.shape
    chans = 3 * levels
    payload = 2 * chans
    per_chunk = levels // CHUNKS
    loads = []
    for chunk in range(CHUNKS):
        some = pl.ds(chunk * per_chunk, per_chunk)
        loads.append(pltpu.make_async_copy(prog.at[:, some], tile.at[:, some], in_sems.at[chunk]))
        loads[-1].start()
    row_id = lax.broadcasted_iota(jnp.int32, (rows, width), 0)
    col_id = lax.broadcasted_iota(jnp.int32, (rows, width), 1)
    lane_id = lax.broadcasted_iota(jnp.int32, (rows, HALF), 1)
    first_row, last_row = row_id == 0, row_id == rows - 1
    first_col, last_col = col_id == 0, col_id == width - 1
    zon, cor = zonal[...], coriolis[...]
    edge_rows = jnp.zeros((rows, HALF), jnp.float32)
    for l in range(levels):
        if l % per_chunk == 0:
            loads[l // per_chunk].wait()
        centre, dx, dy, sx = [], [], [], []
        for f in range(3):
            c = f * levels + l
            here = tile[f, l]
            e = jnp.where(last_col, 0.0, pltpu.roll(here, width - 1, 1))
            w = jnp.where(first_col, 0.0, pltpu.roll(here, 1, 1))
            n = jnp.where(last_row, 0.0, pltpu.roll(here, rows - 1, 0))
            s = jnp.where(first_row, 0.0, pltpu.roll(here, 1, 0))
            centre.append(here)
            dx.append(e - w)
            dy.append(n - s)
            sx.append(e + w + n + s - 4.0 * here)
            first = here[:, :HALF]
            last = here[:, width - HALF :]
            if c:
                first = pltpu.roll(first, c, 1)
            last = pltpu.roll(last, (chans + c + 1) % HALF, 1)
            edge_rows = jnp.where(lane_id == c, first, jnp.where(lane_id == chans + c, last, edge_rows))
        tends = (
            -zon * dx[2] + cor * centre[1] + VISCOSITY * sx[0],
            -MERIDIONAL * dy[2] - cor * centre[0] + VISCOSITY * sx[1],
            -zon * dx[0] - MERIDIONAL * dy[1],
        )
        for f in range(3):
            for half in range(2):
                turn[f, half, l * rows : (l + 1) * rows, :] = tends[f][:, half * HALF : (half + 1) * HALF]
    edges[...] = edge_rows
    per_chunk = rows // CHUNKS
    copies = []
    for chunk in range(CHUNKS):
        for j in range(chunk * per_chunk, (chunk + 1) * per_chunk):
            for f in range(3):
                for half in range(2):
                    at = (2 * f + half) * levels
                    value = turn[f, half, pl.ds(j, levels, stride=rows), :]
                    stage[j, at : at + levels, :] = value
                    if j in (0, rows - 1):
                        ends[min(j, 1), at : at + levels, :] = value
            stage[j, payload:, :] = jnp.broadcast_to(edges[j : j + 1, :], (SUBLANES, HALF))
        some = pl.ds(chunk * per_chunk, per_chunk)
        copies.append(pltpu.make_async_copy(stage.at[some], out.at[some], out_sems.at[chunk]))
        copies[-1].start()
    for copy in copies:
        copy.wait()


def seam_kernel(ends, south, north, tend, out, stage, sems):
    del tend
    chans = south.shape[0]
    levels = chans // 3
    copies = []
    for at, beyond, sign in ((0, south, -1.0), (1, north, 1.0)):
        for half in range(2):
            lanes = slice(half * HALF, (half + 1) * HALF)
            u, v, h = (beyond[f * levels : (f + 1) * levels, lanes] for f in range(3))
            slope = sign * MERIDIONAL
            for f, term in enumerate((VISCOSITY * u, VISCOSITY * v - slope * h, -slope * v)):
                some = slice((2 * f + half) * levels, (2 * f + half + 1) * levels)
                stage[at, some, :] = ends[at, some, :] + term
        row = at * (out.shape[0] - 1)
        copies.append(pltpu.make_async_copy(stage.at[at], out.at[row, pl.ds(0, 2 * chans)], sems.at[at]))
        copies[-1].start()
    for copy in copies:
        copy.wait()


def split2(x):
    hi = x.astype(jnp.bfloat16)
    return hi, (x - hi.astype(jnp.float32)).astype(jnp.bfloat16)


def mix_operand(matrix):
    hi, lo = split2(matrix)
    return jnp.concatenate([hi, hi, lo], axis=1)


def filter_kernel(
    own_row, half_width, filter_mask, zonal, tend, matrices, out, halves, parts, seam, matrix, stage, matrix_sem, sems
):
    blocks, lev_parts, levels = out.shape[0], out.shape[1], out.shape[4]
    chans = 3 * levels
    payload = 2 * chans
    count = 2 * blocks
    both = lev_parts * chans
    row = own_row[0]
    fetch = pltpu.make_async_copy(matrices.at[row], matrix, matrix_sem)
    fetch.start()
    reach = half_width[row]
    whole = reach == count // 2
    norm = jnp.where(whole, count * HALF, 2 * HALF * reach + 1).astype(jnp.float32)
    filtered = filter_mask[row] == 1
    edge_gain = jnp.where(whole, 0.0, 1.0).astype(jnp.float32)

    for b in range(blocks):
        for part in range(lev_parts):
            at = b * lev_parts + part
            seam[at : at + 1, :] = tend[b, part, payload : payload + 1, :]
    columns = seam[...].T
    zon = zonal[row]
    u, v, h = (columns[f * levels : (f + 1) * levels] for f in range(3))
    from_east = jnp.concatenate([VISCOSITY * u - zon * h, VISCOSITY * v, -zon * u], axis=0)
    u, v, h = (columns[chans + f * levels : chans + (f + 1) * levels] for f in range(3))
    from_west = jnp.concatenate([VISCOSITY * u + zon * h, VISCOSITY * v, zon * u], axis=0)
    lane_id = lax.broadcasted_iota(jnp.int32, (levels, HALF), 1)
    window = jnp.zeros((both, HALF), jnp.float32)
    for g in range(count):
        b, half = divmod(g, 2)
        beyond = (b + 1) % blocks if half else (b + blocks - 1) % blocks
        terms, lane = (from_east, HALF - 1) if half else (from_west, 0)
        pieces = []
        for part in range(lev_parts):
            source = beyond * lev_parts + part
            for f in range(3):
                here = tend[b, part, (2 * f + half) * levels : (2 * f + half + 1) * levels, :]
                term = terms[f * levels : (f + 1) * levels, source : source + 1]
                pieces.append(here + jnp.where(lane_id == lane, term, 0.0))
        value = jnp.concatenate(pieces, axis=0)
        halves[g] = value
        inside = lax.rem(g + reach, count) < 2 * reach
        window = window + jnp.where(inside, 1.0, 0.0).astype(jnp.float32) * value

    src = lax.broadcasted_iota(jnp.int32, (2 * HALF, HALF), 0)
    dst = lax.broadcasted_iota(jnp.int32, (2 * HALF, HALF), 1)
    sums = jnp.where((src <= dst) | (src >= HALF), 1.0, 0.0).astype(jnp.bfloat16)
    fetch.wait()
    mixer = mix_operand(matrix[...])
    scale = TIME_STEP / norm

    def split_group(g0, window):
        for g in range(g0, g0 + GROUP):
            ahead = halves[lax.rem(g + reach, count)]
            behind = halves[lax.rem(g + count - reach, count)]
            change = ahead - behind
            for k, (a, b) in enumerate(zip(split2(change), split2(window))):
                parts[k, g * both : (g + 1) * both, :HALF] = a
                parts[k, g * both : (g + 1) * both, HALF:] = b
            window = window + change
        return window

    copies = []

    def finish_group(g0):
        lo, hi = g0 * both, (g0 + GROUP) * both
        box = jnp.dot(parts[1, lo:hi, :], sums, preferred_element_type=jnp.float32) + jnp.dot(
            parts[0, lo:hi, :], sums, preferred_element_type=jnp.float32
        )
        for pair in range(GROUP // 2):
            b = g0 // 2 + pair
            steps = []
            for half in range(2):
                g = 2 * b + half
                at = (g - g0) * both
                behind = halves[lax.rem(g + count - reach, count)]
                smooth = (box[at : at + both] + edge_gain * behind) * scale
                step = jnp.where(filtered, smooth, TIME_STEP * halves[g])
                for p in range(lev_parts):
                    stage[b, p, 2, half] = step[p * chans + 2 * levels : (p + 1) * chans]
                steps.append(step)
            step = jnp.concatenate(steps, axis=1)
            for f in range(2):
                wind = jnp.concatenate(
                    [step[p * chans + f * levels : p * chans + (f + 1) * levels] for p in range(lev_parts)], axis=0
                )
                wind_hi, wind_lo = split2(wind)
                mixed = jnp.dot(
                    mixer,
                    jnp.concatenate([wind_hi, wind_lo, wind_hi], axis=0),
                    preferred_element_type=jnp.float32,
                )
                for p in range(lev_parts):
                    for half in range(2):
                        stage[b, p, f, half] = mixed[
                            p * levels : (p + 1) * levels, half * HALF : (half + 1) * HALF
                        ]
            copies.append(pltpu.make_async_copy(stage.at[b], out.at[b], sems.at[b]))
            copies[-1].start()

    window = split_group(0, window)
    for g0 in range(0, count, GROUP):
        if g0 + GROUP < count:
            window = split_group(g0 + GROUP, window)
        finish_group(g0)
    for copy in copies:
        copy.wait()


def base_kernel(own_part, own, other, matrix, out):
    _, levels, rows, width = own.shape
    mine = own.reshape(3, levels * rows, width)
    theirs = other.reshape(2, levels * rows, width)
    lower = own_part[0] == 0
    for j in range(rows):
        mixer = mix_operand(matrix[j])
        winds = []
        for f in range(2):
            a = mine[f, pl.ds(j, levels, stride=rows), :]
            b = theirs[f, pl.ds(j, levels, stride=rows), :]
            winds.append(jnp.concatenate([jnp.where(lower, a, b), jnp.where(lower, b, a)], axis=0))
        wind_hi, wind_lo = split2(jnp.concatenate(winds, axis=1))
        mixed = jnp.dot(
            mixer, jnp.concatenate([wind_hi, wind_lo, wind_hi], axis=0), preferred_element_type=jnp.float32
        )
        kept = jnp.where(lower, mixed[:levels], mixed[levels:])
        for f in range(2):
            out[j, f, 0] = kept[:, f * width : (f + 1) * width]
        out[j, 2, 0] = mine[2, pl.ds(j, levels, stride=rows), :]


def finish_kernel(step, base, out, added, stage, in_sems, out_sems):
    fields, levels, rows, _ = out.shape
    loads, copies = [], []
    for f in range(fields):
        loads.append(pltpu.make_async_copy(base.at[:, f], added.at[f], in_sems.at[f]))
        loads[-1].start()
    for f in range(fields):
        loads[f].wait()
        for half in range(2):
            for j in range(rows):
                stage[f, half, pl.ds(j, levels, stride=rows), :] = step[j, f, half] + added[f, j, half]
            copies.append(
                pltpu.make_async_copy(
                    stage.at[f, half].reshape(levels, rows, HALF),
                    out.at[f, :, :, pl.ds(half * HALF, HALF)],
                    out_sems.at[2 * f + half],
                )
            )
            copies[-1].start()
    for copy in copies:
        copy.wait()


def per_device(prognostic, half_width, filter_mask, column_inverse):
    fields, levels, rows, width = prognostic.shape
    lon_devices, lat_devices, lev_devices = (lax.axis_size(a) for a in ("lon", "lat", "lev"))
    lon_index, lat_index, lev_index = (lax.axis_index(a) for a in ("lon", "lat", "lev"))
    chans = fields * levels
    halves = width // HALF
    params = pltpu.CompilerParams(vmem_limit_bytes=VMEM_LIMIT)
    hbm = pl.BlockSpec(memory_space=pltpu.HBM)
    vmem = pl.BlockSpec(memory_space=pltpu.VMEM)

    south = lax.ppermute(
        prognostic[:, :, rows - 1, :].reshape(chans, width), "lat", [(i, i + 1) for i in range(lat_devices - 1)]
    )
    north = lax.ppermute(
        prognostic[:, :, 0, :].reshape(chans, width), "lat", [(i + 1, i) for i in range(lat_devices - 1)]
    )
    other = lax.ppermute(prognostic[:2], "lev", [(0, 1), (1, 0)])

    global_rows = (lat_index * rows + jnp.arange(rows)).astype(jnp.float32)
    cosine, sine = latitudes(global_rows, rows * lat_devices)
    zonal = 0.25 / (cosine + 0.05)
    zonal_field = jnp.broadcast_to(zonal[:, None], (rows, width))
    coriolis_field = jnp.broadcast_to((0.5 * sine)[:, None], (rows, width))

    sent_rows = halves * chans + SUBLANES
    with jax.named_scope("tendencies"):
        tend, ends = pl.pallas_call(
            tendency_kernel,
            out_shape=(
                jax.ShapeDtypeStruct((rows, sent_rows, HALF), jnp.float32),
                jax.ShapeDtypeStruct((2, halves * chans, HALF), jnp.float32),
            ),
            in_specs=[hbm, vmem, vmem],
            out_specs=(hbm, vmem),
            scratch_shapes=[
                pltpu.VMEM(prognostic.shape, jnp.float32),
                pltpu.VMEM((fields, halves, levels * rows, HALF), jnp.float32),
                pltpu.VMEM((rows, HALF), jnp.float32),
                pltpu.VMEM((rows, sent_rows, HALF), jnp.float32),
                pltpu.SemaphoreType.DMA((CHUNKS,)),
                pltpu.SemaphoreType.DMA((CHUNKS,)),
            ],
            compiler_params=params,
        )(prognostic, zonal_field, coriolis_field)

    with jax.named_scope("seam_rows"):
        tend = pl.pallas_call(
            seam_kernel,
            out_shape=jax.ShapeDtypeStruct(tend.shape, jnp.float32),
            in_specs=[vmem, vmem, vmem, hbm],
            out_specs=hbm,
            input_output_aliases={3: 0},
            scratch_shapes=[pltpu.VMEM(ends.shape, jnp.float32), pltpu.SemaphoreType.DMA((2,))],
            compiler_params=params,
        )(ends, south, north, tend)

    whole_rows = lax.all_to_all(tend, ("lon", "lev"), 0, 0, tiled=True)

    own_row = (lon_index * lev_devices + lev_index).astype(jnp.int32).reshape(1)
    stepped_shape = (lon_devices, lev_devices, fields, halves, levels, HALF)
    count = halves * lon_devices
    both = lev_devices * chans
    with jax.named_scope("row_filter"):
        stepped = pl.pallas_call(
            filter_kernel,
            out_shape=jax.ShapeDtypeStruct(stepped_shape, jnp.float32),
            grid_spec=pltpu.PrefetchScalarGridSpec(
                num_scalar_prefetch=4,
                grid=(1,),
                in_specs=[vmem, hbm],
                out_specs=hbm,
                scratch_shapes=[
                    pltpu.VMEM((count, both, HALF), jnp.float32),
                    pltpu.VMEM((2, count * both, 2 * HALF), jnp.bfloat16),
                    pltpu.VMEM((HALF, HALF), jnp.float32),
                    pltpu.VMEM(column_inverse.shape[1:], jnp.float32),
                    pltpu.VMEM(stepped_shape, jnp.float32),
                    pltpu.SemaphoreType.DMA,
                    pltpu.SemaphoreType.DMA((lon_devices,)),
                ],
            ),
            compiler_params=params,
        )(
            own_row,
            half_width,
            filter_mask,
            zonal,
            whole_rows.reshape(lon_devices, lev_devices, sent_rows, HALF),
            column_inverse,
        )

    returned = lax.all_to_all(
        stepped.reshape((rows,) + stepped_shape[2:]), ("lon", "lev"), 0, 0, tiled=True
    )

    with jax.named_scope("base"):
        base = pl.pallas_call(
            base_kernel,
            out_shape=jax.ShapeDtypeStruct(returned.shape, jnp.float32),
            grid_spec=pltpu.PrefetchScalarGridSpec(
                num_scalar_prefetch=1,
                grid=(halves,),
                in_specs=[
                    pl.BlockSpec((fields, levels, rows, HALF), lambda i, *_: (0, 0, 0, i)),
                    pl.BlockSpec((2, levels, rows, HALF), lambda i, *_: (0, 0, 0, i)),
                    pl.BlockSpec(column_inverse.shape, lambda i, *_: (0, 0, 0)),
                ],
                out_specs=pl.BlockSpec((rows, fields, 1, levels, HALF), lambda i, *_: (0, 0, i, 0, 0)),
            ),
            compiler_params=params,
        )(lev_index.astype(jnp.int32).reshape(1), prognostic, other, column_inverse)

    with jax.named_scope("finish"):
        return pl.pallas_call(
            finish_kernel,
            out_shape=jax.ShapeDtypeStruct(prognostic.shape, jnp.float32),
            in_specs=[vmem, hbm],
            out_specs=hbm,
            scratch_shapes=[
                pltpu.VMEM((fields, rows, halves, levels, HALF), jnp.float32),
                pltpu.VMEM((fields, halves, levels * rows, HALF), jnp.float32),
                pltpu.SemaphoreType.DMA((fields,)),
                pltpu.SemaphoreType.DMA((fields * halves,)),
            ],
            compiler_params=params,
        )(returned, base)


def solution(mesh):
    placed = (P(None, "lev", "lat", "lon"), P("lat"), P("lat"), P("lat", None, None))
    return jax.shard_map(
        per_device,
        mesh=mesh,
        in_specs=placed,
        out_specs=P(None, "lev", "lat", "lon"),
        check_vma=False,
    )
```

```python
import jax
import jax.numpy as jnp
from jax import lax
from jax.experimental import pallas as pl
from jax.experimental.pallas import tpu as pltpu
from jax.sharding import PartitionSpec as P

TIME_STEP = 0.5
VISCOSITY = 0.05
MERIDIONAL = 0.25
HALF = 128
SUBLANES = 8
VMEM_LIMIT = 32 * 1024 * 1024
GROUP = 4


def latitudes(global_rows, row_total):
    latitude_angle = -0.5 * jnp.pi + (global_rows + 0.5) * jnp.pi / row_total
    return (jnp.cos(latitude_angle), jnp.sin(latitude_angle))


def flip(tiles):
    row = lax.broadcasted_iota(jnp.int32, tiles[0].shape, 0)
    for d in (4, 2, 1):
        keep = (row & d) == 0
        turned = list(tiles)
        for i in range(SUBLANES):
            if not i & d:
                a, b = tiles[i], tiles[i + d]
                turned[i] = jnp.where(keep, a, pltpu.roll(b, d, 0))
                turned[i + d] = jnp.where(keep, pltpu.roll(a, SUBLANES - d, 0), b)
        tiles = turned
    return tiles


def outer_rows_kernel(prog, last, first):
    _, levels, rows, _ = prog.shape
    for f in range(3):
        for l in range(levels):
            c = f * levels + l
            last[c : c + 1, :] = prog[f, l, rows - 1 : rows, :]
            first[c : c + 1, :] = prog[f, l, 0:1, :]


def tendency_kernel(prog, zonal, coriolis, out, ends, turn, edges, stage, out_sems):
    _, levels, rows, width = prog.shape
    chans = 3 * levels
    payload = 2 * chans
    row_id = lax.broadcasted_iota(jnp.int32, (rows, width), 0)
    col_id = lax.broadcasted_iota(jnp.int32, (rows, width), 1)
    lane_id = lax.broadcasted_iota(jnp.int32, (rows, HALF), 1)
    first_row, last_row = row_id == 0, row_id == rows - 1
    first_col, last_col = col_id == 0, col_id == width - 1
    zon, cor = zonal[...], coriolis[...]
    edge_rows = jnp.zeros((rows, HALF), jnp.float32)
    for l in range(levels):
        centre, dx, dy, sx = [], [], [], []
        for f in range(3):
            c = f * levels + l
            here = prog[f, l]
            e = jnp.where(last_col, 0.0, pltpu.roll(here, width - 1, 1))
            w = jnp.where(first_col, 0.0, pltpu.roll(here, 1, 1))
            n = jnp.where(last_row, 0.0, pltpu.roll(here, rows - 1, 0))
            s = jnp.where(first_row, 0.0, pltpu.roll(here, 1, 0))
            centre.append(here)
            dx.append(e - w)
            dy.append(n - s)
            sx.append(e + w + n + s - 4.0 * here)
            first = here[:, :HALF]
            last = here[:, width - HALF :]
            if c:
                first = pltpu.roll(first, c, 1)
            last = pltpu.roll(last, (chans + c + 1) % HALF, 1)
            edge_rows = jnp.where(lane_id == c, first, jnp.where(lane_id == chans + c, last, edge_rows))
        tends = (
            -zon * dx[2] + cor * centre[1] + VISCOSITY * sx[0],
            -MERIDIONAL * dy[2] - cor * centre[0] + VISCOSITY * sx[1],
            -zon * dx[0] - MERIDIONAL * dy[1],
        )
        for f in range(3):
            turn[f, l] = tends[f]
    edges[...] = edge_rows
    copies = []
    for chunk in range(rows // SUBLANES):
        some = slice(chunk * SUBLANES, (chunk + 1) * SUBLANES)
        for f in range(3):
            for half in range(2):
                for l0 in range(0, levels, SUBLANES):
                    at = (2 * f + half) * levels + l0
                    flipped = flip(
                        [turn[f, l0 + i, some, half * HALF : (half + 1) * HALF] for i in range(SUBLANES)]
                    )
                    for k, value in enumerate(flipped):
                        j = chunk * SUBLANES + k
                        stage[j, at : at + SUBLANES, :] = value
                        if j in (0, rows - 1):
                            ends[min(j, 1), at : at + SUBLANES, :] = value
        for k in range(SUBLANES):
            j = chunk * SUBLANES + k
            stage[j, payload:, :] = jnp.broadcast_to(edges[j : j + 1, :], (SUBLANES, HALF))
        some = pl.ds(chunk * SUBLANES, SUBLANES)
        copies.append(pltpu.make_async_copy(stage.at[some], out.at[some], out_sems.at[chunk]))
        copies[-1].start()
    for copy in copies:
        copy.wait()


def seam_kernel(ends, south, north, tend, out, stage, sems):
    del tend
    chans = south.shape[0]
    levels = chans // 3
    copies = []
    for at, beyond, sign in ((0, south, -1.0), (1, north, 1.0)):
        for half in range(2):
            lanes = slice(half * HALF, (half + 1) * HALF)
            u, v, h = (beyond[f * levels : (f + 1) * levels, lanes] for f in range(3))
            slope = sign * MERIDIONAL
            for f, term in enumerate((VISCOSITY * u, VISCOSITY * v - slope * h, -slope * v)):
                some = slice((2 * f + half) * levels, (2 * f + half + 1) * levels)
                stage[at, some, :] = ends[at, some, :] + term
        row = at * (out.shape[0] - 1)
        copies.append(pltpu.make_async_copy(stage.at[at], out.at[row, pl.ds(0, 2 * chans)], sems.at[at]))
        copies[-1].start()
    for copy in copies:
        copy.wait()


def split2(x):
    hi = x.astype(jnp.bfloat16)
    return hi, (x - hi.astype(jnp.float32)).astype(jnp.bfloat16)


def mix_operand(matrix):
    hi, lo = split2(matrix)
    return jnp.concatenate([hi, hi, lo], axis=1)


def filter_kernel(
    own_row, half_width, filter_mask, zonal, tend, matrices, out, halves, parts, seam, matrix, stage, matrix_sem, sems
):
    blocks, lev_parts, levels = out.shape[0], out.shape[1], out.shape[4]
    chans = 3 * levels
    payload = 2 * chans
    count = 2 * blocks
    both = lev_parts * chans
    row = own_row[0]
    fetch = pltpu.make_async_copy(matrices.at[row], matrix, matrix_sem)
    fetch.start()
    reach = half_width[row]
    whole = reach == count // 2
    norm = jnp.where(whole, count * HALF, 2 * HALF * reach + 1).astype(jnp.float32)
    filtered = filter_mask[row] == 1
    edge_gain = jnp.where(whole, 0.0, 1.0).astype(jnp.float32)

    for b in range(blocks):
        for part in range(lev_parts):
            at = b * lev_parts + part
            seam[at : at + 1, :] = tend[b, part, payload : payload + 1, :]
    columns = seam[...].T
    zon = zonal[row]
    u, v, h = (columns[f * levels : (f + 1) * levels] for f in range(3))
    from_east = jnp.concatenate([VISCOSITY * u - zon * h, VISCOSITY * v, -zon * u], axis=0)
    u, v, h = (columns[chans + f * levels : chans + (f + 1) * levels] for f in range(3))
    from_west = jnp.concatenate([VISCOSITY * u + zon * h, VISCOSITY * v, zon * u], axis=0)
    lane_id = lax.broadcasted_iota(jnp.int32, (levels, HALF), 1)
    window = jnp.zeros((both, HALF), jnp.float32)
    for g in range(count):
        b, half = divmod(g, 2)
        beyond = (b + 1) % blocks if half else (b + blocks - 1) % blocks
        terms, lane = (from_east, HALF - 1) if half else (from_west, 0)
        pieces = []
        for part in range(lev_parts):
            source = beyond * lev_parts + part
            for f in range(3):
                here = tend[b, part, (2 * f + half) * levels : (2 * f + half + 1) * levels, :]
                term = terms[f * levels : (f + 1) * levels, source : source + 1]
                pieces.append(here + jnp.where(lane_id == lane, term, 0.0))
        value = jnp.concatenate(pieces, axis=0)
        halves[g] = value
        inside = lax.rem(g + reach, count) < 2 * reach
        window = window + jnp.where(inside, 1.0, 0.0).astype(jnp.float32) * value

    src = lax.broadcasted_iota(jnp.int32, (2 * HALF, HALF), 0)
    dst = lax.broadcasted_iota(jnp.int32, (2 * HALF, HALF), 1)
    sums = jnp.where((src <= dst) | (src >= HALF), 1.0, 0.0).astype(jnp.bfloat16)
    fetch.wait()
    mixer = mix_operand(matrix[...])
    scale = TIME_STEP / norm

    def split_group(g0, window):
        for g in range(g0, g0 + GROUP):
            ahead = halves[lax.rem(g + reach, count)]
            behind = halves[lax.rem(g + count - reach, count)]
            change = ahead - behind
            for k, (a, b) in enumerate(zip(split2(change), split2(window))):
                parts[k, g * both : (g + 1) * both, :HALF] = a
                parts[k, g * both : (g + 1) * both, HALF:] = b
            window = window + change
        return window

    copies = []

    def finish_group(g0):
        lo, hi = g0 * both, (g0 + GROUP) * both
        box = jnp.dot(parts[1, lo:hi, :], sums, preferred_element_type=jnp.float32) + jnp.dot(
            parts[0, lo:hi, :], sums, preferred_element_type=jnp.float32
        )
        for pair in range(GROUP // 2):
            b = g0 // 2 + pair
            steps = []
            for half in range(2):
                g = 2 * b + half
                at = (g - g0) * both
                behind = halves[lax.rem(g + count - reach, count)]
                smooth = (box[at : at + both] + edge_gain * behind) * scale
                step = jnp.where(filtered, smooth, TIME_STEP * halves[g])
                for p in range(lev_parts):
                    stage[b, p, 2, half] = step[p * chans + 2 * levels : (p + 1) * chans]
                steps.append(step)
            step = jnp.concatenate(steps, axis=1)
            for f in range(2):
                wind = jnp.concatenate(
                    [step[p * chans + f * levels : p * chans + (f + 1) * levels] for p in range(lev_parts)], axis=0
                )
                wind_hi, wind_lo = split2(wind)
                mixed = jnp.dot(
                    mixer,
                    jnp.concatenate([wind_hi, wind_lo, wind_hi], axis=0),
                    preferred_element_type=jnp.float32,
                )
                for p in range(lev_parts):
                    for half in range(2):
                        stage[b, p, f, half] = mixed[
                            p * levels : (p + 1) * levels, half * HALF : (half + 1) * HALF
                        ]
            copies.append(pltpu.make_async_copy(stage.at[b], out.at[b], sems.at[b]))
            copies[-1].start()

    window = split_group(0, window)
    for g0 in range(0, count, GROUP):
        if g0 + GROUP < count:
            window = split_group(g0 + GROUP, window)
        finish_group(g0)
    for copy in copies:
        copy.wait()


def base_kernel(own_part, own, other, matrix, out):
    _, levels, rows, width = own.shape
    lower = own_part[0] == 0

    def by_row(ref, f, j0):
        flipped = [
            flip([ref[f, l0 + i, j0 : j0 + SUBLANES, :] for i in range(SUBLANES)])
            for l0 in range(0, levels, SUBLANES)
        ]
        return [jnp.concatenate([part[k] for part in flipped], axis=0) for k in range(SUBLANES)]

    for j0 in range(0, rows, SUBLANES):
        mine = [by_row(own, f, j0) for f in range(3)]
        theirs = [by_row(other, f, j0) for f in range(2)]
        for k in range(SUBLANES):
            j = j0 + k
            winds = []
            for f in range(2):
                a, b = mine[f][k], theirs[f][k]
                winds.append(jnp.concatenate([jnp.where(lower, a, b), jnp.where(lower, b, a)], axis=0))
            wind_hi, wind_lo = split2(jnp.concatenate(winds, axis=1))
            mixed = jnp.dot(
                mix_operand(matrix[j]),
                jnp.concatenate([wind_hi, wind_lo, wind_hi], axis=0),
                preferred_element_type=jnp.float32,
            )
            kept = jnp.where(lower, mixed[:levels], mixed[levels:])
            for f in range(2):
                out[j, f, 0] = kept[:, f * width : (f + 1) * width]
            out[j, 2, 0] = mine[2][k]


def finish_kernel(step, base, out, added, stage, in_sems, out_sems):
    fields, levels, rows, _ = out.shape
    loads, copies = [], []
    for f in range(fields):
        loads.append(pltpu.make_async_copy(base.at[:, f], added.at[f], in_sems.at[f]))
        loads[-1].start()
    for f in range(fields):
        loads[f].wait()
        for l0 in range(0, levels, SUBLANES):
            some = slice(l0, l0 + SUBLANES)
            for half in range(2):
                for j0 in range(0, rows, SUBLANES):
                    flipped = flip(
                        [step[j0 + k, f, half, some, :] + added[f, j0 + k, half, some, :] for k in range(SUBLANES)]
                    )
                    for i, value in enumerate(flipped):
                        stage[f, l0 + i, j0 : j0 + SUBLANES, half * HALF : (half + 1) * HALF] = value
            at = f * (levels // SUBLANES) + l0 // SUBLANES
            some = pl.ds(l0, SUBLANES)
            copies.append(pltpu.make_async_copy(stage.at[f, some], out.at[f, some], out_sems.at[at]))
            copies[-1].start()
    for copy in copies:
        copy.wait()


def per_device(prognostic, half_width, filter_mask, column_inverse):
    fields, levels, rows, width = prognostic.shape
    lon_devices, lat_devices, lev_devices = (lax.axis_size(a) for a in ("lon", "lat", "lev"))
    lon_index, lat_index, lev_index = (lax.axis_index(a) for a in ("lon", "lat", "lev"))
    chans = fields * levels
    halves = width // HALF
    params = pltpu.CompilerParams(vmem_limit_bytes=VMEM_LIMIT)
    hbm = pl.BlockSpec(memory_space=pltpu.HBM)
    vmem = pl.BlockSpec(memory_space=pltpu.VMEM)

    with jax.named_scope("outer_rows"):
        last, first = pl.pallas_call(
            outer_rows_kernel,
            out_shape=(jax.ShapeDtypeStruct((chans, width), jnp.float32),) * 2,
            in_specs=[vmem],
            out_specs=(vmem, vmem),
            compiler_params=params,
        )(prognostic)
    south = lax.ppermute(last, "lat", [(i, i + 1) for i in range(lat_devices - 1)])
    north = lax.ppermute(first, "lat", [(i + 1, i) for i in range(lat_devices - 1)])
    other = lax.ppermute(prognostic[:2], "lev", [(0, 1), (1, 0)])

    global_rows = (lat_index * rows + jnp.arange(rows)).astype(jnp.float32)
    cosine, sine = latitudes(global_rows, rows * lat_devices)
    zonal = 0.25 / (cosine + 0.05)
    zonal_field = jnp.broadcast_to(zonal[:, None], (rows, width))
    coriolis_field = jnp.broadcast_to((0.5 * sine)[:, None], (rows, width))

    sent_rows = halves * chans + SUBLANES
    with jax.named_scope("tendencies"):
        tend, ends = pl.pallas_call(
            tendency_kernel,
            out_shape=(
                jax.ShapeDtypeStruct((rows, sent_rows, HALF), jnp.float32),
                jax.ShapeDtypeStruct((2, halves * chans, HALF), jnp.float32),
            ),
            in_specs=[vmem, vmem, vmem],
            out_specs=(hbm, vmem),
            scratch_shapes=[
                pltpu.VMEM(prognostic.shape, jnp.float32),
                pltpu.VMEM((rows, HALF), jnp.float32),
                pltpu.VMEM((rows, sent_rows, HALF), jnp.float32),
                pltpu.SemaphoreType.DMA((rows // SUBLANES,)),
            ],
            compiler_params=params,
        )(prognostic, zonal_field, coriolis_field)

    with jax.named_scope("seam_rows"):
        tend = pl.pallas_call(
            seam_kernel,
            out_shape=jax.ShapeDtypeStruct(tend.shape, jnp.float32),
            in_specs=[vmem, vmem, vmem, hbm],
            out_specs=hbm,
            input_output_aliases={3: 0},
            scratch_shapes=[pltpu.VMEM(ends.shape, jnp.float32), pltpu.SemaphoreType.DMA((2,))],
            compiler_params=params,
        )(ends, south, north, tend)

    whole_rows = lax.all_to_all(tend, ("lon", "lev"), 0, 0, tiled=True)

    own_row = (lon_index * lev_devices + lev_index).astype(jnp.int32).reshape(1)
    stepped_shape = (lon_devices, lev_devices, fields, halves, levels, HALF)
    count = halves * lon_devices
    both = lev_devices * chans
    with jax.named_scope("row_filter"):
        stepped = pl.pallas_call(
            filter_kernel,
            out_shape=jax.ShapeDtypeStruct(stepped_shape, jnp.float32),
            grid_spec=pltpu.PrefetchScalarGridSpec(
                num_scalar_prefetch=4,
                grid=(1,),
                in_specs=[vmem, hbm],
                out_specs=hbm,
                scratch_shapes=[
                    pltpu.VMEM((count, both, HALF), jnp.float32),
                    pltpu.VMEM((2, count * both, 2 * HALF), jnp.bfloat16),
                    pltpu.VMEM((HALF, HALF), jnp.float32),
                    pltpu.VMEM(column_inverse.shape[1:], jnp.float32),
                    pltpu.VMEM(stepped_shape, jnp.float32),
                    pltpu.SemaphoreType.DMA,
                    pltpu.SemaphoreType.DMA((lon_devices,)),
                ],
            ),
            compiler_params=params,
        )(
            own_row,
            half_width,
            filter_mask,
            zonal,
            whole_rows.reshape(lon_devices, lev_devices, sent_rows, HALF),
            column_inverse,
        )

    returned = lax.all_to_all(
        stepped.reshape((rows,) + stepped_shape[2:]), ("lon", "lev"), 0, 0, tiled=True
    )

    with jax.named_scope("base"):
        base = pl.pallas_call(
            base_kernel,
            out_shape=jax.ShapeDtypeStruct(returned.shape, jnp.float32),
            grid_spec=pltpu.PrefetchScalarGridSpec(
                num_scalar_prefetch=1,
                grid=(halves,),
                in_specs=[
                    pl.BlockSpec((fields, levels, rows, HALF), lambda i, *_: (0, 0, 0, i)),
                    pl.BlockSpec((2, levels, rows, HALF), lambda i, *_: (0, 0, 0, i)),
                    pl.BlockSpec(column_inverse.shape, lambda i, *_: (0, 0, 0)),
                ],
                out_specs=pl.BlockSpec((rows, fields, 1, levels, HALF), lambda i, *_: (0, 0, i, 0, 0)),
            ),
            compiler_params=params,
        )(lev_index.astype(jnp.int32).reshape(1), prognostic, other, column_inverse)

    with jax.named_scope("finish"):
        return pl.pallas_call(
            finish_kernel,
            out_shape=jax.ShapeDtypeStruct(prognostic.shape, jnp.float32),
            in_specs=[vmem, hbm],
            out_specs=hbm,
            scratch_shapes=[
                pltpu.VMEM((fields, rows, halves, levels, HALF), jnp.float32),
                pltpu.VMEM(prognostic.shape, jnp.float32),
                pltpu.SemaphoreType.DMA((fields,)),
                pltpu.SemaphoreType.DMA((fields * levels // SUBLANES,)),
            ],
            compiler_params=params,
        )(returned, base)


def solution(mesh):
    placed = (P(None, "lev", "lat", "lon"), P("lat"), P("lat"), P("lat", None, None))
    return jax.shard_map(
        per_device,
        mesh=mesh,
        in_specs=placed,
        out_specs=P(None, "lev", "lat", "lon"),
        check_vma=False,
    )
```

```python
import jax
import jax.numpy as jnp
from jax import lax
from jax.experimental import pallas as pl
from jax.experimental.pallas import tpu as pltpu
from jax.sharding import PartitionSpec as P

TIME_STEP = 0.5
VISCOSITY = 0.05
MERIDIONAL = 0.25
HALF = 128
SUBLANES = 8
VMEM_LIMIT = 32 * 1024 * 1024
VMEM_MOST = 60 * 1024 * 1024
GROUP = 4


def latitudes(global_rows, row_total):
    latitude_angle = -0.5 * jnp.pi + (global_rows + 0.5) * jnp.pi / row_total
    return (jnp.cos(latitude_angle), jnp.sin(latitude_angle))


def flip(tiles):
    row = lax.broadcasted_iota(jnp.int32, tiles[0].shape, 0)
    for d in (4, 2, 1):
        keep = (row & d) == 0
        turned = list(tiles)
        for i in range(SUBLANES):
            if not i & d:
                a, b = tiles[i], tiles[i + d]
                turned[i] = jnp.where(keep, a, pltpu.roll(b, d, 0))
                turned[i + d] = jnp.where(keep, pltpu.roll(a, SUBLANES - d, 0), b)
        tiles = turned
    return tiles


def outer_rows_kernel(prog, last, first):
    _, levels, rows, _ = prog.shape
    for f in range(3):
        for l in range(levels):
            c = f * levels + l
            last[c : c + 1, :] = prog[f, l, rows - 1 : rows, :]
            first[c : c + 1, :] = prog[f, l, 0:1, :]


def tendency_kernel(prog, zonal, coriolis, out, ends, turn, edges, stage, out_sems):
    _, levels, rows, width = prog.shape
    chans = 3 * levels
    payload = 2 * chans
    row_id = lax.broadcasted_iota(jnp.int32, (rows, width), 0)
    col_id = lax.broadcasted_iota(jnp.int32, (rows, width), 1)
    lane_id = lax.broadcasted_iota(jnp.int32, (rows, HALF), 1)
    first_row, last_row = row_id == 0, row_id == rows - 1
    first_col, last_col = col_id == 0, col_id == width - 1
    zon, cor = zonal[...], coriolis[...]
    edge_rows = jnp.zeros((rows, HALF), jnp.float32)
    for l in range(levels):
        centre, dx, dy, sx = [], [], [], []
        for f in range(3):
            c = f * levels + l
            here = prog[f, l]
            e = jnp.where(last_col, 0.0, pltpu.roll(here, width - 1, 1))
            w = jnp.where(first_col, 0.0, pltpu.roll(here, 1, 1))
            n = jnp.where(last_row, 0.0, pltpu.roll(here, rows - 1, 0))
            s = jnp.where(first_row, 0.0, pltpu.roll(here, 1, 0))
            centre.append(here)
            dx.append(e - w)
            dy.append(n - s)
            sx.append(e + w + n + s - 4.0 * here)
            first = here[:, :HALF]
            last = here[:, width - HALF :]
            if c:
                first = pltpu.roll(first, c, 1)
            last = pltpu.roll(last, (chans + c + 1) % HALF, 1)
            edge_rows = jnp.where(lane_id == c, first, jnp.where(lane_id == chans + c, last, edge_rows))
        tends = (
            -zon * dx[2] + cor * centre[1] + VISCOSITY * sx[0],
            -MERIDIONAL * dy[2] - cor * centre[0] + VISCOSITY * sx[1],
            -zon * dx[0] - MERIDIONAL * dy[1],
        )
        for f in range(3):
            turn[f, l] = tends[f]
    edges[...] = edge_rows
    copies = []
    for chunk in range(rows // SUBLANES):
        some = slice(chunk * SUBLANES, (chunk + 1) * SUBLANES)
        for f in range(3):
            for half in range(2):
                for l0 in range(0, levels, SUBLANES):
                    at = (2 * f + half) * levels + l0
                    flipped = flip(
                        [turn[f, l0 + i, some, half * HALF : (half + 1) * HALF] for i in range(SUBLANES)]
                    )
                    for k, value in enumerate(flipped):
                        j = chunk * SUBLANES + k
                        stage[j, at : at + SUBLANES, :] = value
                        if j in (0, rows - 1):
                            ends[min(j, 1), at : at + SUBLANES, :] = value
        for k in range(SUBLANES):
            j = chunk * SUBLANES + k
            stage[j, payload:, :] = jnp.broadcast_to(edges[j : j + 1, :], (SUBLANES, HALF))
        some = pl.ds(chunk * SUBLANES, SUBLANES)
        copies.append(pltpu.make_async_copy(stage.at[some], out.at[some], out_sems.at[chunk]))
        copies[-1].start()
    for copy in copies:
        copy.wait()


def seam_kernel(ends, south, north, tend, out, stage, sems):
    del tend
    chans = south.shape[0]
    levels = chans // 3
    copies = []
    for at, beyond, sign in ((0, south, -1.0), (1, north, 1.0)):
        for half in range(2):
            lanes = slice(half * HALF, (half + 1) * HALF)
            u, v, h = (beyond[f * levels : (f + 1) * levels, lanes] for f in range(3))
            slope = sign * MERIDIONAL
            for f, term in enumerate((VISCOSITY * u, VISCOSITY * v - slope * h, -slope * v)):
                some = slice((2 * f + half) * levels, (2 * f + half + 1) * levels)
                stage[at, some, :] = ends[at, some, :] + term
        row = at * (out.shape[0] - 1)
        copies.append(pltpu.make_async_copy(stage.at[at], out.at[row, pl.ds(0, 2 * chans)], sems.at[at]))
        copies[-1].start()
    for copy in copies:
        copy.wait()


def split2(x):
    hi = x.astype(jnp.bfloat16)
    return hi, (x - hi.astype(jnp.float32)).astype(jnp.bfloat16)


def mix_operand(matrix):
    hi, lo = split2(matrix)
    return jnp.concatenate([hi, hi, lo], axis=1)


def filter_kernel(
    own_row, half_width, filter_mask, zonal, tend, matrix, out, halves, parts, seam, stage, sems
):
    blocks, lev_parts, levels = out.shape[0], out.shape[1], out.shape[4]
    chans = 3 * levels
    payload = 2 * chans
    count = 2 * blocks
    both = lev_parts * chans
    row = own_row[0]
    reach = half_width[row]
    whole = reach == count // 2
    norm = jnp.where(whole, count * HALF, 2 * HALF * reach + 1).astype(jnp.float32)
    filtered = filter_mask[row] == 1
    edge_gain = jnp.where(whole, 0.0, 1.0).astype(jnp.float32)

    for b in range(blocks):
        for part in range(lev_parts):
            at = b * lev_parts + part
            seam[at : at + 1, :] = tend[b, part, payload : payload + 1, :]
    columns = seam[...].T
    zon = zonal[row]
    u, v, h = (columns[f * levels : (f + 1) * levels] for f in range(3))
    from_east = jnp.concatenate([VISCOSITY * u - zon * h, VISCOSITY * v, -zon * u], axis=0)
    u, v, h = (columns[chans + f * levels : chans + (f + 1) * levels] for f in range(3))
    from_west = jnp.concatenate([VISCOSITY * u + zon * h, VISCOSITY * v, zon * u], axis=0)
    lane_id = lax.broadcasted_iota(jnp.int32, (levels, HALF), 1)
    window = jnp.zeros((both, HALF), jnp.float32)
    for g in range(count):
        b, half = divmod(g, 2)
        beyond = (b + 1) % blocks if half else (b + blocks - 1) % blocks
        terms, lane = (from_east, HALF - 1) if half else (from_west, 0)
        pieces = []
        for part in range(lev_parts):
            source = beyond * lev_parts + part
            for f in range(3):
                here = tend[b, part, (2 * f + half) * levels : (2 * f + half + 1) * levels, :]
                term = terms[f * levels : (f + 1) * levels, source : source + 1]
                pieces.append(here + jnp.where(lane_id == lane, term, 0.0))
        value = jnp.concatenate(pieces, axis=0)
        halves[g] = value
        inside = lax.rem(g + reach, count) < 2 * reach
        window = window + jnp.where(inside, 1.0, 0.0).astype(jnp.float32) * value

    src = lax.broadcasted_iota(jnp.int32, (2 * HALF, HALF), 0)
    dst = lax.broadcasted_iota(jnp.int32, (2 * HALF, HALF), 1)
    sums = jnp.where((src <= dst) | (src >= HALF), 1.0, 0.0).astype(jnp.bfloat16)
    mixer = mix_operand(matrix[...])
    scale = TIME_STEP / norm

    def split_group(g0, window):
        for g in range(g0, g0 + GROUP):
            ahead = halves[lax.rem(g + reach, count)]
            behind = halves[lax.rem(g + count - reach, count)]
            change = ahead - behind
            for k, (a, b) in enumerate(zip(split2(change), split2(window))):
                parts[k, g * both : (g + 1) * both, :HALF] = a
                parts[k, g * both : (g + 1) * both, HALF:] = b
            window = window + change
        return window

    copies = []

    def finish_group(g0):
        lo, hi = g0 * both, (g0 + GROUP) * both
        box = jnp.dot(parts[1, lo:hi, :], sums, preferred_element_type=jnp.float32) + jnp.dot(
            parts[0, lo:hi, :], sums, preferred_element_type=jnp.float32
        )
        for pair in range(GROUP // 2):
            b = g0 // 2 + pair
            steps = []
            for half in range(2):
                g = 2 * b + half
                at = (g - g0) * both
                behind = halves[lax.rem(g + count - reach, count)]
                smooth = (box[at : at + both] + edge_gain * behind) * scale
                step = jnp.where(filtered, smooth, TIME_STEP * halves[g])
                for p in range(lev_parts):
                    stage[b, p, 2, half] = step[p * chans + 2 * levels : (p + 1) * chans]
                steps.append(step)
            step = jnp.concatenate(steps, axis=1)
            for f in range(2):
                wind = jnp.concatenate(
                    [step[p * chans + f * levels : p * chans + (f + 1) * levels] for p in range(lev_parts)], axis=0
                )
                wind_hi, wind_lo = split2(wind)
                mixed = jnp.dot(
                    mixer,
                    jnp.concatenate([wind_hi, wind_lo, wind_hi], axis=0),
                    preferred_element_type=jnp.float32,
                )
                for p in range(lev_parts):
                    for half in range(2):
                        stage[b, p, f, half] = mixed[
                            p * levels : (p + 1) * levels, half * HALF : (half + 1) * HALF
                        ]
            copies.append(pltpu.make_async_copy(stage.at[b], out.at[b], sems.at[b]))
            copies[-1].start()

    window = split_group(0, window)
    for g0 in range(0, count, GROUP):
        if g0 + GROUP < count:
            window = split_group(g0 + GROUP, window)
        finish_group(g0)
    for copy in copies:
        copy.wait()


def base_kernel(own_part, own, other, matrix, out):
    _, levels, rows, width = own.shape
    lower = own_part[0] == 0

    def by_row(ref, f, j0):
        flipped = [
            flip([ref[f, l0 + i, j0 : j0 + SUBLANES, :] for i in range(SUBLANES)])
            for l0 in range(0, levels, SUBLANES)
        ]
        return [jnp.concatenate([part[k] for part in flipped], axis=0) for k in range(SUBLANES)]

    for j0 in range(0, rows, SUBLANES):
        mine = [by_row(own, f, j0) for f in range(3)]
        theirs = [by_row(other, f, j0) for f in range(2)]
        for k in range(SUBLANES):
            j = j0 + k
            winds = []
            for f in range(2):
                a, b = mine[f][k], theirs[f][k]
                winds.append(jnp.concatenate([jnp.where(lower, a, b), jnp.where(lower, b, a)], axis=0))
            wind_hi, wind_lo = split2(jnp.concatenate(winds, axis=1))
            mixed = jnp.dot(
                mix_operand(matrix[j]),
                jnp.concatenate([wind_hi, wind_lo, wind_hi], axis=0),
                preferred_element_type=jnp.float32,
            )
            kept = jnp.where(lower, mixed[:levels], mixed[levels:])
            for f in range(2):
                out[j, f, 0] = kept[:, f * width : (f + 1) * width]
            out[j, 2, 0] = mine[2][k]


def finish_kernel(step, base, out, added, stage, in_sems, out_sems):
    fields, levels, rows, _ = out.shape
    loads, copies = [], []
    for f in range(fields):
        loads.append(pltpu.make_async_copy(base.at[:, f], added.at[f], in_sems.at[f]))
        loads[-1].start()
    for f in range(fields):
        loads[f].wait()
        for l0 in range(0, levels, SUBLANES):
            some = slice(l0, l0 + SUBLANES)
            for half in range(2):
                for j0 in range(0, rows, SUBLANES):
                    flipped = flip(
                        [step[j0 + k, f, half, some, :] + added[f, j0 + k, half, some, :] for k in range(SUBLANES)]
                    )
                    for i, value in enumerate(flipped):
                        stage[f, l0 + i, j0 : j0 + SUBLANES, half * HALF : (half + 1) * HALF] = value
            at = f * (levels // SUBLANES) + l0 // SUBLANES
            some = pl.ds(l0, SUBLANES)
            copies.append(pltpu.make_async_copy(stage.at[f, some], out.at[f, some], out_sems.at[at]))
            copies[-1].start()
    for copy in copies:
        copy.wait()


def per_device(prognostic, half_width, filter_mask, column_inverse):
    fields, levels, rows, width = prognostic.shape
    lon_devices, lat_devices, lev_devices = (lax.axis_size(a) for a in ("lon", "lat", "lev"))
    lon_index, lat_index, lev_index = (lax.axis_index(a) for a in ("lon", "lat", "lev"))
    chans = fields * levels
    halves = width // HALF
    params = pltpu.CompilerParams(vmem_limit_bytes=VMEM_LIMIT)
    most = pltpu.CompilerParams(vmem_limit_bytes=VMEM_MOST)
    hbm = pl.BlockSpec(memory_space=pltpu.HBM)
    vmem = pl.BlockSpec(memory_space=pltpu.VMEM)

    with jax.named_scope("outer_rows"):
        last, first = pl.pallas_call(
            outer_rows_kernel,
            out_shape=(jax.ShapeDtypeStruct((chans, width), jnp.float32),) * 2,
            in_specs=[vmem],
            out_specs=(vmem, vmem),
            compiler_params=params,
        )(prognostic)
    south = lax.ppermute(last, "lat", [(i, i + 1) for i in range(lat_devices - 1)])
    north = lax.ppermute(first, "lat", [(i + 1, i) for i in range(lat_devices - 1)])
    other = lax.ppermute(prognostic[:2], "lev", [(0, 1), (1, 0)])

    global_rows = (lat_index * rows + jnp.arange(rows)).astype(jnp.float32)
    cosine, sine = latitudes(global_rows, rows * lat_devices)
    zonal = 0.25 / (cosine + 0.05)
    zonal_field = jnp.broadcast_to(zonal[:, None], (rows, width))
    coriolis_field = jnp.broadcast_to((0.5 * sine)[:, None], (rows, width))

    sent_rows = halves * chans + SUBLANES
    with jax.named_scope("tendencies"):
        tend, ends = pl.pallas_call(
            tendency_kernel,
            out_shape=(
                jax.ShapeDtypeStruct((rows, sent_rows, HALF), jnp.float32),
                jax.ShapeDtypeStruct((2, halves * chans, HALF), jnp.float32),
            ),
            in_specs=[vmem, vmem, vmem],
            out_specs=(hbm, vmem),
            scratch_shapes=[
                pltpu.VMEM(prognostic.shape, jnp.float32),
                pltpu.VMEM((rows, HALF), jnp.float32),
                pltpu.VMEM((rows, sent_rows, HALF), jnp.float32),
                pltpu.SemaphoreType.DMA((rows // SUBLANES,)),
            ],
            compiler_params=params,
        )(prognostic, zonal_field, coriolis_field)

    with jax.named_scope("seam_rows"):
        tend = pl.pallas_call(
            seam_kernel,
            out_shape=jax.ShapeDtypeStruct(tend.shape, jnp.float32),
            in_specs=[vmem, vmem, vmem, hbm],
            out_specs=hbm,
            input_output_aliases={3: 0},
            scratch_shapes=[pltpu.VMEM(ends.shape, jnp.float32), pltpu.SemaphoreType.DMA((2,))],
            compiler_params=params,
        )(ends, south, north, tend)

    whole_rows = lax.all_to_all(tend, ("lon", "lev"), 0, 0, tiled=True)

    own_row = (lon_index * lev_devices + lev_index).astype(jnp.int32).reshape(1)
    stepped_shape = (lon_devices, lev_devices, fields, halves, levels, HALF)
    count = halves * lon_devices
    both = lev_devices * chans
    with jax.named_scope("row_filter"):
        stepped = pl.pallas_call(
            filter_kernel,
            out_shape=jax.ShapeDtypeStruct(stepped_shape, jnp.float32),
            grid_spec=pltpu.PrefetchScalarGridSpec(
                num_scalar_prefetch=4,
                grid=(1,),
                in_specs=[vmem, vmem],
                out_specs=hbm,
                scratch_shapes=[
                    pltpu.VMEM((count, both, HALF), jnp.float32),
                    pltpu.VMEM((2, count * both, 2 * HALF), jnp.bfloat16),
                    pltpu.VMEM((HALF, HALF), jnp.float32),
                    pltpu.VMEM(stepped_shape, jnp.float32),
                    pltpu.SemaphoreType.DMA((lon_devices,)),
                ],
            ),
            compiler_params=most,
        )(
            own_row,
            half_width,
            filter_mask,
            zonal,
            whole_rows.reshape(lon_devices, lev_devices, sent_rows, HALF),
            lax.dynamic_index_in_dim(column_inverse, own_row[0], 0, keepdims=False),
        )

    returned = lax.all_to_all(
        stepped.reshape((rows,) + stepped_shape[2:]), ("lon", "lev"), 0, 0, tiled=True
    )

    with jax.named_scope("base"):
        base = pl.pallas_call(
            base_kernel,
            out_shape=jax.ShapeDtypeStruct(returned.shape, jnp.float32),
            grid_spec=pltpu.PrefetchScalarGridSpec(
                num_scalar_prefetch=1,
                grid=(halves,),
                in_specs=[
                    pl.BlockSpec((fields, levels, rows, HALF), lambda i, *_: (0, 0, 0, i)),
                    pl.BlockSpec((2, levels, rows, HALF), lambda i, *_: (0, 0, 0, i)),
                    pl.BlockSpec(column_inverse.shape, lambda i, *_: (0, 0, 0)),
                ],
                out_specs=pl.BlockSpec((rows, fields, 1, levels, HALF), lambda i, *_: (0, 0, i, 0, 0)),
            ),
            compiler_params=params,
        )(lev_index.astype(jnp.int32).reshape(1), prognostic, other, column_inverse)

    with jax.named_scope("finish"):
        return pl.pallas_call(
            finish_kernel,
            out_shape=jax.ShapeDtypeStruct(prognostic.shape, jnp.float32),
            in_specs=[vmem, hbm],
            out_specs=hbm,
            scratch_shapes=[
                pltpu.VMEM((fields, rows, halves, levels, HALF), jnp.float32),
                pltpu.VMEM(prognostic.shape, jnp.float32),
                pltpu.SemaphoreType.DMA((fields,)),
                pltpu.SemaphoreType.DMA((fields * levels // SUBLANES,)),
            ],
            compiler_params=most,
        )(returned, base)


def solution(mesh):
    placed = (P(None, "lev", "lat", "lon"), P("lat"), P("lat"), P("lat", None, None))
    return jax.shard_map(
        per_device,
        mesh=mesh,
        in_specs=placed,
        out_specs=P(None, "lev", "lat", "lon"),
        check_vma=False,
    )
```

```python
import jax
import jax.numpy as jnp
from jax import lax
from jax.experimental import pallas as pl
from jax.experimental.pallas import tpu as pltpu
from jax.sharding import PartitionSpec as P

TIME_STEP = 0.5
VISCOSITY = 0.05
MERIDIONAL = 0.25
HALF = 128
SUBLANES = 8
VMEM_LIMIT = 32 * 1024 * 1024
GROUP = 4


def latitudes(global_rows, row_total):
    latitude_angle = -0.5 * jnp.pi + (global_rows + 0.5) * jnp.pi / row_total
    return (jnp.cos(latitude_angle), jnp.sin(latitude_angle))


def flip(tiles):
    row = lax.broadcasted_iota(jnp.int32, tiles[0].shape, 0)
    for d in (4, 2, 1):
        keep = (row & d) == 0
        turned = list(tiles)
        for i in range(SUBLANES):
            if not i & d:
                a, b = tiles[i], tiles[i + d]
                turned[i] = jnp.where(keep, a, pltpu.roll(b, d, 0))
                turned[i + d] = jnp.where(keep, pltpu.roll(a, SUBLANES - d, 0), b)
        tiles = turned
    return tiles


def outer_rows_kernel(prog, last, first):
    _, levels, rows, _ = prog.shape
    for f in range(3):
        for l in range(levels):
            c = f * levels + l
            last[c : c + 1, :] = prog[f, l, rows - 1 : rows, :]
            first[c : c + 1, :] = prog[f, l, 0:1, :]


def tendency_kernel(prog, zonal, coriolis, out, ends, turn, edges, stage, out_sems):
    _, levels, rows, width = prog.shape
    chans = 3 * levels
    payload = 2 * chans
    row_id = lax.broadcasted_iota(jnp.int32, (rows, width), 0)
    col_id = lax.broadcasted_iota(jnp.int32, (rows, width), 1)
    lane_id = lax.broadcasted_iota(jnp.int32, (rows, HALF), 1)
    first_row, last_row = row_id == 0, row_id == rows - 1
    first_col, last_col = col_id == 0, col_id == width - 1
    zon, cor = zonal[...], coriolis[...]
    edge_rows = jnp.zeros((rows, HALF), jnp.float32)
    for l in range(levels):
        centre, dx, dy, sx = [], [], [], []
        for f in range(3):
            c = f * levels + l
            here = prog[f, l]
            e = jnp.where(last_col, 0.0, pltpu.roll(here, width - 1, 1))
            w = jnp.where(first_col, 0.0, pltpu.roll(here, 1, 1))
            n = jnp.where(last_row, 0.0, pltpu.roll(here, rows - 1, 0))
            s = jnp.where(first_row, 0.0, pltpu.roll(here, 1, 0))
            centre.append(here)
            dx.append(e - w)
            dy.append(n - s)
            sx.append(e + w + n + s - 4.0 * here)
            first = here[:, :HALF]
            last = here[:, width - HALF :]
            if c:
                first = pltpu.roll(first, c, 1)
            last = pltpu.roll(last, (chans + c + 1) % HALF, 1)
            edge_rows = jnp.where(lane_id == c, first, jnp.where(lane_id == chans + c, last, edge_rows))
        tends = (
            -zon * dx[2] + cor * centre[1] + VISCOSITY * sx[0],
            -MERIDIONAL * dy[2] - cor * centre[0] + VISCOSITY * sx[1],
            -zon * dx[0] - MERIDIONAL * dy[1],
        )
        for f in range(3):
            turn[f, l] = tends[f]
    edges[...] = edge_rows
    copies = []
    for chunk in range(rows // SUBLANES):
        some = slice(chunk * SUBLANES, (chunk + 1) * SUBLANES)
        for f in range(3):
            for half in range(2):
                for l0 in range(0, levels, SUBLANES):
                    at = (2 * f + half) * levels + l0
                    flipped = flip(
                        [turn[f, l0 + i, some, half * HALF : (half + 1) * HALF] for i in range(SUBLANES)]
                    )
                    for k, value in enumerate(flipped):
                        j = chunk * SUBLANES + k
                        stage[j, at : at + SUBLANES, :] = value
                        if j in (0, rows - 1):
                            ends[min(j, 1), at : at + SUBLANES, :] = value
        for k in range(SUBLANES):
            j = chunk * SUBLANES + k
            stage[j, payload:, :] = jnp.broadcast_to(edges[j : j + 1, :], (SUBLANES, HALF))
        some = pl.ds(chunk * SUBLANES, SUBLANES)
        copies.append(pltpu.make_async_copy(stage.at[some], out.at[some], out_sems.at[chunk]))
        copies[-1].start()
    for copy in copies:
        copy.wait()


def seam_kernel(ends, south, north, tend, out, stage, sems):
    del tend
    chans = south.shape[0]
    levels = chans // 3
    copies = []
    for at, beyond, sign in ((0, south, -1.0), (1, north, 1.0)):
        for half in range(2):
            lanes = slice(half * HALF, (half + 1) * HALF)
            u, v, h = (beyond[f * levels : (f + 1) * levels, lanes] for f in range(3))
            slope = sign * MERIDIONAL
            for f, term in enumerate((VISCOSITY * u, VISCOSITY * v - slope * h, -slope * v)):
                some = slice((2 * f + half) * levels, (2 * f + half + 1) * levels)
                stage[at, some, :] = ends[at, some, :] + term
        row = at * (out.shape[0] - 1)
        copies.append(pltpu.make_async_copy(stage.at[at], out.at[row, pl.ds(0, 2 * chans)], sems.at[at]))
        copies[-1].start()
    for copy in copies:
        copy.wait()


def split2(x):
    hi = x.astype(jnp.bfloat16)
    return hi, (x - hi.astype(jnp.float32)).astype(jnp.bfloat16)


def mix_operand(matrix):
    hi, lo = split2(matrix)
    return jnp.concatenate([hi, hi, lo], axis=1)


def filter_kernel(first_row, half_width, filter_mask, zonal, tend, out, halves, parts, seam, stage, sems):
    blocks, own_rows, levels = out.shape[0], out.shape[1], out.shape[4]
    chans = 3 * levels
    payload = 2 * chans
    count = 2 * blocks
    both = own_rows * chans
    reach, scale, filtered, edge_gain, sides = [], [], [], [], []
    for b in range(blocks):
        for part in range(own_rows):
            at = b * own_rows + part
            seam[at : at + 1, :] = tend[b, part, payload : payload + 1, :]
    columns = seam[...].T
    for part in range(own_rows):
        row = first_row[0] + part
        reach.append(half_width[row])
        whole = reach[part] == count // 2
        norm = jnp.where(whole, count * HALF, 2 * HALF * reach[part] + 1).astype(jnp.float32)
        scale.append(TIME_STEP / norm)
        filtered.append(filter_mask[row] == 1)
        edge_gain.append(jnp.where(whole, 0.0, 1.0).astype(jnp.float32))
        zon = zonal[row]
        terms = []
        for start, sign in ((chans, 1.0), (0, -1.0)):
            u, v, h = (columns[start + f * levels : start + (f + 1) * levels] for f in range(3))
            terms.append(jnp.concatenate([VISCOSITY * u + sign * zon * h, VISCOSITY * v, sign * zon * u], axis=0))
        sides.append(terms)
    lane_id = lax.broadcasted_iota(jnp.int32, (chans, HALF), 1)
    windows = [jnp.zeros((chans, HALF), jnp.float32) for _ in range(own_rows)]
    for g in range(count):
        b, half = divmod(g, 2)
        beyond = (b + 1) % blocks if half else (b + blocks - 1) % blocks
        lane = HALF - 1 if half else 0
        for part in range(own_rows):
            source = beyond * own_rows + part
            here = jnp.concatenate(
                [tend[b, part, (2 * f + half) * levels : (2 * f + half + 1) * levels, :] for f in range(3)], axis=0
            )
            value = here + jnp.where(lane_id == lane, sides[part][half][:, source : source + 1], 0.0)
            halves[g, part * chans : (part + 1) * chans, :] = value
            inside = lax.rem(g + reach[part], count) < 2 * reach[part]
            windows[part] = windows[part] + jnp.where(inside, 1.0, 0.0).astype(jnp.float32) * value

    src = lax.broadcasted_iota(jnp.int32, (2 * HALF, HALF), 0)
    dst = lax.broadcasted_iota(jnp.int32, (2 * HALF, HALF), 1)
    sums = jnp.where((src <= dst) | (src >= HALF), 1.0, 0.0).astype(jnp.bfloat16)

    def split_group(g0):
        for g in range(g0, g0 + GROUP):
            for part in range(own_rows):
                some = slice(part * chans, (part + 1) * chans)
                ahead = halves[lax.rem(g + reach[part], count), some, :]
                behind = halves[lax.rem(g + count - reach[part], count), some, :]
                change = ahead - behind
                at = g * both + part * chans
                for k, (a, b) in enumerate(zip(split2(change), split2(windows[part]))):
                    parts[k, at : at + chans, :HALF] = a
                    parts[k, at : at + chans, HALF:] = b
                windows[part] = windows[part] + change

    copies = []

    def finish_group(g0):
        lo, hi = g0 * both, (g0 + GROUP) * both
        box = jnp.dot(parts[1, lo:hi, :], sums, preferred_element_type=jnp.float32) + jnp.dot(
            parts[0, lo:hi, :], sums, preferred_element_type=jnp.float32
        )
        for g in range(g0, g0 + GROUP):
            b, half = divmod(g, 2)
            for part in range(own_rows):
                some = slice(part * chans, (part + 1) * chans)
                at = (g - g0) * both + part * chans
                behind = halves[lax.rem(g + count - reach[part], count), some, :]
                smooth = (box[at : at + chans] + edge_gain[part] * behind) * scale[part]
                step = jnp.where(filtered[part], smooth, TIME_STEP * halves[g, some, :])
                for f in range(3):
                    stage[b, part, f, half] = step[f * levels : (f + 1) * levels]
            if half:
                copies.append(pltpu.make_async_copy(stage.at[b], out.at[b], sems.at[b]))
                copies[-1].start()

    split_group(0)
    for g0 in range(0, count, GROUP):
        if g0 + GROUP < count:
            split_group(g0 + GROUP)
        finish_group(g0)
    for copy in copies:
        copy.wait()


def base_kernel(own_part, own, other, matrix, out):
    _, levels, rows, width = own.shape
    lower = own_part[0] == 0

    def by_row(ref, f, j0):
        flipped = [
            flip([ref[f, l0 + i, j0 : j0 + SUBLANES, :] for i in range(SUBLANES)])
            for l0 in range(0, levels, SUBLANES)
        ]
        return [jnp.concatenate([part[k] for part in flipped], axis=0) for k in range(SUBLANES)]

    for j0 in range(0, rows, SUBLANES):
        mine = [by_row(own, f, j0) for f in range(3)]
        theirs = [by_row(other, f, j0) for f in range(2)]
        for k in range(SUBLANES):
            j = j0 + k
            winds = []
            for f in range(2):
                a, b = mine[f][k], theirs[f][k]
                winds.append(jnp.concatenate([jnp.where(lower, a, b), jnp.where(lower, b, a)], axis=0))
            wind_hi, wind_lo = split2(jnp.concatenate(winds, axis=1))
            mixed = jnp.dot(
                mix_operand(matrix[j]),
                jnp.concatenate([wind_hi, wind_lo, wind_hi], axis=0),
                preferred_element_type=jnp.float32,
            )
            kept = jnp.where(lower, mixed[:levels], mixed[levels:])
            for f in range(2):
                out[j, f, 0] = kept[:, f * width : (f + 1) * width]
            out[j, 2, 0] = mine[2][k]


def finish_kernel(own_part, step, other, base, matrix, out, added, stage, in_sems, out_sems):
    fields, levels, rows, _ = out.shape
    lower = own_part[0] == 0
    loads, copies = [], []
    for part in range(rows // SUBLANES):
        some = pl.ds(part * SUBLANES, SUBLANES)
        loads.append(pltpu.make_async_copy(base.at[some], added.at[some], in_sems.at[part]))
        loads[-1].start()
    for part in range(rows // SUBLANES):
        loads[part].wait()
        j0 = part * SUBLANES
        values = []
        for j in range(j0, j0 + SUBLANES):
            winds = []
            for f in range(2):
                for half in range(2):
                    a, b = step[j, f, half], other[j, f, half]
                    winds.append(jnp.concatenate([jnp.where(lower, a, b), jnp.where(lower, b, a)], axis=0))
            wind_hi, wind_lo = split2(jnp.concatenate(winds, axis=1))
            mixed = jnp.dot(
                mix_operand(matrix[j]),
                jnp.concatenate([wind_hi, wind_lo, wind_hi], axis=0),
                preferred_element_type=jnp.float32,
            )
            kept = jnp.where(lower, mixed[:levels], mixed[levels:])
            pieces = [kept[:, n * HALF : (n + 1) * HALF] for n in range(4)] + [step[j, 2, 0], step[j, 2, 1]]
            values.append([piece + added[j, n // 2, n % 2] for n, piece in enumerate(pieces)])
        for n in range(6):
            f, half = divmod(n, 2)
            for l0 in range(0, levels, SUBLANES):
                flipped = flip([values[k][n][l0 : l0 + SUBLANES] for k in range(SUBLANES)])
                for i, value in enumerate(flipped):
                    stage[f, l0 + i, j0 : j0 + SUBLANES, half * HALF : (half + 1) * HALF] = value
        some = pl.ds(j0, SUBLANES)
        copies.append(pltpu.make_async_copy(stage.at[:, :, some], out.at[:, :, some], out_sems.at[part]))
        copies[-1].start()
    for copy in copies:
        copy.wait()


def per_device(prognostic, half_width, filter_mask, column_inverse):
    fields, levels, rows, width = prognostic.shape
    lon_devices, lat_devices = (lax.axis_size(a) for a in ("lon", "lat"))
    lon_index, lat_index, lev_index = (lax.axis_index(a) for a in ("lon", "lat", "lev"))
    chans = fields * levels
    halves = width // HALF
    params = pltpu.CompilerParams(vmem_limit_bytes=VMEM_LIMIT)
    hbm = pl.BlockSpec(memory_space=pltpu.HBM)
    vmem = pl.BlockSpec(memory_space=pltpu.VMEM)

    def in_hbm(x):
        return pltpu.with_memory_space_constraint(x, pltpu.HBM)

    def in_vmem(x):
        return pltpu.with_memory_space_constraint(x, pltpu.VMEM)


    with jax.named_scope("outer_rows"):
        last, first = pl.pallas_call(
            outer_rows_kernel,
            out_shape=(pltpu.VMEM((chans, width), jnp.float32),) * 2,
            in_specs=[vmem],
            out_specs=(vmem, vmem),
            compiler_params=params,
        )(in_vmem(prognostic))
    south = lax.ppermute(last, "lat", [(i, i + 1) for i in range(lat_devices - 1)])
    north = lax.ppermute(first, "lat", [(i + 1, i) for i in range(lat_devices - 1)])
    other = lax.ppermute(prognostic[:2], "lev", [(0, 1), (1, 0)])

    global_rows = (lat_index * rows + jnp.arange(rows)).astype(jnp.float32)
    cosine, sine = latitudes(global_rows, rows * lat_devices)
    zonal = 0.25 / (cosine + 0.05)
    zonal_field = jnp.broadcast_to(zonal[:, None], (rows, width))
    coriolis_field = jnp.broadcast_to((0.5 * sine)[:, None], (rows, width))

    sent_rows = halves * chans + SUBLANES
    with jax.named_scope("tendencies"):
        tend, ends = pl.pallas_call(
            tendency_kernel,
            out_shape=(
                pltpu.HBM((rows, sent_rows, HALF), jnp.float32),
                pltpu.VMEM((2, halves * chans, HALF), jnp.float32),
            ),
            in_specs=[vmem, vmem, vmem],
            out_specs=(hbm, vmem),
            scratch_shapes=[
                pltpu.VMEM(prognostic.shape, jnp.float32),
                pltpu.VMEM((rows, HALF), jnp.float32),
                pltpu.VMEM((rows, sent_rows, HALF), jnp.float32),
                pltpu.SemaphoreType.DMA((rows // SUBLANES,)),
            ],
            compiler_params=params,
        )(in_vmem(prognostic), zonal_field, coriolis_field)

    with jax.named_scope("seam_rows"):
        tend = pl.pallas_call(
            seam_kernel,
            out_shape=pltpu.HBM(tend.shape, jnp.float32),
            in_specs=[vmem, vmem, vmem, hbm],
            out_specs=hbm,
            input_output_aliases={3: 0},
            scratch_shapes=[pltpu.VMEM(ends.shape, jnp.float32), pltpu.SemaphoreType.DMA((2,))],
            compiler_params=params,
        )(in_vmem(ends), in_vmem(south), in_vmem(north), in_hbm(tend))

    own_rows = rows // lon_devices
    whole_rows = lax.all_to_all(
        tend.reshape(lon_devices, own_rows, sent_rows, HALF), "lon", 0, 0, tiled=True
    )

    stepped_shape = (lon_devices, own_rows, fields, halves, levels, HALF)
    count = halves * lon_devices
    both = own_rows * chans
    with jax.named_scope("row_filter"):
        stepped = pl.pallas_call(
            filter_kernel,
            out_shape=pltpu.HBM(stepped_shape, jnp.float32),
            grid_spec=pltpu.PrefetchScalarGridSpec(
                num_scalar_prefetch=4,
                grid=(1,),
                in_specs=[vmem],
                out_specs=hbm,
                scratch_shapes=[
                    pltpu.VMEM((count, both, HALF), jnp.float32),
                    pltpu.VMEM((2, count * both, 2 * HALF), jnp.bfloat16),
                    pltpu.VMEM((HALF, HALF), jnp.float32),
                    pltpu.VMEM(stepped_shape, jnp.float32),
                    pltpu.SemaphoreType.DMA((lon_devices,)),
                ],
            ),
            compiler_params=params,
        )(
            (lon_index * own_rows).astype(jnp.int32).reshape(1),
            half_width,
            filter_mask,
            zonal,
            in_vmem(whole_rows),
        )

    returned = lax.all_to_all(stepped, "lon", 0, 0, tiled=True).reshape((rows,) + stepped_shape[2:])
    winds_beyond = lax.ppermute(returned[:, :2], "lev", [(0, 1), (1, 0)])

    with jax.named_scope("base"):
        base = pl.pallas_call(
            base_kernel,
            out_shape=pltpu.HBM(returned.shape, jnp.float32),
            grid_spec=pltpu.PrefetchScalarGridSpec(
                num_scalar_prefetch=1,
                grid=(halves,),
                in_specs=[
                    pl.BlockSpec((fields, levels, rows, HALF), lambda i, *_: (0, 0, 0, i)),
                    pl.BlockSpec((2, levels, rows, HALF), lambda i, *_: (0, 0, 0, i)),
                    pl.BlockSpec(column_inverse.shape, lambda i, *_: (0, 0, 0)),
                ],
                out_specs=pl.BlockSpec((rows, fields, 1, levels, HALF), lambda i, *_: (0, 0, i, 0, 0)),
            ),
            compiler_params=params,
        )(lev_index.astype(jnp.int32).reshape(1), prognostic, other, column_inverse)

    with jax.named_scope("finish"):
        return pl.pallas_call(
            finish_kernel,
            out_shape=jax.ShapeDtypeStruct(prognostic.shape, jnp.float32),
            grid_spec=pltpu.PrefetchScalarGridSpec(
                num_scalar_prefetch=1,
                grid=(1,),
                in_specs=[vmem, vmem, hbm, vmem],
                out_specs=hbm,
                scratch_shapes=[
                    pltpu.VMEM(returned.shape, jnp.float32),
                    pltpu.VMEM(prognostic.shape, jnp.float32),
                    pltpu.SemaphoreType.DMA((rows // SUBLANES,)),
                    pltpu.SemaphoreType.DMA((rows // SUBLANES,)),
                ],
            ),
            compiler_params=params,
        )(
            lev_index.astype(jnp.int32).reshape(1),
            in_vmem(returned),
            in_vmem(winds_beyond),
            in_hbm(base),
            column_inverse,
        )


def solution(mesh):
    placed = (P(None, "lev", "lat", "lon"), P("lat"), P("lat"), P("lat", None, None))
    return jax.shard_map(
        per_device,
        mesh=mesh,
        in_specs=placed,
        out_specs=P(None, "lev", "lat", "lon"),
        check_vma=False,
    )
```

```python
import jax
import jax.numpy as jnp
from jax import lax
from jax.experimental import pallas as pl
from jax.experimental.pallas import tpu as pltpu
from jax.sharding import PartitionSpec as P

TIME_STEP = 0.5
VISCOSITY = 0.05
MERIDIONAL = 0.25
HALF = 128
SUBLANES = 8
VMEM_LIMIT = 32 * 1024 * 1024
GROUP = 4


def latitudes(global_rows, row_total):
    latitude_angle = -0.5 * jnp.pi + (global_rows + 0.5) * jnp.pi / row_total
    return (jnp.cos(latitude_angle), jnp.sin(latitude_angle))


def flip(tiles):
    row = lax.broadcasted_iota(jnp.int32, tiles[0].shape, 0)
    for d in (4, 2, 1):
        keep = (row & d) == 0
        turned = list(tiles)
        for i in range(SUBLANES):
            if not i & d:
                a, b = tiles[i], tiles[i + d]
                turned[i] = jnp.where(keep, a, pltpu.roll(b, d, 0))
                turned[i + d] = jnp.where(keep, pltpu.roll(a, SUBLANES - d, 0), b)
        tiles = turned
    return tiles


def outer_rows_kernel(prog, last, first):
    _, levels, rows, _ = prog.shape
    for f in range(3):
        for l in range(levels):
            c = f * levels + l
            last[c : c + 1, :] = prog[f, l, rows - 1 : rows, :]
            first[c : c + 1, :] = prog[f, l, 0:1, :]


def tendency_kernel(prog, zonal, coriolis, out, turn, edges):
    _, levels, rows, width = prog.shape
    chans = 3 * levels
    payload = 2 * chans
    row_id = lax.broadcasted_iota(jnp.int32, (rows, width), 0)
    col_id = lax.broadcasted_iota(jnp.int32, (rows, width), 1)
    lane_id = lax.broadcasted_iota(jnp.int32, (rows, HALF), 1)
    first_row, last_row = row_id == 0, row_id == rows - 1
    first_col, last_col = col_id == 0, col_id == width - 1
    zon, cor = zonal[...], coriolis[...]
    edge_rows = jnp.zeros((rows, HALF), jnp.float32)
    for l in range(levels):
        centre, dx, dy, sx = [], [], [], []
        for f in range(3):
            c = f * levels + l
            here = prog[f, l]
            e = jnp.where(last_col, 0.0, pltpu.roll(here, width - 1, 1))
            w = jnp.where(first_col, 0.0, pltpu.roll(here, 1, 1))
            n = jnp.where(last_row, 0.0, pltpu.roll(here, rows - 1, 0))
            s = jnp.where(first_row, 0.0, pltpu.roll(here, 1, 0))
            centre.append(here)
            dx.append(e - w)
            dy.append(n - s)
            sx.append(e + w + n + s - 4.0 * here)
            first = here[:, :HALF]
            last = here[:, width - HALF :]
            if c:
                first = pltpu.roll(first, c, 1)
            last = pltpu.roll(last, (chans + c + 1) % HALF, 1)
            edge_rows = jnp.where(lane_id == c, first, jnp.where(lane_id == chans + c, last, edge_rows))
        tends = (
            -zon * dx[2] + cor * centre[1] + VISCOSITY * sx[0],
            -MERIDIONAL * dy[2] - cor * centre[0] + VISCOSITY * sx[1],
            -zon * dx[0] - MERIDIONAL * dy[1],
        )
        for f in range(3):
            turn[f, l] = tends[f]
    edges[...] = edge_rows
    for chunk in range(rows // SUBLANES):
        some = slice(chunk * SUBLANES, (chunk + 1) * SUBLANES)
        for f in range(3):
            for half in range(2):
                for l0 in range(0, levels, SUBLANES):
                    at = (2 * f + half) * levels + l0
                    flipped = flip(
                        [turn[f, l0 + i, some, half * HALF : (half + 1) * HALF] for i in range(SUBLANES)]
                    )
                    for k, value in enumerate(flipped):
                        j = chunk * SUBLANES + k
                        out[j, at : at + SUBLANES, :] = value
        for k in range(SUBLANES):
            j = chunk * SUBLANES + k
            out[j, payload:, :] = jnp.broadcast_to(edges[j : j + 1, :], (SUBLANES, HALF))


def seam_kernel(own_block, south, north, tend, whole, *outs_and_sems):
    del tend
    outs, sems = outs_and_sems[:-1], outs_and_sems[-1]
    chans = south.shape[0]
    levels = chans // 3
    rows = whole.shape[0]
    per_owner = rows // len(outs)
    for row, beyond, slope in ((0, south, -MERIDIONAL), (rows - 1, north, MERIDIONAL)):
        for half in range(2):
            lanes = slice(half * HALF, (half + 1) * HALF)
            u, v, h = (beyond[f * levels : (f + 1) * levels, lanes] for f in range(3))
            for f, term in enumerate((VISCOSITY * u, VISCOSITY * v - slope * h, -slope * v)):
                some = slice((2 * f + half) * levels, (2 * f + half + 1) * levels)
                whole[row, some, :] = whole[row, some, :] + term
    copies = []
    for s, out in enumerate(outs):
        first = (own_block[0] ^ s) * per_owner
        copies.append(pltpu.make_async_copy(whole.at[pl.ds(first, per_owner)], out, sems.at[s]))
        copies[-1].start()
    for copy in copies:
        copy.wait()


def split2(x):
    hi = x.astype(jnp.bfloat16)
    return hi, (x - hi.astype(jnp.float32)).astype(jnp.bfloat16)


def mix_operand(matrix):
    hi, lo = split2(matrix)
    return jnp.concatenate([hi, hi, lo], axis=1)


def filter_kernel(own_block, half_width, filter_mask, zonal, *refs):
    halves, parts, seam, beyond_east, beyond_west = refs[-5:]
    blocks = (len(refs) - 5) // 2
    arrived, outs = refs[:blocks], refs[blocks : 2 * blocks]
    own_rows, _, _, levels, _ = outs[0].shape
    chans = 3 * levels
    payload = 2 * chans
    count = 2 * blocks
    both = own_rows * chans
    me = own_block[0]
    reach, scale, filtered, edge_gain, sides = [], [], [], [], []
    for s, tend in enumerate(arrived):
        for part in range(own_rows):
            seam[pl.ds((me ^ s) * own_rows + part, 1), :] = tend[part, payload : payload + 1, :]
    for s in range(blocks):
        for side, turn in ((beyond_east, 1), (beyond_west, blocks - 1)):
            source = lax.rem((me ^ s) + turn, blocks) * own_rows
            for part in range(own_rows):
                at = s * own_rows + part
                side[at : at + 1, :] = seam[pl.ds(source + part, 1), :]
    columns = (beyond_west[...].T, beyond_east[...].T)
    for part in range(own_rows):
        row = me * own_rows + part
        reach.append(half_width[row])
        whole = reach[part] == count // 2
        norm = jnp.where(whole, count * HALF, 2 * HALF * reach[part] + 1).astype(jnp.float32)
        scale.append(TIME_STEP / norm)
        filtered.append(filter_mask[row] == 1)
        edge_gain.append(jnp.where(whole, 0.0, 1.0).astype(jnp.float32))
        zon = zonal[row]
        terms = []
        for start, sign, side in ((chans, 1.0, columns[0]), (0, -1.0, columns[1])):
            u, v, h = (side[start + f * levels : start + (f + 1) * levels] for f in range(3))
            terms.append(jnp.concatenate([VISCOSITY * u + sign * zon * h, VISCOSITY * v, sign * zon * u], axis=0))
        sides.append(terms)
    lane_id = lax.broadcasted_iota(jnp.int32, (chans, HALF), 1)
    windows = [jnp.zeros((chans, HALF), jnp.float32) for _ in range(own_rows)]
    for s, tend in enumerate(arrived):
        for half in range(2):
            g = 2 * (me ^ s) + half
            lane = HALF - 1 if half else 0
            for part in range(own_rows):
                source = s * own_rows + part
                here = jnp.concatenate(
                    [tend[part, (2 * f + half) * levels : (2 * f + half + 1) * levels, :] for f in range(3)], axis=0
                )
                value = here + jnp.where(lane_id == lane, sides[part][half][:, source : source + 1], 0.0)
                halves[g, part * chans : (part + 1) * chans, :] = value
                inside = lax.rem(g + reach[part], count) < 2 * reach[part]
                windows[part] = windows[part] + jnp.where(inside, 1.0, 0.0).astype(jnp.float32) * value

    src = lax.broadcasted_iota(jnp.int32, (2 * HALF, HALF), 0)
    dst = lax.broadcasted_iota(jnp.int32, (2 * HALF, HALF), 1)
    sums = jnp.where((src <= dst) | (src >= HALF), 1.0, 0.0).astype(jnp.bfloat16)

    for g in range(count):
        for part in range(own_rows):
            some = slice(part * chans, (part + 1) * chans)
            ahead = halves[lax.rem(g + reach[part], count), some, :]
            behind = halves[lax.rem(g + count - reach[part], count), some, :]
            change = ahead - behind
            at = g * both + part * chans
            for k, (a, b) in enumerate(zip(split2(change), split2(windows[part]))):
                parts[k, at : at + chans, :HALF] = a
                parts[k, at : at + chans, HALF:] = b
            windows[part] = windows[part] + change

    for s, out in enumerate(outs):
        b = me ^ s
        some = pl.ds(pl.multiple_of(b * 2 * both, 2 * both), 2 * both)
        box = jnp.dot(parts[1, some, :], sums, preferred_element_type=jnp.float32) + jnp.dot(
            parts[0, some, :], sums, preferred_element_type=jnp.float32
        )
        for half in range(2):
            g = 2 * b + half
            for part in range(own_rows):
                some = slice(part * chans, (part + 1) * chans)
                at = half * both + part * chans
                behind = halves[lax.rem(g + count - reach[part], count), some, :]
                smooth = (box[at : at + chans] + edge_gain[part] * behind) * scale[part]
                step = jnp.where(filtered[part], smooth, TIME_STEP * halves[g, some, :])
                for f in range(3):
                    out[part, f, half] = step[f * levels : (f + 1) * levels]


def gather_kernel(own_block, *refs):
    returned, (winds, height) = refs[:-2], refs[-2:]
    for s, part in enumerate(returned):
        for row in range(part.shape[0]):
            j = (own_block[0] ^ s) * part.shape[0] + row
            winds[j] = part[row, :2]
            height[j] = part[row, 2]


def base_kernel(own_part, own, other, matrix, out):
    _, levels, rows, width = own.shape
    lower = own_part[0] == 0

    def by_row(ref, f, j0):
        flipped = [
            flip([ref[f, l0 + i, j0 : j0 + SUBLANES, :] for i in range(SUBLANES)])
            for l0 in range(0, levels, SUBLANES)
        ]
        return [jnp.concatenate([part[k] for part in flipped], axis=0) for k in range(SUBLANES)]

    for j0 in range(0, rows, SUBLANES):
        mine = [by_row(own, f, j0) for f in range(3)]
        theirs = [by_row(other, f, j0) for f in range(2)]
        for k in range(SUBLANES):
            j = j0 + k
            winds = []
            for f in range(2):
                a, b = mine[f][k], theirs[f][k]
                winds.append(jnp.concatenate([jnp.where(lower, a, b), jnp.where(lower, b, a)], axis=0))
            wind_hi, wind_lo = split2(jnp.concatenate(winds, axis=1))
            mixed = jnp.dot(
                mix_operand(matrix[j]),
                jnp.concatenate([wind_hi, wind_lo, wind_hi], axis=0),
                preferred_element_type=jnp.float32,
            )
            kept = jnp.where(lower, mixed[:levels], mixed[levels:])
            for f in range(2):
                out[j, f, 0] = kept[:, f * width : (f + 1) * width]
            out[j, 2, 0] = mine[2][k]


def finish_kernel(own_part, step, height, other, base, matrix, out, added, stage, in_sems, out_sems):
    fields, levels, rows, _ = out.shape
    lower = own_part[0] == 0
    loads, copies = [], []
    for part in range(rows // SUBLANES):
        some = pl.ds(part * SUBLANES, SUBLANES)
        loads.append(pltpu.make_async_copy(base.at[some], added.at[some], in_sems.at[part]))
        loads[-1].start()
    for part in range(rows // SUBLANES):
        loads[part].wait()
        j0 = part * SUBLANES
        values = []
        for j in range(j0, j0 + SUBLANES):
            winds = []
            for f in range(2):
                for half in range(2):
                    a, b = step[j, f, half], other[j, f, half]
                    winds.append(jnp.concatenate([jnp.where(lower, a, b), jnp.where(lower, b, a)], axis=0))
            wind_hi, wind_lo = split2(jnp.concatenate(winds, axis=1))
            mixed = jnp.dot(
                mix_operand(matrix[j]),
                jnp.concatenate([wind_hi, wind_lo, wind_hi], axis=0),
                preferred_element_type=jnp.float32,
            )
            kept = jnp.where(lower, mixed[:levels], mixed[levels:])
            pieces = [kept[:, n * HALF : (n + 1) * HALF] for n in range(4)] + [height[j, 0], height[j, 1]]
            values.append([piece + added[j, n // 2, n % 2] for n, piece in enumerate(pieces)])
        for n in range(6):
            f, half = divmod(n, 2)
            for l0 in range(0, levels, SUBLANES):
                flipped = flip([values[k][n][l0 : l0 + SUBLANES] for k in range(SUBLANES)])
                for i, value in enumerate(flipped):
                    stage[f, l0 + i, j0 : j0 + SUBLANES, half * HALF : (half + 1) * HALF] = value
        some = pl.ds(j0, SUBLANES)
        copies.append(pltpu.make_async_copy(stage.at[:, :, some], out.at[:, :, some], out_sems.at[part]))
        copies[-1].start()
    for copy in copies:
        copy.wait()


def per_device(prognostic, half_width, filter_mask, column_inverse):
    fields, levels, rows, width = prognostic.shape
    lon_devices, lat_devices = (lax.axis_size(a) for a in ("lon", "lat"))
    lon_index, lat_index, lev_index = (lax.axis_index(a) for a in ("lon", "lat", "lev"))
    chans = fields * levels
    halves = width // HALF
    params = pltpu.CompilerParams(vmem_limit_bytes=VMEM_LIMIT)
    hbm = pl.BlockSpec(memory_space=pltpu.HBM)
    vmem = pl.BlockSpec(memory_space=pltpu.VMEM)

    def in_hbm(x):
        return pltpu.with_memory_space_constraint(x, pltpu.HBM)

    def in_vmem(x):
        return pltpu.with_memory_space_constraint(x, pltpu.VMEM)


    with jax.named_scope("outer_rows"):
        last, first = pl.pallas_call(
            outer_rows_kernel,
            out_shape=(pltpu.VMEM((chans, width), jnp.float32),) * 2,
            in_specs=[vmem],
            out_specs=(vmem, vmem),
            compiler_params=params,
        )(in_vmem(prognostic))
    south = lax.ppermute(last, "lat", [(i, i + 1) for i in range(lat_devices - 1)])
    north = lax.ppermute(first, "lat", [(i + 1, i) for i in range(lat_devices - 1)])
    other = lax.ppermute(prognostic[:2], "lev", [(0, 1), (1, 0)])

    global_rows = (lat_index * rows + jnp.arange(rows)).astype(jnp.float32)
    cosine, sine = latitudes(global_rows, rows * lat_devices)
    zonal = 0.25 / (cosine + 0.05)
    zonal_field = jnp.broadcast_to(zonal[:, None], (rows, width))
    coriolis_field = jnp.broadcast_to((0.5 * sine)[:, None], (rows, width))

    sent_rows = halves * chans + SUBLANES
    with jax.named_scope("tendencies"):
        tend = pl.pallas_call(
            tendency_kernel,
            out_shape=pltpu.VMEM((rows, sent_rows, HALF), jnp.float32),
            in_specs=[vmem, vmem, vmem],
            out_specs=vmem,
            scratch_shapes=[
                pltpu.VMEM(prognostic.shape, jnp.float32),
                pltpu.VMEM((rows, HALF), jnp.float32),
            ],
            compiler_params=params,
        )(in_vmem(prognostic), zonal_field, coriolis_field)

    own_rows = rows // lon_devices
    own_block = lon_index.astype(jnp.int32).reshape(1)

    def exchange(pieces):
        return [pieces[0]] + [
            lax.ppermute(piece, "lon", [(i, i ^ s) for i in range(lon_devices)])
            for s, piece in enumerate(pieces)
            if s
        ]

    with jax.named_scope("seam_rows"):
        parted = pl.pallas_call(
            seam_kernel,
            out_shape=(pltpu.VMEM(tend.shape, jnp.float32),)
            + (pltpu.VMEM((own_rows, sent_rows, HALF), jnp.float32),) * lon_devices,
            grid_spec=pltpu.PrefetchScalarGridSpec(
                num_scalar_prefetch=1,
                grid=(1,),
                in_specs=[vmem] * 3,
                out_specs=(vmem,) * (lon_devices + 1),
                scratch_shapes=[pltpu.SemaphoreType.DMA((lon_devices,))],
            ),
            input_output_aliases={3: 0},
            compiler_params=params,
        )(own_block, in_vmem(south), in_vmem(north), in_vmem(tend))[1:]

    arrived = exchange(parted)

    stepped_shape = (own_rows, fields, halves, levels, HALF)
    count = halves * lon_devices
    both = own_rows * chans
    with jax.named_scope("row_filter"):
        stepped = pl.pallas_call(
            filter_kernel,
            out_shape=(pltpu.VMEM(stepped_shape, jnp.float32),) * lon_devices,
            grid_spec=pltpu.PrefetchScalarGridSpec(
                num_scalar_prefetch=4,
                grid=(1,),
                in_specs=[vmem] * lon_devices,
                out_specs=(vmem,) * lon_devices,
                scratch_shapes=[
                    pltpu.VMEM((count, both, HALF), jnp.float32),
                    pltpu.VMEM((2, count * both, 2 * HALF), jnp.bfloat16),
                ]
                + [pltpu.VMEM((HALF, HALF), jnp.float32)] * 3,
            ),
            compiler_params=params,
        )(own_block, half_width, filter_mask, zonal, *[in_vmem(piece) for piece in arrived])

    returned = exchange(stepped)
    with jax.named_scope("gather_rows"):
        winds, height = pl.pallas_call(
            gather_kernel,
            out_shape=(
                pltpu.VMEM((rows, 2) + stepped_shape[2:], jnp.float32),
                pltpu.VMEM((rows,) + stepped_shape[2:], jnp.float32),
            ),
            grid_spec=pltpu.PrefetchScalarGridSpec(
                num_scalar_prefetch=1,
                grid=(1,),
                in_specs=[vmem] * lon_devices,
                out_specs=(vmem, vmem),
            ),
            compiler_params=params,
        )(own_block, *[in_vmem(piece) for piece in returned])
    winds_beyond = lax.ppermute(winds, "lev", [(0, 1), (1, 0)])

    with jax.named_scope("base"):
        base = pl.pallas_call(
            base_kernel,
            out_shape=pltpu.HBM((rows,) + stepped_shape[1:], jnp.float32),
            grid_spec=pltpu.PrefetchScalarGridSpec(
                num_scalar_prefetch=1,
                grid=(halves,),
                in_specs=[
                    pl.BlockSpec((fields, levels, rows, HALF), lambda i, *_: (0, 0, 0, i)),
                    pl.BlockSpec((2, levels, rows, HALF), lambda i, *_: (0, 0, 0, i)),
                    pl.BlockSpec(column_inverse.shape, lambda i, *_: (0, 0, 0)),
                ],
                out_specs=pl.BlockSpec((rows, fields, 1, levels, HALF), lambda i, *_: (0, 0, i, 0, 0)),
            ),
            compiler_params=params,
        )(lev_index.astype(jnp.int32).reshape(1), prognostic, other, column_inverse)

    with jax.named_scope("finish"):
        return pl.pallas_call(
            finish_kernel,
            out_shape=jax.ShapeDtypeStruct(prognostic.shape, jnp.float32),
            grid_spec=pltpu.PrefetchScalarGridSpec(
                num_scalar_prefetch=1,
                grid=(1,),
                in_specs=[vmem, vmem, vmem, hbm, vmem],
                out_specs=hbm,
                scratch_shapes=[
                    pltpu.VMEM((rows,) + stepped_shape[1:], jnp.float32),
                    pltpu.VMEM(prognostic.shape, jnp.float32),
                    pltpu.SemaphoreType.DMA((rows // SUBLANES,)),
                    pltpu.SemaphoreType.DMA((rows // SUBLANES,)),
                ],
            ),
            compiler_params=params,
        )(
            lev_index.astype(jnp.int32).reshape(1),
            in_vmem(winds),
            in_vmem(height),
            in_vmem(winds_beyond),
            in_hbm(base),
            column_inverse,
        )


def solution(mesh):
    placed = (P(None, "lev", "lat", "lon"), P("lat"), P("lat"), P("lat", None, None))
    return jax.shard_map(
        per_device,
        mesh=mesh,
        in_specs=placed,
        out_specs=P(None, "lev", "lat", "lon"),
        check_vma=False,
    )
```

```python
import jax
import jax.numpy as jnp
from jax import lax
from jax.experimental import pallas as pl
from jax.experimental.pallas import tpu as pltpu
from jax.sharding import PartitionSpec as P

TIME_STEP = 0.5
VISCOSITY = 0.05
MERIDIONAL = 0.25
HALF = 128
SUBLANES = 8
VMEM_LIMIT = 32 * 1024 * 1024
GROUP = 4
LOADS = 4


def latitudes(global_rows, row_total):
    latitude_angle = -0.5 * jnp.pi + (global_rows + 0.5) * jnp.pi / row_total
    return (jnp.cos(latitude_angle), jnp.sin(latitude_angle))


def flip(tiles):
    row = lax.broadcasted_iota(jnp.int32, tiles[0].shape, 0)
    for d in (4, 2, 1):
        keep = (row & d) == 0
        turned = list(tiles)
        for i in range(SUBLANES):
            if not i & d:
                a, b = tiles[i], tiles[i + d]
                turned[i] = jnp.where(keep, a, pltpu.roll(b, d, 0))
                turned[i + d] = jnp.where(keep, pltpu.roll(a, SUBLANES - d, 0), b)
        tiles = turned
    return tiles


def fetch_kernel(prog, tile, last, first, sems):
    fields, levels, rows, _ = prog.shape
    per_load = levels // LOADS
    loads = []
    for f in range(fields):
        for load in range(LOADS):
            some = pl.ds(load * per_load, per_load)
            loads.append(pltpu.make_async_copy(prog.at[f, some], tile.at[f, some], sems.at[f, load]))
            loads[-1].start()
    for f in range(fields):
        for l in range(levels):
            if l % per_load == 0:
                loads[f * LOADS + l // per_load].wait()
            c = f * levels + l
            last[c : c + 1, :] = tile[f, l, rows - 1 : rows, :]
            first[c : c + 1, :] = tile[f, l, 0:1, :]


def tendency_kernel(prog, zonal, coriolis, out, ends, turn, edges, stage, out_sems):
    _, levels, rows, width = prog.shape
    chans = 3 * levels
    payload = 2 * chans
    row_id = lax.broadcasted_iota(jnp.int32, (rows, width), 0)
    col_id = lax.broadcasted_iota(jnp.int32, (rows, width), 1)
    lane_id = lax.broadcasted_iota(jnp.int32, (rows, HALF), 1)
    first_row, last_row = row_id == 0, row_id == rows - 1
    first_col, last_col = col_id == 0, col_id == width - 1
    zon, cor = zonal[...], coriolis[...]
    edge_rows = jnp.zeros((rows, HALF), jnp.float32)
    for l in range(levels):
        centre, dx, dy, sx = [], [], [], []
        for f in range(3):
            c = f * levels + l
            here = prog[f, l]
            e = jnp.where(last_col, 0.0, pltpu.roll(here, width - 1, 1))
            w = jnp.where(first_col, 0.0, pltpu.roll(here, 1, 1))
            n = jnp.where(last_row, 0.0, pltpu.roll(here, rows - 1, 0))
            s = jnp.where(first_row, 0.0, pltpu.roll(here, 1, 0))
            centre.append(here)
            dx.append(e - w)
            dy.append(n - s)
            sx.append(e + w + n + s - 4.0 * here)
            first = here[:, :HALF]
            last = here[:, width - HALF :]
            if c:
                first = pltpu.roll(first, c, 1)
            last = pltpu.roll(last, (chans + c + 1) % HALF, 1)
            edge_rows = jnp.where(lane_id == c, first, jnp.where(lane_id == chans + c, last, edge_rows))
        tends = (
            -zon * dx[2] + cor * centre[1] + VISCOSITY * sx[0],
            -MERIDIONAL * dy[2] - cor * centre[0] + VISCOSITY * sx[1],
            -zon * dx[0] - MERIDIONAL * dy[1],
        )
        for f in range(3):
            turn[f, l] = tends[f]
    edges[...] = edge_rows
    copies = []
    for chunk in range(rows // SUBLANES):
        some = slice(chunk * SUBLANES, (chunk + 1) * SUBLANES)
        for f in range(3):
            for half in range(2):
                for l0 in range(0, levels, SUBLANES):
                    at = (2 * f + half) * levels + l0
                    flipped = flip(
                        [turn[f, l0 + i, some, half * HALF : (half + 1) * HALF] for i in range(SUBLANES)]
                    )
                    for k, value in enumerate(flipped):
                        j = chunk * SUBLANES + k
                        stage[j, at : at + SUBLANES, :] = value
                        if j in (0, rows - 1):
                            ends[min(j, 1), at : at + SUBLANES, :] = value
        for k in range(SUBLANES):
            j = chunk * SUBLANES + k
            stage[j, payload:, :] = jnp.broadcast_to(edges[j : j + 1, :], (SUBLANES, HALF))
        some = pl.ds(chunk * SUBLANES, SUBLANES)
        copies.append(pltpu.make_async_copy(stage.at[some], out.at[some], out_sems.at[chunk]))
        copies[-1].start()
    for copy in copies:
        copy.wait()


def seam_kernel(ends, south, north, tend, out, stage, sems):
    del tend
    chans = south.shape[0]
    levels = chans // 3
    copies = []
    for at, beyond, sign in ((0, south, -1.0), (1, north, 1.0)):
        for half in range(2):
            lanes = slice(half * HALF, (half + 1) * HALF)
            u, v, h = (beyond[f * levels : (f + 1) * levels, lanes] for f in range(3))
            slope = sign * MERIDIONAL
            for f, term in enumerate((VISCOSITY * u, VISCOSITY * v - slope * h, -slope * v)):
                some = slice((2 * f + half) * levels, (2 * f + half + 1) * levels)
                stage[at, some, :] = ends[at, some, :] + term
        row = at * (out.shape[0] - 1)
        copies.append(pltpu.make_async_copy(stage.at[at], out.at[row, pl.ds(0, 2 * chans)], sems.at[at]))
        copies[-1].start()
    for copy in copies:
        copy.wait()


def split2(x):
    hi = x.astype(jnp.bfloat16)
    return hi, (x - hi.astype(jnp.float32)).astype(jnp.bfloat16)


def mix_operand(matrix):
    hi, lo = split2(matrix)
    return jnp.concatenate([hi, hi, lo], axis=1)


def pair_mix_operand(matrix):
    hi, lo = split2(matrix)
    none = jnp.zeros_like(hi)
    return jnp.concatenate(
        [
            jnp.concatenate([hi, hi, none, none], axis=1),
            jnp.concatenate([none, none, hi, hi], axis=1),
            jnp.concatenate([lo, none, none, none], axis=1),
            jnp.concatenate([none, none, lo, none], axis=1),
        ],
        axis=0,
    )


def filter_kernel(
    own_row, half_width, filter_mask, zonal, tend, matrices, out, halves, parts, seam, matrix, stage, matrix_sem, sems
):
    blocks, lev_parts, levels = out.shape[0], out.shape[1], out.shape[4]
    chans = 3 * levels
    payload = 2 * chans
    count = 2 * blocks
    both = lev_parts * chans
    row = own_row[0]
    fetch = pltpu.make_async_copy(matrices.at[row], matrix, matrix_sem)
    fetch.start()
    reach = half_width[row]
    whole = reach == count // 2
    norm = jnp.where(whole, count * HALF, 2 * HALF * reach + 1).astype(jnp.float32)
    filtered = filter_mask[row] == 1
    edge_gain = jnp.where(whole, 0.0, 1.0).astype(jnp.float32)

    for b in range(blocks):
        for part in range(lev_parts):
            at = b * lev_parts + part
            seam[at : at + 1, :] = tend[b, part, payload : payload + 1, :]
    columns = seam[...].T
    zon = zonal[row]
    u, v, h = (columns[f * levels : (f + 1) * levels] for f in range(3))
    from_east = jnp.concatenate([VISCOSITY * u - zon * h, VISCOSITY * v, -zon * u], axis=0)
    u, v, h = (columns[chans + f * levels : chans + (f + 1) * levels] for f in range(3))
    from_west = jnp.concatenate([VISCOSITY * u + zon * h, VISCOSITY * v, zon * u], axis=0)
    lane_id = lax.broadcasted_iota(jnp.int32, (levels, HALF), 1)
    window = jnp.zeros((both, HALF), jnp.float32)
    for g in range(count):
        b, half = divmod(g, 2)
        beyond = (b + 1) % blocks if half else (b + blocks - 1) % blocks
        terms, lane = (from_east, HALF - 1) if half else (from_west, 0)
        pieces = []
        for part in range(lev_parts):
            source = beyond * lev_parts + part
            for f in range(3):
                here = tend[b, part, (2 * f + half) * levels : (2 * f + half + 1) * levels, :]
                term = terms[f * levels : (f + 1) * levels, source : source + 1]
                pieces.append(here + jnp.where(lane_id == lane, term, 0.0))
        value = jnp.concatenate(pieces, axis=0)
        halves[g] = value
        inside = lax.rem(g + reach, count) < 2 * reach
        window = window + jnp.where(inside, 1.0, 0.0).astype(jnp.float32) * value

    src = lax.broadcasted_iota(jnp.int32, (2 * HALF, 2 * HALF), 0)
    dst = lax.broadcasted_iota(jnp.int32, (2 * HALF, 2 * HALF), 1)
    sums = jnp.where((src & (HALF - 1)) <= dst, 1.0, 0.0).astype(jnp.bfloat16)
    fetch.wait()
    mixer = pair_mix_operand(matrix[...])
    scale = TIME_STEP / norm
    total = jnp.dot(
        jnp.concatenate(split2(window), axis=1), sums, preferred_element_type=jnp.float32
    )[:, HALF:]

    def split_group(g0):
        for g in range(g0, g0 + GROUP):
            ahead = halves[lax.rem(g + reach, count)]
            behind = halves[lax.rem(g + count - reach, count)]
            hi, lo = split2(ahead - behind)
            parts[g * both : (g + 1) * both, :HALF] = hi
            parts[g * both : (g + 1) * both, HALF:] = lo

    copies = []

    def finish_group(g0, total):
        box = jnp.dot(parts[g0 * both : (g0 + GROUP) * both, :], sums, preferred_element_type=jnp.float32)
        for pair in range(GROUP // 2):
            b = g0 // 2 + pair
            steps = []
            for half in range(2):
                g = 2 * b + half
                at = (g - g0) * both
                behind = halves[lax.rem(g + count - reach, count)]
                smooth = (box[at : at + both, :HALF] + total + edge_gain * behind) * scale
                total = total + box[at : at + both, HALF:]
                step = jnp.where(filtered, smooth, TIME_STEP * halves[g])
                for p in range(lev_parts):
                    stage[b, p, 2, half] = step[p * chans + 2 * levels : (p + 1) * chans]
                steps.append(step)
            step = jnp.concatenate(steps, axis=1)
            winds = []
            for f in range(2):
                winds += split2(
                    jnp.concatenate(
                        [step[p * chans + f * levels : p * chans + (f + 1) * levels] for p in range(lev_parts)],
                        axis=0,
                    )
                )
            mixed = jnp.dot(mixer, jnp.concatenate(winds, axis=0), preferred_element_type=jnp.float32)
            mixed = mixed[: 2 * lev_parts * levels] + mixed[2 * lev_parts * levels :]
            for f in range(2):
                for p in range(lev_parts):
                    at = (f * lev_parts + p) * levels
                    for half in range(2):
                        stage[b, p, f, half] = mixed[at : at + levels, half * HALF : (half + 1) * HALF]
            copies.append(pltpu.make_async_copy(stage.at[b], out.at[b], sems.at[b]))
            copies[-1].start()
        return total

    split_group(0)
    for g0 in range(0, count, GROUP):
        if g0 + GROUP < count:
            split_group(g0 + GROUP)
        total = finish_group(g0, total)
    for copy in copies:
        copy.wait()


def base_kernel(own_part, own, other, matrix, out):
    _, levels, rows, width = own.shape
    lower = own_part[0] == 0

    def by_row(ref, f, j0):
        flipped = [
            flip([ref[f, l0 + i, j0 : j0 + SUBLANES, :] for i in range(SUBLANES)])
            for l0 in range(0, levels, SUBLANES)
        ]
        return [jnp.concatenate([part[k] for part in flipped], axis=0) for k in range(SUBLANES)]

    for j0 in range(0, rows, SUBLANES):
        mine = [by_row(own, f, j0) for f in range(3)]
        theirs = [by_row(other, f, j0) for f in range(2)]
        for k in range(SUBLANES):
            j = j0 + k
            winds = []
            for f in range(2):
                a, b = mine[f][k], theirs[f][k]
                winds.append(jnp.concatenate([jnp.where(lower, a, b), jnp.where(lower, b, a)], axis=0))
            wind_hi, wind_lo = split2(jnp.concatenate(winds, axis=1))
            mixed = jnp.dot(
                mix_operand(matrix[j]),
                jnp.concatenate([wind_hi, wind_lo, wind_hi], axis=0),
                preferred_element_type=jnp.float32,
            )
            kept = jnp.where(lower, mixed[:levels], mixed[levels:])
            for f in range(2):
                out[j, f, 0] = kept[:, f * width : (f + 1) * width]
            out[j, 2, 0] = mine[2][k]


def finish_kernel(step, base, out, added, stage, in_sems, out_sems):
    fields, levels, rows, _ = out.shape
    blocks = levels // SUBLANES
    loads, copies = [], []
    for f in range(fields):
        for n in range(blocks):
            some = pl.ds(n * SUBLANES, SUBLANES)
            loads.append(
                pltpu.make_async_copy(base.at[:, f, :, some], added.at[:, f, :, some], in_sems.at[f * blocks + n])
            )
            loads[-1].start()
    for f in range(fields):
        for n in range(blocks):
            loads[f * blocks + n].wait()
            l0 = n * SUBLANES
            some = slice(l0, l0 + SUBLANES)
            for half in range(2):
                for j0 in range(0, rows, SUBLANES):
                    flipped = flip(
                        [step[j0 + k, f, half, some, :] + added[j0 + k, f, half, some, :] for k in range(SUBLANES)]
                    )
                    for i, value in enumerate(flipped):
                        stage[f, l0 + i, j0 : j0 + SUBLANES, half * HALF : (half + 1) * HALF] = value
            some = pl.ds(l0, SUBLANES)
            copies.append(
                pltpu.make_async_copy(stage.at[f, some], out.at[f, some], out_sems.at[f * blocks + n])
            )
            copies[-1].start()
    for copy in copies:
        copy.wait()


def per_device(prognostic, half_width, filter_mask, column_inverse):
    fields, levels, rows, width = prognostic.shape
    lon_devices, lat_devices, lev_devices = (lax.axis_size(a) for a in ("lon", "lat", "lev"))
    lon_index, lat_index, lev_index = (lax.axis_index(a) for a in ("lon", "lat", "lev"))
    chans = fields * levels
    halves = width // HALF
    params = pltpu.CompilerParams(vmem_limit_bytes=VMEM_LIMIT)
    hbm = pl.BlockSpec(memory_space=pltpu.HBM)
    vmem = pl.BlockSpec(memory_space=pltpu.VMEM)

    def in_hbm(x):
        return pltpu.with_memory_space_constraint(x, pltpu.HBM)

    def in_vmem(x):
        return pltpu.with_memory_space_constraint(x, pltpu.VMEM)


    with jax.named_scope("fetch"):
        tile, last, first = pl.pallas_call(
            fetch_kernel,
            out_shape=(
                pltpu.VMEM(prognostic.shape, jnp.float32),
                pltpu.VMEM((chans, width), jnp.float32),
                pltpu.VMEM((chans, width), jnp.float32),
            ),
            in_specs=[hbm],
            out_specs=(vmem, vmem, vmem),
            scratch_shapes=[pltpu.SemaphoreType.DMA((fields, LOADS))],
            compiler_params=params,
        )(in_hbm(prognostic))
    south = lax.ppermute(last, "lat", [(i, i + 1) for i in range(lat_devices - 1)])
    north = lax.ppermute(first, "lat", [(i + 1, i) for i in range(lat_devices - 1)])
    other = lax.ppermute(prognostic[:2], "lev", [(0, 1), (1, 0)])

    global_rows = (lat_index * rows + jnp.arange(rows)).astype(jnp.float32)
    cosine, sine = latitudes(global_rows, rows * lat_devices)
    zonal = 0.25 / (cosine + 0.05)
    zonal_field = jnp.broadcast_to(zonal[:, None], (rows, width))
    coriolis_field = jnp.broadcast_to((0.5 * sine)[:, None], (rows, width))

    sent_rows = halves * chans + SUBLANES
    with jax.named_scope("tendencies"):
        tend, ends = pl.pallas_call(
            tendency_kernel,
            out_shape=(
                pltpu.HBM((rows, sent_rows, HALF), jnp.float32),
                pltpu.VMEM((2, halves * chans, HALF), jnp.float32),
            ),
            in_specs=[vmem, vmem, vmem],
            out_specs=(hbm, vmem),
            scratch_shapes=[
                pltpu.VMEM(prognostic.shape, jnp.float32),
                pltpu.VMEM((rows, HALF), jnp.float32),
                pltpu.VMEM((rows, sent_rows, HALF), jnp.float32),
                pltpu.SemaphoreType.DMA((rows // SUBLANES,)),
            ],
            compiler_params=params,
        )(in_vmem(tile), zonal_field, coriolis_field)

    with jax.named_scope("seam_rows"):
        tend = pl.pallas_call(
            seam_kernel,
            out_shape=pltpu.HBM(tend.shape, jnp.float32),
            in_specs=[vmem, vmem, vmem, hbm],
            out_specs=hbm,
            input_output_aliases={3: 0},
            scratch_shapes=[pltpu.VMEM(ends.shape, jnp.float32), pltpu.SemaphoreType.DMA((2,))],
            compiler_params=params,
        )(in_vmem(ends), in_vmem(south), in_vmem(north), in_hbm(tend))

    whole_rows = lax.all_to_all(tend, ("lon", "lev"), 0, 0, tiled=True)

    own_row = (lon_index * lev_devices + lev_index).astype(jnp.int32).reshape(1)
    stepped_shape = (lon_devices, lev_devices, fields, halves, levels, HALF)
    count = halves * lon_devices
    both = lev_devices * chans
    with jax.named_scope("row_filter"):
        stepped = pl.pallas_call(
            filter_kernel,
            out_shape=pltpu.HBM(stepped_shape, jnp.float32),
            grid_spec=pltpu.PrefetchScalarGridSpec(
                num_scalar_prefetch=4,
                grid=(1,),
                in_specs=[vmem, hbm],
                out_specs=hbm,
                scratch_shapes=[
                    pltpu.VMEM((count, both, HALF), jnp.float32),
                    pltpu.VMEM((count * both, 2 * HALF), jnp.bfloat16),
                    pltpu.VMEM((HALF, HALF), jnp.float32),
                    pltpu.VMEM(column_inverse.shape[1:], jnp.float32),
                    pltpu.VMEM(stepped_shape, jnp.float32),
                    pltpu.SemaphoreType.DMA,
                    pltpu.SemaphoreType.DMA((lon_devices,)),
                ],
            ),
            compiler_params=params,
        )(
            own_row,
            half_width,
            filter_mask,
            zonal,
            in_vmem(whole_rows.reshape(lon_devices, lev_devices, sent_rows, HALF)),
            in_hbm(column_inverse),
        )

    returned = lax.all_to_all(
        stepped.reshape((rows,) + stepped_shape[2:]), ("lon", "lev"), 0, 0, tiled=True
    )

    with jax.named_scope("base"):
        base = pl.pallas_call(
            base_kernel,
            out_shape=pltpu.HBM(returned.shape, jnp.float32),
            grid_spec=pltpu.PrefetchScalarGridSpec(
                num_scalar_prefetch=1,
                grid=(halves,),
                in_specs=[
                    pl.BlockSpec((fields, levels, rows, HALF), lambda i, *_: (0, 0, 0, i)),
                    pl.BlockSpec((2, levels, rows, HALF), lambda i, *_: (0, 0, 0, i)),
                    pl.BlockSpec(column_inverse.shape, lambda i, *_: (0, 0, 0)),
                ],
                out_specs=pl.BlockSpec((rows, fields, 1, levels, HALF), lambda i, *_: (0, 0, i, 0, 0)),
            ),
            compiler_params=params,
        )(lev_index.astype(jnp.int32).reshape(1), prognostic, other, column_inverse)

    with jax.named_scope("finish"):
        return pl.pallas_call(
            finish_kernel,
            out_shape=jax.ShapeDtypeStruct(prognostic.shape, jnp.float32),
            in_specs=[vmem, hbm],
            out_specs=hbm,
            scratch_shapes=[
                pltpu.VMEM(returned.shape, jnp.float32),
                pltpu.VMEM(prognostic.shape, jnp.float32),
                pltpu.SemaphoreType.DMA((fields * levels // SUBLANES,)),
                pltpu.SemaphoreType.DMA((fields * levels // SUBLANES,)),
            ],
            compiler_params=params,
        )(in_vmem(returned), in_hbm(base))


def solution(mesh):
    placed = (P(None, "lev", "lat", "lon"), P("lat"), P("lat"), P("lat", None, None))
    return jax.shard_map(
        per_device,
        mesh=mesh,
        in_specs=placed,
        out_specs=P(None, "lev", "lat", "lon"),
        check_vma=False,
    )
```

```python
import jax
import jax.numpy as jnp
from jax import lax
from jax.experimental import pallas as pl
from jax.experimental.pallas import tpu as pltpu
from jax.sharding import PartitionSpec as P

TIME_STEP = 0.5
VISCOSITY = 0.05
MERIDIONAL = 0.25
HALF = 128
SUBLANES = 8
VMEM_LIMIT = 32 * 1024 * 1024
GROUP = 4
LOADS = 4


def latitudes(global_rows, row_total):
    latitude_angle = -0.5 * jnp.pi + (global_rows + 0.5) * jnp.pi / row_total
    return (jnp.cos(latitude_angle), jnp.sin(latitude_angle))


def flip(tiles):
    row = lax.broadcasted_iota(jnp.int32, tiles[0].shape, 0)
    for d in (4, 2, 1):
        keep = (row & d) == 0
        turned = list(tiles)
        for i in range(SUBLANES):
            if not i & d:
                a, b = tiles[i], tiles[i + d]
                turned[i] = jnp.where(keep, a, pltpu.roll(b, d, 0))
                turned[i + d] = jnp.where(keep, pltpu.roll(a, SUBLANES - d, 0), b)
        tiles = turned
    return tiles


def fetch_kernel(prog, tile, last, first, sems):
    fields, levels, rows, _ = prog.shape
    per_load = levels // LOADS
    loads = []
    for f in range(fields):
        for load in range(LOADS):
            some = pl.ds(load * per_load, per_load)
            loads.append(pltpu.make_async_copy(prog.at[f, some], tile.at[f, some], sems.at[f, load]))
            loads[-1].start()
    for f in range(fields):
        for l in range(levels):
            if l % per_load == 0:
                loads[f * LOADS + l // per_load].wait()
            c = f * levels + l
            last[c : c + 1, :] = tile[f, l, rows - 1 : rows, :]
            first[c : c + 1, :] = tile[f, l, 0:1, :]


def tendency_kernel(prog, zonal, coriolis, out, ends, turn, edges, stage, out_sems):
    _, levels, rows, width = prog.shape
    chans = 3 * levels
    payload = 2 * chans
    row_id = lax.broadcasted_iota(jnp.int32, (rows, width), 0)
    col_id = lax.broadcasted_iota(jnp.int32, (rows, width), 1)
    lane_id = lax.broadcasted_iota(jnp.int32, (rows, HALF), 1)
    first_row, last_row = row_id == 0, row_id == rows - 1
    first_col, last_col = col_id == 0, col_id == width - 1
    zon, cor = zonal[...], coriolis[...]
    edge_rows = jnp.zeros((rows, HALF), jnp.float32)
    for l in range(levels):
        centre, dx, dy, sx = [], [], [], []
        for f in range(3):
            c = f * levels + l
            here = prog[f, l]
            e = jnp.where(last_col, 0.0, pltpu.roll(here, width - 1, 1))
            w = jnp.where(first_col, 0.0, pltpu.roll(here, 1, 1))
            n = jnp.where(last_row, 0.0, pltpu.roll(here, rows - 1, 0))
            s = jnp.where(first_row, 0.0, pltpu.roll(here, 1, 0))
            centre.append(here)
            dx.append(e - w)
            dy.append(n - s)
            sx.append(e + w + n + s - 4.0 * here)
            first = here[:, :HALF]
            last = here[:, width - HALF :]
            if c:
                first = pltpu.roll(first, c, 1)
            last = pltpu.roll(last, (chans + c + 1) % HALF, 1)
            edge_rows = jnp.where(lane_id == c, first, jnp.where(lane_id == chans + c, last, edge_rows))
        tends = (
            -zon * dx[2] + cor * centre[1] + VISCOSITY * sx[0],
            -MERIDIONAL * dy[2] - cor * centre[0] + VISCOSITY * sx[1],
            -zon * dx[0] - MERIDIONAL * dy[1],
        )
        for f in range(3):
            turn[f, l] = tends[f]
    edges[...] = edge_rows
    copies = []
    for chunk in range(rows // SUBLANES):
        some = slice(chunk * SUBLANES, (chunk + 1) * SUBLANES)
        for f in range(3):
            for half in range(2):
                for l0 in range(0, levels, SUBLANES):
                    at = (2 * f + half) * levels + l0
                    flipped = flip(
                        [turn[f, l0 + i, some, half * HALF : (half + 1) * HALF] for i in range(SUBLANES)]
                    )
                    for k, value in enumerate(flipped):
                        j = chunk * SUBLANES + k
                        stage[j, at : at + SUBLANES, :] = value
                        if j in (0, rows - 1):
                            ends[min(j, 1), at : at + SUBLANES, :] = value
        for k in range(SUBLANES):
            j = chunk * SUBLANES + k
            stage[j, payload:, :] = jnp.broadcast_to(edges[j : j + 1, :], (SUBLANES, HALF))
        some = pl.ds(chunk * SUBLANES, SUBLANES)
        copies.append(pltpu.make_async_copy(stage.at[some], out.at[some], out_sems.at[chunk]))
        copies[-1].start()
    for copy in copies:
        copy.wait()


def seam_kernel(ends, south, north, tend, out, stage, sems):
    del tend
    chans = south.shape[0]
    levels = chans // 3
    copies = []
    for at, beyond, sign in ((0, south, -1.0), (1, north, 1.0)):
        for half in range(2):
            lanes = slice(half * HALF, (half + 1) * HALF)
            u, v, h = (beyond[f * levels : (f + 1) * levels, lanes] for f in range(3))
            slope = sign * MERIDIONAL
            for f, term in enumerate((VISCOSITY * u, VISCOSITY * v - slope * h, -slope * v)):
                some = slice((2 * f + half) * levels, (2 * f + half + 1) * levels)
                stage[at, some, :] = ends[at, some, :] + term
        row = at * (out.shape[0] - 1)
        copies.append(pltpu.make_async_copy(stage.at[at], out.at[row, pl.ds(0, 2 * chans)], sems.at[at]))
        copies[-1].start()
    for copy in copies:
        copy.wait()


def split2(x):
    hi = x.astype(jnp.bfloat16)
    return hi, (x - hi.astype(jnp.float32)).astype(jnp.bfloat16)


def mix_operand(matrix):
    hi, lo = split2(matrix)
    return jnp.concatenate([hi, hi, lo], axis=1)


def pair_mix_operand(matrix):
    hi, lo = split2(matrix)
    none = jnp.zeros_like(hi)
    return jnp.concatenate(
        [
            jnp.concatenate([hi, hi, none, none], axis=1),
            jnp.concatenate([none, none, hi, hi], axis=1),
            jnp.concatenate([lo, none, none, none], axis=1),
            jnp.concatenate([none, none, lo, none], axis=1),
        ],
        axis=0,
    )


def filter_kernel(
    own_row, half_width, filter_mask, zonal, tend, matrices, out, halves, parts, seam, matrix, stage, matrix_sem, sems
):
    lev_parts, blocks, levels = out.shape[0], out.shape[1], out.shape[4]
    chans = 3 * levels
    payload = 2 * chans
    count = 2 * blocks
    both = lev_parts * chans
    row = own_row[0]
    fetch = pltpu.make_async_copy(matrices.at[row], matrix, matrix_sem)
    fetch.start()
    reach = half_width[row]
    whole = reach == count // 2
    norm = jnp.where(whole, count * HALF, 2 * HALF * reach + 1).astype(jnp.float32)
    filtered = filter_mask[row] == 1
    edge_gain = jnp.where(whole, 0.0, 1.0).astype(jnp.float32)

    for b in range(blocks):
        for part in range(lev_parts):
            at = b * lev_parts + part
            seam[at : at + 1, :] = tend[part, b, payload : payload + 1, :]
    columns = seam[...].T
    zon = zonal[row]
    u, v, h = (columns[f * levels : (f + 1) * levels] for f in range(3))
    from_east = jnp.concatenate([VISCOSITY * u - zon * h, VISCOSITY * v, -zon * u], axis=0)
    u, v, h = (columns[chans + f * levels : chans + (f + 1) * levels] for f in range(3))
    from_west = jnp.concatenate([VISCOSITY * u + zon * h, VISCOSITY * v, zon * u], axis=0)
    lane_id = lax.broadcasted_iota(jnp.int32, (levels, HALF), 1)
    window = jnp.zeros((both, HALF), jnp.float32)
    for g in range(count):
        b, half = divmod(g, 2)
        beyond = (b + 1) % blocks if half else (b + blocks - 1) % blocks
        terms, lane = (from_east, HALF - 1) if half else (from_west, 0)
        pieces = []
        for part in range(lev_parts):
            source = beyond * lev_parts + part
            for f in range(3):
                here = tend[part, b, (2 * f + half) * levels : (2 * f + half + 1) * levels, :]
                term = terms[f * levels : (f + 1) * levels, source : source + 1]
                pieces.append(here + jnp.where(lane_id == lane, term, 0.0))
        value = jnp.concatenate(pieces, axis=0)
        halves[g] = value
        inside = lax.rem(g + reach, count) < 2 * reach
        window = window + jnp.where(inside, 1.0, 0.0).astype(jnp.float32) * value

    src = lax.broadcasted_iota(jnp.int32, (2 * HALF, 2 * HALF), 0)
    dst = lax.broadcasted_iota(jnp.int32, (2 * HALF, 2 * HALF), 1)
    sums = jnp.where((src & (HALF - 1)) <= dst, 1.0, 0.0).astype(jnp.bfloat16)
    fetch.wait()
    mixer = pair_mix_operand(matrix[...])
    scale = TIME_STEP / norm
    total = jnp.dot(
        jnp.concatenate(split2(window), axis=1), sums, preferred_element_type=jnp.float32
    )[:, HALF:]

    def split_group(g0):
        for g in range(g0, g0 + GROUP):
            ahead = halves[lax.rem(g + reach, count)]
            behind = halves[lax.rem(g + count - reach, count)]
            hi, lo = split2(ahead - behind)
            parts[g * both : (g + 1) * both, :HALF] = hi
            parts[g * both : (g + 1) * both, HALF:] = lo

    copies = []

    def finish_group(g0, total):
        box = jnp.dot(parts[g0 * both : (g0 + GROUP) * both, :], sums, preferred_element_type=jnp.float32)
        for pair in range(GROUP // 2):
            b = g0 // 2 + pair
            steps = []
            for half in range(2):
                g = 2 * b + half
                at = (g - g0) * both
                behind = halves[lax.rem(g + count - reach, count)]
                smooth = (box[at : at + both, :HALF] + total + edge_gain * behind) * scale
                total = total + box[at : at + both, HALF:]
                step = jnp.where(filtered, smooth, TIME_STEP * halves[g])
                for p in range(lev_parts):
                    stage[p, b, 2, half] = step[p * chans + 2 * levels : (p + 1) * chans]
                steps.append(step)
            step = jnp.concatenate(steps, axis=1)
            winds = []
            for f in range(2):
                winds += split2(
                    jnp.concatenate(
                        [step[p * chans + f * levels : p * chans + (f + 1) * levels] for p in range(lev_parts)],
                        axis=0,
                    )
                )
            mixed = jnp.dot(mixer, jnp.concatenate(winds, axis=0), preferred_element_type=jnp.float32)
            mixed = mixed[: 2 * lev_parts * levels] + mixed[2 * lev_parts * levels :]
            for f in range(2):
                for p in range(lev_parts):
                    at = (f * lev_parts + p) * levels
                    for half in range(2):
                        stage[p, b, f, half] = mixed[at : at + levels, half * HALF : (half + 1) * HALF]
            copies.append(pltpu.make_async_copy(stage.at[:, b], out.at[:, b], sems.at[b]))
            copies[-1].start()
        return total

    split_group(0)
    for g0 in range(0, count, GROUP):
        if g0 + GROUP < count:
            split_group(g0 + GROUP)
        total = finish_group(g0, total)
    for copy in copies:
        copy.wait()


def base_kernel(own_part, own, other, matrix, out):
    _, levels, rows, width = own.shape
    lower = own_part[0] == 0

    def by_row(ref, f, j0):
        flipped = [
            flip([ref[f, l0 + i, j0 : j0 + SUBLANES, :] for i in range(SUBLANES)])
            for l0 in range(0, levels, SUBLANES)
        ]
        return [jnp.concatenate([part[k] for part in flipped], axis=0) for k in range(SUBLANES)]

    for j0 in range(0, rows, SUBLANES):
        mine = [by_row(own, f, j0) for f in range(3)]
        theirs = [by_row(other, f, j0) for f in range(2)]
        for k in range(SUBLANES):
            j = j0 + k
            winds = []
            for f in range(2):
                a, b = mine[f][k], theirs[f][k]
                winds.append(jnp.concatenate([jnp.where(lower, a, b), jnp.where(lower, b, a)], axis=0))
            wind_hi, wind_lo = split2(jnp.concatenate(winds, axis=1))
            mixed = jnp.dot(
                mix_operand(matrix[j]),
                jnp.concatenate([wind_hi, wind_lo, wind_hi], axis=0),
                preferred_element_type=jnp.float32,
            )
            kept = jnp.where(lower, mixed[:levels], mixed[levels:])
            for f in range(2):
                out[j, f, 0] = kept[:, f * width : (f + 1) * width]
            out[j, 2, 0] = mine[2][k]


def finish_kernel(step, base, out, added, stage, in_sems, out_sems):
    fields, levels, rows, _ = out.shape
    blocks = levels // SUBLANES
    loads, copies = [], []
    for f in range(fields):
        for n in range(blocks):
            some = pl.ds(n * SUBLANES, SUBLANES)
            loads.append(
                pltpu.make_async_copy(base.at[:, f, :, some], added.at[:, f, :, some], in_sems.at[f * blocks + n])
            )
            loads[-1].start()
    for f in range(fields):
        for n in range(blocks):
            loads[f * blocks + n].wait()
            l0 = n * SUBLANES
            some = slice(l0, l0 + SUBLANES)
            for half in range(2):
                for j0 in range(0, rows, SUBLANES):
                    flipped = flip(
                        [step[j0 + k, f, half, some, :] + added[j0 + k, f, half, some, :] for k in range(SUBLANES)]
                    )
                    for i, value in enumerate(flipped):
                        stage[f, l0 + i, j0 : j0 + SUBLANES, half * HALF : (half + 1) * HALF] = value
            some = pl.ds(l0, SUBLANES)
            copies.append(
                pltpu.make_async_copy(stage.at[f, some], out.at[f, some], out_sems.at[f * blocks + n])
            )
            copies[-1].start()
    for copy in copies:
        copy.wait()


def per_device(prognostic, half_width, filter_mask, column_inverse):
    fields, levels, rows, width = prognostic.shape
    lon_devices, lat_devices, lev_devices = (lax.axis_size(a) for a in ("lon", "lat", "lev"))
    lon_index, lat_index, lev_index = (lax.axis_index(a) for a in ("lon", "lat", "lev"))
    chans = fields * levels
    halves = width // HALF
    params = pltpu.CompilerParams(vmem_limit_bytes=VMEM_LIMIT)
    hbm = pl.BlockSpec(memory_space=pltpu.HBM)
    vmem = pl.BlockSpec(memory_space=pltpu.VMEM)

    def in_hbm(x):
        return pltpu.with_memory_space_constraint(x, pltpu.HBM)

    def in_vmem(x):
        return pltpu.with_memory_space_constraint(x, pltpu.VMEM)


    with jax.named_scope("fetch"):
        tile, last, first = pl.pallas_call(
            fetch_kernel,
            out_shape=(
                pltpu.VMEM(prognostic.shape, jnp.float32),
                pltpu.VMEM((chans, width), jnp.float32),
                pltpu.VMEM((chans, width), jnp.float32),
            ),
            in_specs=[hbm],
            out_specs=(vmem, vmem, vmem),
            scratch_shapes=[pltpu.SemaphoreType.DMA((fields, LOADS))],
            compiler_params=params,
        )(in_hbm(prognostic))
    south = lax.ppermute(last, "lat", [(i, i + 1) for i in range(lat_devices - 1)])
    north = lax.ppermute(first, "lat", [(i + 1, i) for i in range(lat_devices - 1)])
    other = lax.ppermute(prognostic[:2], "lev", [(0, 1), (1, 0)])

    global_rows = (lat_index * rows + jnp.arange(rows)).astype(jnp.float32)
    cosine, sine = latitudes(global_rows, rows * lat_devices)
    zonal = 0.25 / (cosine + 0.05)
    zonal_field = jnp.broadcast_to(zonal[:, None], (rows, width))
    coriolis_field = jnp.broadcast_to((0.5 * sine)[:, None], (rows, width))

    sent_rows = halves * chans + SUBLANES
    with jax.named_scope("tendencies"):
        tend, ends = pl.pallas_call(
            tendency_kernel,
            out_shape=(
                pltpu.HBM((rows, sent_rows, HALF), jnp.float32),
                pltpu.VMEM((2, halves * chans, HALF), jnp.float32),
            ),
            in_specs=[vmem, vmem, vmem],
            out_specs=(hbm, vmem),
            scratch_shapes=[
                pltpu.VMEM(prognostic.shape, jnp.float32),
                pltpu.VMEM((rows, HALF), jnp.float32),
                pltpu.VMEM((rows, sent_rows, HALF), jnp.float32),
                pltpu.SemaphoreType.DMA((rows // SUBLANES,)),
            ],
            compiler_params=params,
        )(in_vmem(tile), zonal_field, coriolis_field)

    with jax.named_scope("seam_rows"):
        tend = pl.pallas_call(
            seam_kernel,
            out_shape=pltpu.HBM(tend.shape, jnp.float32),
            in_specs=[vmem, vmem, vmem, hbm],
            out_specs=hbm,
            input_output_aliases={3: 0},
            scratch_shapes=[pltpu.VMEM(ends.shape, jnp.float32), pltpu.SemaphoreType.DMA((2,))],
            compiler_params=params,
        )(in_vmem(ends), in_vmem(south), in_vmem(north), in_hbm(tend))

    whole_rows = lax.all_to_all(tend, ("lev", "lon"), 0, 0, tiled=True)

    own_row = (lev_index * lon_devices + lon_index).astype(jnp.int32).reshape(1)
    stepped_shape = (lev_devices, lon_devices, fields, halves, levels, HALF)
    count = halves * lon_devices
    both = lev_devices * chans
    with jax.named_scope("row_filter"):
        stepped = pl.pallas_call(
            filter_kernel,
            out_shape=pltpu.HBM(stepped_shape, jnp.float32),
            grid_spec=pltpu.PrefetchScalarGridSpec(
                num_scalar_prefetch=4,
                grid=(1,),
                in_specs=[vmem, hbm],
                out_specs=hbm,
                scratch_shapes=[
                    pltpu.VMEM((count, both, HALF), jnp.float32),
                    pltpu.VMEM((count * both, 2 * HALF), jnp.bfloat16),
                    pltpu.VMEM((HALF, HALF), jnp.float32),
                    pltpu.VMEM(column_inverse.shape[1:], jnp.float32),
                    pltpu.VMEM(stepped_shape, jnp.float32),
                    pltpu.SemaphoreType.DMA,
                    pltpu.SemaphoreType.DMA((lon_devices,)),
                ],
            ),
            compiler_params=params,
        )(
            own_row,
            half_width,
            filter_mask,
            zonal,
            in_vmem(whole_rows.reshape(lev_devices, lon_devices, sent_rows, HALF)),
            in_hbm(column_inverse),
        )

    returned = lax.all_to_all(
        stepped.reshape((rows,) + stepped_shape[2:]), ("lev", "lon"), 0, 0, tiled=True
    )

    with jax.named_scope("base"):
        base = pl.pallas_call(
            base_kernel,
            out_shape=pltpu.HBM(returned.shape, jnp.float32),
            grid_spec=pltpu.PrefetchScalarGridSpec(
                num_scalar_prefetch=1,
                grid=(halves,),
                in_specs=[
                    pl.BlockSpec((fields, levels, rows, HALF), lambda i, *_: (0, 0, 0, i)),
                    pl.BlockSpec((2, levels, rows, HALF), lambda i, *_: (0, 0, 0, i)),
                    pl.BlockSpec(column_inverse.shape, lambda i, *_: (0, 0, 0)),
                ],
                out_specs=pl.BlockSpec((rows, fields, 1, levels, HALF), lambda i, *_: (0, 0, i, 0, 0)),
            ),
            compiler_params=params,
        )(lev_index.astype(jnp.int32).reshape(1), prognostic, other, column_inverse)

    with jax.named_scope("finish"):
        return pl.pallas_call(
            finish_kernel,
            out_shape=jax.ShapeDtypeStruct(prognostic.shape, jnp.float32),
            in_specs=[vmem, hbm],
            out_specs=hbm,
            scratch_shapes=[
                pltpu.VMEM(returned.shape, jnp.float32),
                pltpu.VMEM(prognostic.shape, jnp.float32),
                pltpu.SemaphoreType.DMA((fields * levels // SUBLANES,)),
                pltpu.SemaphoreType.DMA((fields * levels // SUBLANES,)),
            ],
            compiler_params=params,
        )(in_vmem(returned), in_hbm(base))


def solution(mesh):
    placed = (P(None, "lev", "lat", "lon"), P("lat"), P("lat"), P("lat", None, None))
    return jax.shard_map(
        per_device,
        mesh=mesh,
        in_specs=placed,
        out_specs=P(None, "lev", "lat", "lon"),
        check_vma=False,
    )
```

```python
import jax
import jax.numpy as jnp
from jax import lax
from jax.experimental import pallas as pl
from jax.experimental.pallas import tpu as pltpu
from jax.sharding import PartitionSpec as P

TIME_STEP = 0.5
VISCOSITY = 0.05
MERIDIONAL = 0.25
HALF = 128
SUBLANES = 8
VMEM_LIMIT = 32 * 1024 * 1024
GROUP = 4
LOADS = 4


def latitudes(global_rows, row_total):
    latitude_angle = -0.5 * jnp.pi + (global_rows + 0.5) * jnp.pi / row_total
    return (jnp.cos(latitude_angle), jnp.sin(latitude_angle))


def flip(tiles):
    row = lax.broadcasted_iota(jnp.int32, tiles[0].shape, 0)
    for d in (4, 2, 1):
        keep = (row & d) == 0
        turned = list(tiles)
        for i in range(SUBLANES):
            if not i & d:
                a, b = tiles[i], tiles[i + d]
                turned[i] = jnp.where(keep, a, pltpu.roll(b, d, 0))
                turned[i + d] = jnp.where(keep, pltpu.roll(a, SUBLANES - d, 0), b)
        tiles = turned
    return tiles


def outer_rows_kernel(prog, first, last, tiles, sems):
    fields, levels, rows, _ = prog.shape
    loads = []
    for f in range(fields):
        for n, start in enumerate((rows - SUBLANES, 0)):
            some = pl.ds(start, SUBLANES)
            loads.append(pltpu.make_async_copy(prog.at[f, :, some], tiles.at[n, f], sems.at[f, n]))
            loads[-1].start()
    for f in range(fields):
        for n, (row, out) in enumerate(((SUBLANES - 1, last), (0, first))):
            loads[2 * f + n].wait()
            for l in range(levels):
                out[f * levels + l : f * levels + l + 1, :] = tiles[n, f, l, row : row + 1, :]


def tendency_kernel(prog, zonal, coriolis, out, ends, tile, turn, stage, in_sems, out_sems):
    _, levels, rows, width = prog.shape
    chans = 3 * levels
    payload = 2 * chans
    per_load = levels // LOADS
    loads, copies = [], []
    for load in range(LOADS):
        some = pl.ds(load * per_load, per_load)
        loads.append(pltpu.make_async_copy(prog.at[:, some], tile.at[:, some], in_sems.at[load]))
        loads[-1].start()

    def send(first, sem):
        some = pl.ds(first, SUBLANES)
        copies.append(pltpu.make_async_copy(stage.at[:, some], out.at[:, some], out_sems.at[sem]))
        copies[-1].start()

    row_id = lax.broadcasted_iota(jnp.int32, (rows, width), 0)
    col_id = lax.broadcasted_iota(jnp.int32, (rows, width), 1)
    lane_id = lax.broadcasted_iota(jnp.int32, (rows, HALF), 1)
    first_row, last_row = row_id == 0, row_id == rows - 1
    first_col, last_col = col_id == 0, col_id == width - 1
    zon, cor = zonal[...], coriolis[...]
    edge_rows = jnp.zeros((rows, HALF), jnp.float32)
    for l in range(levels):
        if l % per_load == 0:
            loads[l // per_load].wait()
        centre, dx, dy, sx = [], [], [], []
        for f in range(3):
            c = f * levels + l
            here = tile[f, l]
            e = jnp.where(last_col, 0.0, pltpu.roll(here, width - 1, 1))
            w = jnp.where(first_col, 0.0, pltpu.roll(here, 1, 1))
            n = jnp.where(last_row, 0.0, pltpu.roll(here, rows - 1, 0))
            s = jnp.where(first_row, 0.0, pltpu.roll(here, 1, 0))
            centre.append(here)
            dx.append(e - w)
            dy.append(n - s)
            sx.append(e + w + n + s - 4.0 * here)
            first = here[:, :HALF]
            last = here[:, width - HALF :]
            if c:
                first = pltpu.roll(first, c, 1)
            last = pltpu.roll(last, (chans + c + 1) % HALF, 1)
            edge_rows = jnp.where(lane_id == c, first, jnp.where(lane_id == chans + c, last, edge_rows))
        tends = (
            -zon * dx[2] + cor * centre[1] + VISCOSITY * sx[0],
            -MERIDIONAL * dy[2] - cor * centre[0] + VISCOSITY * sx[1],
            -zon * dx[0] - MERIDIONAL * dy[1],
        )
        for f in range(3):
            turn[f, l] = tends[f]
        if (l + 1) % SUBLANES:
            continue
        l0 = l + 1 - SUBLANES
        for f in range(3):
            for half in range(2):
                at = (2 * f + half) * levels + l0
                for j0 in range(0, rows, SUBLANES):
                    flipped = flip(
                        [
                            turn[f, l0 + i, j0 : j0 + SUBLANES, half * HALF : (half + 1) * HALF]
                            for i in range(SUBLANES)
                        ]
                    )
                    for k, value in enumerate(flipped):
                        j = j0 + k
                        stage[j, at : at + SUBLANES, :] = value
                        if j in (0, rows - 1):
                            ends[min(j, 1), at : at + SUBLANES, :] = value
                send(at, at // SUBLANES)
    for j in range(rows):
        stage[j, payload:, :] = jnp.broadcast_to(edge_rows[j : j + 1, :], (SUBLANES, HALF))
    send(payload, payload // SUBLANES)
    for copy in copies:
        copy.wait()


def seam_kernel(ends, north, south, tend, out, stage, sems):
    del tend
    chans = south.shape[0]
    levels = chans // 3
    copies = []
    for at, beyond, sign in ((0, south, -1.0), (1, north, 1.0)):
        for half in range(2):
            lanes = slice(half * HALF, (half + 1) * HALF)
            u, v, h = (beyond[f * levels : (f + 1) * levels, lanes] for f in range(3))
            slope = sign * MERIDIONAL
            for f, term in enumerate((VISCOSITY * u, VISCOSITY * v - slope * h, -slope * v)):
                some = slice((2 * f + half) * levels, (2 * f + half + 1) * levels)
                stage[at, some, :] = ends[at, some, :] + term
        row = at * (out.shape[0] - 1)
        copies.append(pltpu.make_async_copy(stage.at[at], out.at[row, pl.ds(0, 2 * chans)], sems.at[at]))
        copies[-1].start()
    for copy in copies:
        copy.wait()


def split2(x):
    hi = x.astype(jnp.bfloat16)
    return hi, (x - hi.astype(jnp.float32)).astype(jnp.bfloat16)


def mix_operand(matrix):
    hi, lo = split2(matrix)
    return jnp.concatenate([hi, hi, lo], axis=1)


def pair_mix_operand(matrix):
    hi, lo = split2(matrix)
    none = jnp.zeros_like(hi)
    return jnp.concatenate(
        [
            jnp.concatenate([hi, hi, none, none], axis=1),
            jnp.concatenate([none, none, hi, hi], axis=1),
            jnp.concatenate([lo, none, none, none], axis=1),
            jnp.concatenate([none, none, lo, none], axis=1),
        ],
        axis=0,
    )


def filter_kernel(
    own_row, half_width, filter_mask, zonal, tend, matrices, out, halves, parts, seam, matrix, stage, matrix_sem, sems
):
    lev_parts, blocks, levels = out.shape[0], out.shape[1], out.shape[4]
    chans = 3 * levels
    payload = 2 * chans
    count = 2 * blocks
    both = lev_parts * chans
    row = own_row[0]
    fetch = pltpu.make_async_copy(matrices.at[row], matrix, matrix_sem)
    fetch.start()
    reach = half_width[row]
    whole = reach == count // 2
    norm = jnp.where(whole, count * HALF, 2 * HALF * reach + 1).astype(jnp.float32)
    filtered = filter_mask[row] == 1
    edge_gain = jnp.where(whole, 0.0, 1.0).astype(jnp.float32)

    for b in range(blocks):
        for part in range(lev_parts):
            at = b * lev_parts + part
            seam[at : at + 1, :] = tend[part, b, payload : payload + 1, :]
    columns = seam[...].T
    zon = zonal[row]
    u, v, h = (columns[f * levels : (f + 1) * levels] for f in range(3))
    from_east = jnp.concatenate([VISCOSITY * u - zon * h, VISCOSITY * v, -zon * u], axis=0)
    u, v, h = (columns[chans + f * levels : chans + (f + 1) * levels] for f in range(3))
    from_west = jnp.concatenate([VISCOSITY * u + zon * h, VISCOSITY * v, zon * u], axis=0)
    lane_id = lax.broadcasted_iota(jnp.int32, (levels, HALF), 1)
    window = jnp.zeros((both, HALF), jnp.float32)
    for g in range(count):
        b, half = divmod(g, 2)
        beyond = (b + 1) % blocks if half else (b + blocks - 1) % blocks
        terms, lane = (from_east, HALF - 1) if half else (from_west, 0)
        pieces = []
        for part in range(lev_parts):
            source = beyond * lev_parts + part
            for f in range(3):
                here = tend[part, b, (2 * f + half) * levels : (2 * f + half + 1) * levels, :]
                term = terms[f * levels : (f + 1) * levels, source : source + 1]
                pieces.append(here + jnp.where(lane_id == lane, term, 0.0))
        value = jnp.concatenate(pieces, axis=0)
        halves[g] = value
        inside = lax.rem(g + reach, count) < 2 * reach
        window = window + jnp.where(inside, 1.0, 0.0).astype(jnp.float32) * value

    src = lax.broadcasted_iota(jnp.int32, (2 * HALF, 2 * HALF), 0)
    dst = lax.broadcasted_iota(jnp.int32, (2 * HALF, 2 * HALF), 1)
    sums = jnp.where((src & (HALF - 1)) <= dst, 1.0, 0.0).astype(jnp.bfloat16)
    fetch.wait()
    mixer = pair_mix_operand(matrix[...])
    scale = TIME_STEP / norm
    total = jnp.dot(
        jnp.concatenate(split2(window), axis=1), sums, preferred_element_type=jnp.float32
    )[:, HALF:]

    def split_group(g0):
        for g in range(g0, g0 + GROUP):
            ahead = halves[lax.rem(g + reach, count)]
            behind = halves[lax.rem(g + count - reach, count)]
            hi, lo = split2(ahead - behind)
            parts[g * both : (g + 1) * both, :HALF] = hi
            parts[g * both : (g + 1) * both, HALF:] = lo

    copies = []

    def finish_group(g0, total):
        box = jnp.dot(parts[g0 * both : (g0 + GROUP) * both, :], sums, preferred_element_type=jnp.float32)
        for pair in range(GROUP // 2):
            b = g0 // 2 + pair
            steps = []
            for half in range(2):
                g = 2 * b + half
                at = (g - g0) * both
                behind = halves[lax.rem(g + count - reach, count)]
                smooth = (box[at : at + both, :HALF] + total + edge_gain * behind) * scale
                total = total + box[at : at + both, HALF:]
                step = jnp.where(filtered, smooth, TIME_STEP * halves[g])
                for p in range(lev_parts):
                    stage[p, b, 2, half] = step[p * chans + 2 * levels : (p + 1) * chans]
                steps.append(step)
            step = jnp.concatenate(steps, axis=1)
            winds = []
            for f in range(2):
                winds += split2(
                    jnp.concatenate(
                        [step[p * chans + f * levels : p * chans + (f + 1) * levels] for p in range(lev_parts)],
                        axis=0,
                    )
                )
            mixed = jnp.dot(mixer, jnp.concatenate(winds, axis=0), preferred_element_type=jnp.float32)
            mixed = mixed[: 2 * lev_parts * levels] + mixed[2 * lev_parts * levels :]
            for f in range(2):
                for p in range(lev_parts):
                    at = (f * lev_parts + p) * levels
                    for half in range(2):
                        stage[p, b, f, half] = mixed[at : at + levels, half * HALF : (half + 1) * HALF]
            copies.append(pltpu.make_async_copy(stage.at[:, b], out.at[:, b], sems.at[b]))
            copies[-1].start()
        return total

    split_group(0)
    for g0 in range(0, count, GROUP):
        if g0 + GROUP < count:
            split_group(g0 + GROUP)
        total = finish_group(g0, total)
    for copy in copies:
        copy.wait()


def base_kernel(own_part, own, other, matrix, out):
    _, levels, rows, width = own.shape
    lower = own_part[0] == 0

    def by_row(ref, f, j0):
        flipped = [
            flip([ref[f, l0 + i, j0 : j0 + SUBLANES, :] for i in range(SUBLANES)])
            for l0 in range(0, levels, SUBLANES)
        ]
        return [jnp.concatenate([part[k] for part in flipped], axis=0) for k in range(SUBLANES)]

    for j0 in range(0, rows, SUBLANES):
        mine = [by_row(own, f, j0) for f in range(3)]
        theirs = [by_row(other, f, j0) for f in range(2)]
        for k in range(SUBLANES):
            j = j0 + k
            winds = []
            for f in range(2):
                a, b = mine[f][k], theirs[f][k]
                winds.append(jnp.concatenate([jnp.where(lower, a, b), jnp.where(lower, b, a)], axis=0))
            wind_hi, wind_lo = split2(jnp.concatenate(winds, axis=1))
            mixed = jnp.dot(
                mix_operand(matrix[j]),
                jnp.concatenate([wind_hi, wind_lo, wind_hi], axis=0),
                preferred_element_type=jnp.float32,
            )
            kept = jnp.where(lower, mixed[:levels], mixed[levels:])
            for f in range(2):
                out[j, f, 0] = kept[:, f * width : (f + 1) * width]
            out[j, 2, 0] = mine[2][k]


def finish_kernel(step, base, out, added, stage, in_sems, out_sems):
    fields, levels, rows, _ = out.shape
    blocks = levels // SUBLANES
    loads, copies = [], []
    for f in range(fields):
        for n in range(blocks):
            some = pl.ds(n * SUBLANES, SUBLANES)
            loads.append(
                pltpu.make_async_copy(base.at[:, f, :, some], added.at[:, f, :, some], in_sems.at[f * blocks + n])
            )
            loads[-1].start()
    for f in range(fields):
        for n in range(blocks):
            loads[f * blocks + n].wait()
            l0 = n * SUBLANES
            some = slice(l0, l0 + SUBLANES)
            for half in range(2):
                for j0 in range(0, rows, SUBLANES):
                    flipped = flip(
                        [step[j0 + k, f, half, some, :] + added[j0 + k, f, half, some, :] for k in range(SUBLANES)]
                    )
                    for i, value in enumerate(flipped):
                        stage[f, l0 + i, j0 : j0 + SUBLANES, half * HALF : (half + 1) * HALF] = value
            some = pl.ds(l0, SUBLANES)
            copies.append(
                pltpu.make_async_copy(stage.at[f, some], out.at[f, some], out_sems.at[f * blocks + n])
            )
            copies[-1].start()
    for copy in copies:
        copy.wait()


def per_device(prognostic, half_width, filter_mask, column_inverse):
    fields, levels, rows, width = prognostic.shape
    lon_devices, lat_devices, lev_devices = (lax.axis_size(a) for a in ("lon", "lat", "lev"))
    lon_index, lat_index, lev_index = (lax.axis_index(a) for a in ("lon", "lat", "lev"))
    chans = fields * levels
    halves = width // HALF
    params = pltpu.CompilerParams(vmem_limit_bytes=VMEM_LIMIT)
    hbm = pl.BlockSpec(memory_space=pltpu.HBM)
    vmem = pl.BlockSpec(memory_space=pltpu.VMEM)

    def in_hbm(x):
        return pltpu.with_memory_space_constraint(x, pltpu.HBM)

    def in_vmem(x):
        return pltpu.with_memory_space_constraint(x, pltpu.VMEM)


    with jax.named_scope("outer_rows"):
        first, last = pl.pallas_call(
            outer_rows_kernel,
            out_shape=(pltpu.VMEM((chans, width), jnp.float32),) * 2,
            in_specs=[hbm],
            out_specs=(vmem, vmem),
            scratch_shapes=[
                pltpu.VMEM((2, fields, levels, SUBLANES, width), jnp.float32),
                pltpu.SemaphoreType.DMA((fields, 2)),
            ],
            compiler_params=params,
        )(in_hbm(prognostic))
    north = lax.ppermute(first, "lat", [(i + 1, i) for i in range(lat_devices - 1)])
    south = lax.ppermute(last, "lat", [(i, i + 1) for i in range(lat_devices - 1)])
    other = lax.ppermute(prognostic[:2], "lev", [(0, 1), (1, 0)])

    global_rows = (lat_index * rows + jnp.arange(rows)).astype(jnp.float32)
    cosine, sine = latitudes(global_rows, rows * lat_devices)
    zonal = 0.25 / (cosine + 0.05)
    zonal_field = jnp.broadcast_to(zonal[:, None], (rows, width))
    coriolis_field = jnp.broadcast_to((0.5 * sine)[:, None], (rows, width))

    sent_rows = halves * chans + SUBLANES
    with jax.named_scope("tendencies"):
        tend, ends = pl.pallas_call(
            tendency_kernel,
            out_shape=(
                pltpu.HBM((rows, sent_rows, HALF), jnp.float32),
                pltpu.VMEM((2, halves * chans, HALF), jnp.float32),
            ),
            in_specs=[hbm, vmem, vmem],
            out_specs=(hbm, vmem),
            scratch_shapes=[
                pltpu.VMEM(prognostic.shape, jnp.float32),
                pltpu.VMEM(prognostic.shape, jnp.float32),
                pltpu.VMEM((rows, sent_rows, HALF), jnp.float32),
                pltpu.SemaphoreType.DMA((LOADS,)),
                pltpu.SemaphoreType.DMA((sent_rows // SUBLANES,)),
            ],
            compiler_params=params,
        )(in_hbm(prognostic), in_vmem(zonal_field), in_vmem(coriolis_field))

    with jax.named_scope("seam_rows"):
        tend = pl.pallas_call(
            seam_kernel,
            out_shape=pltpu.HBM(tend.shape, jnp.float32),
            in_specs=[vmem, vmem, vmem, hbm],
            out_specs=hbm,
            input_output_aliases={3: 0},
            scratch_shapes=[pltpu.VMEM(ends.shape, jnp.float32), pltpu.SemaphoreType.DMA((2,))],
            compiler_params=params,
        )(in_vmem(ends), in_vmem(north), in_vmem(south), in_hbm(tend))

    whole_rows = lax.all_to_all(tend, ("lev", "lon"), 0, 0, tiled=True)

    own_row = (lev_index * lon_devices + lon_index).astype(jnp.int32).reshape(1)
    stepped_shape = (lev_devices, lon_devices, fields, halves, levels, HALF)
    count = halves * lon_devices
    both = lev_devices * chans
    with jax.named_scope("row_filter"):
        stepped = pl.pallas_call(
            filter_kernel,
            out_shape=pltpu.HBM(stepped_shape, jnp.float32),
            grid_spec=pltpu.PrefetchScalarGridSpec(
                num_scalar_prefetch=4,
                grid=(1,),
                in_specs=[vmem, hbm],
                out_specs=hbm,
                scratch_shapes=[
                    pltpu.VMEM((count, both, HALF), jnp.float32),
                    pltpu.VMEM((count * both, 2 * HALF), jnp.bfloat16),
                    pltpu.VMEM((HALF, HALF), jnp.float32),
                    pltpu.VMEM(column_inverse.shape[1:], jnp.float32),
                    pltpu.VMEM(stepped_shape, jnp.float32),
                    pltpu.SemaphoreType.DMA,
                    pltpu.SemaphoreType.DMA((lon_devices,)),
                ],
            ),
            compiler_params=params,
        )(
            own_row,
            half_width,
            filter_mask,
            zonal,
            in_vmem(whole_rows.reshape(lev_devices, lon_devices, sent_rows, HALF)),
            in_hbm(column_inverse),
        )

    returned = lax.all_to_all(
        stepped.reshape((rows,) + stepped_shape[2:]), ("lev", "lon"), 0, 0, tiled=True
    )

    with jax.named_scope("base"):
        base = pl.pallas_call(
            base_kernel,
            out_shape=pltpu.HBM(returned.shape, jnp.float32),
            grid_spec=pltpu.PrefetchScalarGridSpec(
                num_scalar_prefetch=1,
                grid=(halves,),
                in_specs=[
                    pl.BlockSpec((fields, levels, rows, HALF), lambda i, *_: (0, 0, 0, i)),
                    pl.BlockSpec((2, levels, rows, HALF), lambda i, *_: (0, 0, 0, i)),
                    pl.BlockSpec(column_inverse.shape, lambda i, *_: (0, 0, 0)),
                ],
                out_specs=pl.BlockSpec((rows, fields, 1, levels, HALF), lambda i, *_: (0, 0, i, 0, 0)),
            ),
            compiler_params=params,
        )(lev_index.astype(jnp.int32).reshape(1), prognostic, other, column_inverse)

    with jax.named_scope("finish"):
        return pl.pallas_call(
            finish_kernel,
            out_shape=jax.ShapeDtypeStruct(prognostic.shape, jnp.float32),
            in_specs=[vmem, hbm],
            out_specs=hbm,
            scratch_shapes=[
                pltpu.VMEM(returned.shape, jnp.float32),
                pltpu.VMEM(prognostic.shape, jnp.float32),
                pltpu.SemaphoreType.DMA((fields * levels // SUBLANES,)),
                pltpu.SemaphoreType.DMA((fields * levels // SUBLANES,)),
            ],
            compiler_params=params,
        )(in_vmem(returned), in_hbm(base))


def solution(mesh):
    placed = (P(None, "lev", "lat", "lon"), P("lat"), P("lat"), P("lat", None, None))
    return jax.shard_map(
        per_device,
        mesh=mesh,
        in_specs=placed,
        out_specs=P(None, "lev", "lat", "lon"),
        check_vma=False,
    )
```

```python
import jax
import jax.numpy as jnp
from jax import lax
from jax.experimental import pallas as pl
from jax.experimental.pallas import tpu as pltpu
from jax.sharding import PartitionSpec as P

TIME_STEP = 0.5
VISCOSITY = 0.05
MERIDIONAL = 0.25
HALF = 128
SUBLANES = 8
VMEM_LIMIT = 32 * 1024 * 1024
GROUP = 4
LOADS = 8


def latitudes(global_rows, row_total):
    latitude_angle = -0.5 * jnp.pi + (global_rows + 0.5) * jnp.pi / row_total
    return (jnp.cos(latitude_angle), jnp.sin(latitude_angle))


def flip(tiles):
    row = lax.broadcasted_iota(jnp.int32, tiles[0].shape, 0)
    for d in (4, 2, 1):
        keep = (row & d) == 0
        turned = list(tiles)
        for i in range(SUBLANES):
            if not i & d:
                a, b = tiles[i], tiles[i + d]
                turned[i] = jnp.where(keep, a, pltpu.roll(b, d, 0))
                turned[i + d] = jnp.where(keep, pltpu.roll(a, SUBLANES - d, 0), b)
        tiles = turned
    return tiles


def outer_rows_kernel(prog, first, last, sems):
    fields, levels, rows, _ = prog.shape
    copies = []
    for f in range(fields):
        for n, (row, out) in enumerate(((0, first), (rows - 1, last))):
            copies.append(
                pltpu.make_async_copy(prog.at[f, :, row], out.at[pl.ds(f * levels, levels)], sems.at[f, n])
            )
            copies[-1].start()
    for copy in copies:
        copy.wait()


def tendency_kernel(prog, zonal, coriolis, out, ends, tile, turn, stage, in_sems, out_sems):
    _, levels, rows, width = prog.shape
    chans = 3 * levels
    payload = 2 * chans
    per_load = levels // LOADS
    loads, copies = [], []
    for load in range(LOADS):
        some = pl.ds(load * per_load, per_load)
        loads.append(pltpu.make_async_copy(prog.at[:, some], tile.at[:, some], in_sems.at[load]))
        loads[-1].start()

    def send(first, sem):
        some = pl.ds(first, SUBLANES)
        copies.append(pltpu.make_async_copy(stage.at[:, some], out.at[:, some], out_sems.at[sem]))
        copies[-1].start()

    row_id = lax.broadcasted_iota(jnp.int32, (rows, width), 0)
    col_id = lax.broadcasted_iota(jnp.int32, (rows, width), 1)
    lane_id = lax.broadcasted_iota(jnp.int32, (rows, HALF), 1)
    first_row, last_row = row_id == 0, row_id == rows - 1
    first_col, last_col = col_id == 0, col_id == width - 1
    zon, cor = zonal[...], coriolis[...]
    edge_rows = jnp.zeros((rows, HALF), jnp.float32)
    for l in range(levels):
        if l % per_load == 0:
            loads[l // per_load].wait()
        centre, dx, dy, sx = [], [], [], []
        for f in range(3):
            c = f * levels + l
            here = tile[f, l]
            e = jnp.where(last_col, 0.0, pltpu.roll(here, width - 1, 1))
            w = jnp.where(first_col, 0.0, pltpu.roll(here, 1, 1))
            n = jnp.where(last_row, 0.0, pltpu.roll(here, rows - 1, 0))
            s = jnp.where(first_row, 0.0, pltpu.roll(here, 1, 0))
            centre.append(here)
            dx.append(e - w)
            dy.append(n - s)
            sx.append(e + w + n + s - 4.0 * here)
            first = here[:, :HALF]
            last = here[:, width - HALF :]
            if c:
                first = pltpu.roll(first, c, 1)
            last = pltpu.roll(last, (chans + c + 1) % HALF, 1)
            edge_rows = jnp.where(lane_id == c, first, jnp.where(lane_id == chans + c, last, edge_rows))
        tends = (
            -zon * dx[2] + cor * centre[1] + VISCOSITY * sx[0],
            -MERIDIONAL * dy[2] - cor * centre[0] + VISCOSITY * sx[1],
            -zon * dx[0] - MERIDIONAL * dy[1],
        )
        for f in range(3):
            turn[f, l] = tends[f]
        if (l + 1) % SUBLANES:
            continue
        l0 = l + 1 - SUBLANES
        for f in range(3):
            for half in range(2):
                at = (2 * f + half) * levels + l0
                for j0 in range(0, rows, SUBLANES):
                    flipped = flip(
                        [
                            turn[f, l0 + i, j0 : j0 + SUBLANES, half * HALF : (half + 1) * HALF]
                            for i in range(SUBLANES)
                        ]
                    )
                    for k, value in enumerate(flipped):
                        j = j0 + k
                        stage[j, at : at + SUBLANES, :] = value
                        if j in (0, rows - 1):
                            ends[min(j, 1), at : at + SUBLANES, :] = value
                send(at, at // SUBLANES)
    for j in range(rows):
        stage[j, payload:, :] = jnp.broadcast_to(edge_rows[j : j + 1, :], (SUBLANES, HALF))
    send(payload, payload // SUBLANES)
    for copy in copies:
        copy.wait()


def seam_kernel(ends, north, south, tend, out, stage, sems):
    del tend
    chans = south.shape[0]
    levels = chans // 3
    copies = []
    for at, beyond, sign in ((0, south, -1.0), (1, north, 1.0)):
        for half in range(2):
            lanes = slice(half * HALF, (half + 1) * HALF)
            u, v, h = (beyond[f * levels : (f + 1) * levels, lanes] for f in range(3))
            slope = sign * MERIDIONAL
            for f, term in enumerate((VISCOSITY * u, VISCOSITY * v - slope * h, -slope * v)):
                some = slice((2 * f + half) * levels, (2 * f + half + 1) * levels)
                stage[at, some, :] = ends[at, some, :] + term
        row = at * (out.shape[0] - 1)
        copies.append(pltpu.make_async_copy(stage.at[at], out.at[row, pl.ds(0, 2 * chans)], sems.at[at]))
        copies[-1].start()
    for copy in copies:
        copy.wait()


def split2(x):
    hi = x.astype(jnp.bfloat16)
    return hi, (x - hi.astype(jnp.float32)).astype(jnp.bfloat16)


def mix_operand(matrix):
    hi, lo = split2(matrix)
    return jnp.concatenate([hi, hi, lo], axis=1)


def pair_mix_operand(matrix):
    hi, lo = split2(matrix)
    none = jnp.zeros_like(hi)
    return jnp.concatenate(
        [
            jnp.concatenate([hi, hi, none, none], axis=1),
            jnp.concatenate([none, none, hi, hi], axis=1),
            jnp.concatenate([lo, none, none, none], axis=1),
            jnp.concatenate([none, none, lo, none], axis=1),
        ],
        axis=0,
    )


def filter_kernel(
    own_row, half_width, filter_mask, zonal, tend, matrices, out, halves, parts, seam, matrix, stage, matrix_sem, sems
):
    lev_parts, blocks, levels = out.shape[0], out.shape[1], out.shape[4]
    chans = 3 * levels
    payload = 2 * chans
    count = 2 * blocks
    both = lev_parts * chans
    row = own_row[0]
    fetch = pltpu.make_async_copy(matrices.at[row], matrix, matrix_sem)
    fetch.start()
    reach = half_width[row]
    whole = reach == count // 2
    norm = jnp.where(whole, count * HALF, 2 * HALF * reach + 1).astype(jnp.float32)
    filtered = filter_mask[row] == 1
    edge_gain = jnp.where(whole, 0.0, 1.0).astype(jnp.float32)

    for b in range(blocks):
        for part in range(lev_parts):
            at = b * lev_parts + part
            seam[at : at + 1, :] = tend[part, b, payload : payload + 1, :]
    columns = seam[...].T
    zon = zonal[row]
    u, v, h = (columns[f * levels : (f + 1) * levels] for f in range(3))
    from_east = jnp.concatenate([VISCOSITY * u - zon * h, VISCOSITY * v, -zon * u], axis=0)
    u, v, h = (columns[chans + f * levels : chans + (f + 1) * levels] for f in range(3))
    from_west = jnp.concatenate([VISCOSITY * u + zon * h, VISCOSITY * v, zon * u], axis=0)
    lane_id = lax.broadcasted_iota(jnp.int32, (levels, HALF), 1)
    window = jnp.zeros((both, HALF), jnp.float32)
    for g in range(count):
        b, half = divmod(g, 2)
        beyond = (b + 1) % blocks if half else (b + blocks - 1) % blocks
        terms, lane = (from_east, HALF - 1) if half else (from_west, 0)
        pieces = []
        for part in range(lev_parts):
            source = beyond * lev_parts + part
            for f in range(3):
                here = tend[part, b, (2 * f + half) * levels : (2 * f + half + 1) * levels, :]
                term = terms[f * levels : (f + 1) * levels, source : source + 1]
                pieces.append(here + jnp.where(lane_id == lane, term, 0.0))
        value = jnp.concatenate(pieces, axis=0)
        halves[g] = value
        inside = lax.rem(g + reach, count) < 2 * reach
        window = window + jnp.where(inside, 1.0, 0.0).astype(jnp.float32) * value

    src = lax.broadcasted_iota(jnp.int32, (2 * HALF, 2 * HALF), 0)
    dst = lax.broadcasted_iota(jnp.int32, (2 * HALF, 2 * HALF), 1)
    sums = jnp.where((src & (HALF - 1)) <= dst, 1.0, 0.0).astype(jnp.bfloat16)
    fetch.wait()
    mixer = pair_mix_operand(matrix[...])
    scale = TIME_STEP / norm
    total = jnp.dot(
        jnp.concatenate(split2(window), axis=1), sums, preferred_element_type=jnp.float32
    )[:, HALF:]

    def split_group(g0):
        for g in range(g0, g0 + GROUP):
            ahead = halves[lax.rem(g + reach, count)]
            behind = halves[lax.rem(g + count - reach, count)]
            hi, lo = split2(ahead - behind)
            parts[g * both : (g + 1) * both, :HALF] = hi
            parts[g * both : (g + 1) * both, HALF:] = lo

    copies = []

    def finish_group(g0, total):
        box = jnp.dot(parts[g0 * both : (g0 + GROUP) * both, :], sums, preferred_element_type=jnp.float32)
        for pair in range(GROUP // 2):
            b = g0 // 2 + pair
            steps = []
            for half in range(2):
                g = 2 * b + half
                at = (g - g0) * both
                behind = halves[lax.rem(g + count - reach, count)]
                smooth = (box[at : at + both, :HALF] + total + edge_gain * behind) * scale
                total = total + box[at : at + both, HALF:]
                step = jnp.where(filtered, smooth, TIME_STEP * halves[g])
                for p in range(lev_parts):
                    stage[p, b, 2, half] = step[p * chans + 2 * levels : (p + 1) * chans]
                steps.append(step)
            step = jnp.concatenate(steps, axis=1)
            winds = []
            for f in range(2):
                winds += split2(
                    jnp.concatenate(
                        [step[p * chans + f * levels : p * chans + (f + 1) * levels] for p in range(lev_parts)],
                        axis=0,
                    )
                )
            mixed = jnp.dot(mixer, jnp.concatenate(winds, axis=0), preferred_element_type=jnp.float32)
            mixed = mixed[: 2 * lev_parts * levels] + mixed[2 * lev_parts * levels :]
            for f in range(2):
                for p in range(lev_parts):
                    at = (f * lev_parts + p) * levels
                    for half in range(2):
                        stage[p, b, f, half] = mixed[at : at + levels, half * HALF : (half + 1) * HALF]
            copies.append(pltpu.make_async_copy(stage.at[:, b], out.at[:, b], sems.at[b]))
            copies[-1].start()
        return total

    split_group(0)
    for g0 in range(0, count, GROUP):
        if g0 + GROUP < count:
            split_group(g0 + GROUP)
        total = finish_group(g0, total)
    for copy in copies:
        copy.wait()


def base_kernel(own_part, own, other, matrix, out):
    _, levels, rows, width = own.shape
    lower = own_part[0] == 0

    def by_row(ref, f, j0):
        flipped = [
            flip([ref[f, l0 + i, j0 : j0 + SUBLANES, :] for i in range(SUBLANES)])
            for l0 in range(0, levels, SUBLANES)
        ]
        return [jnp.concatenate([part[k] for part in flipped], axis=0) for k in range(SUBLANES)]

    for j0 in range(0, rows, SUBLANES):
        mine = [by_row(own, f, j0) for f in range(3)]
        theirs = [by_row(other, f, j0) for f in range(2)]
        for k in range(SUBLANES):
            j = j0 + k
            winds = []
            for f in range(2):
                a, b = mine[f][k], theirs[f][k]
                winds.append(jnp.concatenate([jnp.where(lower, a, b), jnp.where(lower, b, a)], axis=0))
            wind_hi, wind_lo = split2(jnp.concatenate(winds, axis=1))
            mixed = jnp.dot(
                mix_operand(matrix[j]),
                jnp.concatenate([wind_hi, wind_lo, wind_hi], axis=0),
                preferred_element_type=jnp.float32,
            )
            kept = jnp.where(lower, mixed[:levels], mixed[levels:])
            for f in range(2):
                out[j, f, 0] = kept[:, f * width : (f + 1) * width]
            out[j, 2, 0] = mine[2][k]


def finish_kernel(step, base, out, added, stage, in_sems, out_sems):
    fields, levels, rows, _ = out.shape
    blocks = levels // SUBLANES
    loads, copies = [], []
    for f in range(fields):
        for n in range(blocks):
            some = pl.ds(n * SUBLANES, SUBLANES)
            loads.append(
                pltpu.make_async_copy(base.at[:, f, :, some], added.at[:, f, :, some], in_sems.at[f * blocks + n])
            )
            loads[-1].start()
    for f in range(fields):
        for n in range(blocks):
            loads[f * blocks + n].wait()
            l0 = n * SUBLANES
            some = slice(l0, l0 + SUBLANES)
            for half in range(2):
                for j0 in range(0, rows, SUBLANES):
                    flipped = flip(
                        [step[j0 + k, f, half, some, :] + added[j0 + k, f, half, some, :] for k in range(SUBLANES)]
                    )
                    for i, value in enumerate(flipped):
                        stage[f, l0 + i, j0 : j0 + SUBLANES, half * HALF : (half + 1) * HALF] = value
            some = pl.ds(l0, SUBLANES)
            copies.append(
                pltpu.make_async_copy(stage.at[f, some], out.at[f, some], out_sems.at[f * blocks + n])
            )
            copies[-1].start()
    for copy in copies:
        copy.wait()


def per_device(prognostic, half_width, filter_mask, column_inverse):
    fields, levels, rows, width = prognostic.shape
    lon_devices, lat_devices, lev_devices = (lax.axis_size(a) for a in ("lon", "lat", "lev"))
    lon_index, lat_index, lev_index = (lax.axis_index(a) for a in ("lon", "lat", "lev"))
    chans = fields * levels
    halves = width // HALF
    params = pltpu.CompilerParams(vmem_limit_bytes=VMEM_LIMIT)
    hbm = pl.BlockSpec(memory_space=pltpu.HBM)
    vmem = pl.BlockSpec(memory_space=pltpu.VMEM)

    def in_hbm(x):
        return pltpu.with_memory_space_constraint(x, pltpu.HBM)

    def in_vmem(x):
        return pltpu.with_memory_space_constraint(x, pltpu.VMEM)


    with jax.named_scope("outer_rows"):
        first, last = pl.pallas_call(
            outer_rows_kernel,
            out_shape=(pltpu.VMEM((chans, width), jnp.float32),) * 2,
            in_specs=[hbm],
            out_specs=(vmem, vmem),
            scratch_shapes=[
                pltpu.SemaphoreType.DMA((fields, 2)),
            ],
            compiler_params=params,
        )(in_hbm(prognostic))
    north = lax.ppermute(first, "lat", [(i + 1, i) for i in range(lat_devices - 1)])
    south = lax.ppermute(last, "lat", [(i, i + 1) for i in range(lat_devices - 1)])
    other = lax.ppermute(prognostic[:2], "lev", [(0, 1), (1, 0)])

    global_rows = (lat_index * rows + jnp.arange(rows)).astype(jnp.float32)
    cosine, sine = latitudes(global_rows, rows * lat_devices)
    zonal = 0.25 / (cosine + 0.05)
    zonal_field = jnp.broadcast_to(zonal[:, None], (rows, width))
    coriolis_field = jnp.broadcast_to((0.5 * sine)[:, None], (rows, width))

    sent_rows = halves * chans + SUBLANES
    with jax.named_scope("tendencies"):
        tend, ends = pl.pallas_call(
            tendency_kernel,
            out_shape=(
                pltpu.HBM((rows, sent_rows, HALF), jnp.float32),
                pltpu.VMEM((2, halves * chans, HALF), jnp.float32),
            ),
            in_specs=[hbm, vmem, vmem],
            out_specs=(hbm, vmem),
            scratch_shapes=[
                pltpu.VMEM(prognostic.shape, jnp.float32),
                pltpu.VMEM(prognostic.shape, jnp.float32),
                pltpu.VMEM((rows, sent_rows, HALF), jnp.float32),
                pltpu.SemaphoreType.DMA((LOADS,)),
                pltpu.SemaphoreType.DMA((sent_rows // SUBLANES,)),
            ],
            compiler_params=params,
        )(in_hbm(prognostic), in_vmem(zonal_field), in_vmem(coriolis_field))

    with jax.named_scope("seam_rows"):
        tend = pl.pallas_call(
            seam_kernel,
            out_shape=pltpu.HBM(tend.shape, jnp.float32),
            in_specs=[vmem, vmem, vmem, hbm],
            out_specs=hbm,
            input_output_aliases={3: 0},
            scratch_shapes=[pltpu.VMEM(ends.shape, jnp.float32), pltpu.SemaphoreType.DMA((2,))],
            compiler_params=params,
        )(in_vmem(ends), in_vmem(north), in_vmem(south), in_hbm(tend))

    whole_rows = lax.all_to_all(tend, ("lev", "lon"), 0, 0, tiled=True)

    own_row = (lev_index * lon_devices + lon_index).astype(jnp.int32).reshape(1)
    stepped_shape = (lev_devices, lon_devices, fields, halves, levels, HALF)
    count = halves * lon_devices
    both = lev_devices * chans
    with jax.named_scope("row_filter"):
        stepped = pl.pallas_call(
            filter_kernel,
            out_shape=pltpu.HBM(stepped_shape, jnp.float32),
            grid_spec=pltpu.PrefetchScalarGridSpec(
                num_scalar_prefetch=4,
                grid=(1,),
                in_specs=[vmem, hbm],
                out_specs=hbm,
                scratch_shapes=[
                    pltpu.VMEM((count, both, HALF), jnp.float32),
                    pltpu.VMEM((count * both, 2 * HALF), jnp.bfloat16),
                    pltpu.VMEM((HALF, HALF), jnp.float32),
                    pltpu.VMEM(column_inverse.shape[1:], jnp.float32),
                    pltpu.VMEM(stepped_shape, jnp.float32),
                    pltpu.SemaphoreType.DMA,
                    pltpu.SemaphoreType.DMA((lon_devices,)),
                ],
            ),
            compiler_params=params,
        )(
            own_row,
            half_width,
            filter_mask,
            zonal,
            in_vmem(whole_rows.reshape(lev_devices, lon_devices, sent_rows, HALF)),
            in_hbm(column_inverse),
        )

    returned = lax.all_to_all(
        stepped.reshape((rows,) + stepped_shape[2:]), ("lev", "lon"), 0, 0, tiled=True
    )

    with jax.named_scope("base"):
        base = pl.pallas_call(
            base_kernel,
            out_shape=pltpu.HBM(returned.shape, jnp.float32),
            grid_spec=pltpu.PrefetchScalarGridSpec(
                num_scalar_prefetch=1,
                grid=(halves,),
                in_specs=[
                    pl.BlockSpec((fields, levels, rows, HALF), lambda i, *_: (0, 0, 0, i)),
                    pl.BlockSpec((2, levels, rows, HALF), lambda i, *_: (0, 0, 0, i)),
                    pl.BlockSpec(column_inverse.shape, lambda i, *_: (0, 0, 0)),
                ],
                out_specs=pl.BlockSpec((rows, fields, 1, levels, HALF), lambda i, *_: (0, 0, i, 0, 0)),
            ),
            compiler_params=params,
        )(lev_index.astype(jnp.int32).reshape(1), prognostic, other, column_inverse)

    with jax.named_scope("finish"):
        return pl.pallas_call(
            finish_kernel,
            out_shape=jax.ShapeDtypeStruct(prognostic.shape, jnp.float32),
            in_specs=[vmem, hbm],
            out_specs=hbm,
            scratch_shapes=[
                pltpu.VMEM(returned.shape, jnp.float32),
                pltpu.VMEM(prognostic.shape, jnp.float32),
                pltpu.SemaphoreType.DMA((fields * levels // SUBLANES,)),
                pltpu.SemaphoreType.DMA((fields * levels // SUBLANES,)),
            ],
            compiler_params=params,
        )(in_vmem(returned), in_hbm(base))


def solution(mesh):
    placed = (P(None, "lev", "lat", "lon"), P("lat"), P("lat"), P("lat", None, None))
    return jax.shard_map(
        per_device,
        mesh=mesh,
        in_specs=placed,
        out_specs=P(None, "lev", "lat", "lon"),
        check_vma=False,
    )
```

```python
import jax
import jax.numpy as jnp
from jax import lax
from jax.experimental import pallas as pl
from jax.experimental.pallas import tpu as pltpu
from jax.sharding import PartitionSpec as P

TIME_STEP = 0.5
VISCOSITY = 0.05
MERIDIONAL = 0.25
HALF = 128
SUBLANES = 8
VMEM_LIMIT = 32 * 1024 * 1024
GROUP = 4
LOADS = 4


def latitudes(global_rows, row_total):
    latitude_angle = -0.5 * jnp.pi + (global_rows + 0.5) * jnp.pi / row_total
    return (jnp.cos(latitude_angle), jnp.sin(latitude_angle))


def flip(tiles):
    row = lax.broadcasted_iota(jnp.int32, tiles[0].shape, 0)
    for d in (4, 2, 1):
        keep = (row & d) == 0
        turned = list(tiles)
        for i in range(SUBLANES):
            if not i & d:
                a, b = tiles[i], tiles[i + d]
                turned[i] = jnp.where(keep, a, pltpu.roll(b, d, 0))
                turned[i + d] = jnp.where(keep, pltpu.roll(a, SUBLANES - d, 0), b)
        tiles = turned
    return tiles


def fetch_kernel(prog, tile, first, last, sems):
    fields, levels, rows, _ = prog.shape
    per_load = levels // LOADS
    loads = []
    for f in range(fields):
        for load in range(LOADS):
            some = pl.ds(load * per_load, per_load)
            loads.append(pltpu.make_async_copy(prog.at[f, some], tile.at[f, some], sems.at[f, load]))
            loads[-1].start()
    for f in range(fields):
        for l in range(levels):
            if l % per_load == 0:
                loads[f * LOADS + l // per_load].wait()
            c = f * levels + l
            last[c : c + 1, :] = tile[f, l, rows - 1 : rows, :]
            first[c : c + 1, :] = tile[f, l, 0:1, :]


def tendency_kernel(tile, zonal, coriolis, out, ends, turn, stage, out_sems):
    _, levels, rows, width = tile.shape
    chans = 3 * levels
    payload = 2 * chans
    copies = []

    def send(first, sem):
        some = pl.ds(first, SUBLANES)
        copies.append(pltpu.make_async_copy(stage.at[:, some], out.at[:, some], out_sems.at[sem]))
        copies[-1].start()

    row_id = lax.broadcasted_iota(jnp.int32, (rows, width), 0)
    col_id = lax.broadcasted_iota(jnp.int32, (rows, width), 1)
    lane_id = lax.broadcasted_iota(jnp.int32, (rows, HALF), 1)
    first_row, last_row = row_id == 0, row_id == rows - 1
    first_col, last_col = col_id == 0, col_id == width - 1
    zon, cor = zonal[...], coriolis[...]
    edge_rows = jnp.zeros((rows, HALF), jnp.float32)
    for l in range(levels):
        centre, dx, dy, sx = [], [], [], []
        for f in range(3):
            c = f * levels + l
            here = tile[f, l]
            e = jnp.where(last_col, 0.0, pltpu.roll(here, width - 1, 1))
            w = jnp.where(first_col, 0.0, pltpu.roll(here, 1, 1))
            n = jnp.where(last_row, 0.0, pltpu.roll(here, rows - 1, 0))
            s = jnp.where(first_row, 0.0, pltpu.roll(here, 1, 0))
            centre.append(here)
            dx.append(e - w)
            dy.append(n - s)
            sx.append(e + w + n + s - 4.0 * here)
            first = here[:, :HALF]
            last = here[:, width - HALF :]
            if c:
                first = pltpu.roll(first, c, 1)
            last = pltpu.roll(last, (chans + c + 1) % HALF, 1)
            edge_rows = jnp.where(lane_id == c, first, jnp.where(lane_id == chans + c, last, edge_rows))
        tends = (
            -zon * dx[2] + cor * centre[1] + VISCOSITY * sx[0],
            -MERIDIONAL * dy[2] - cor * centre[0] + VISCOSITY * sx[1],
            -zon * dx[0] - MERIDIONAL * dy[1],
        )
        for f in range(3):
            turn[f, l] = tends[f]
        if (l + 1) % SUBLANES:
            continue
        l0 = l + 1 - SUBLANES
        for f in range(3):
            for half in range(2):
                at = (2 * f + half) * levels + l0
                for j0 in range(0, rows, SUBLANES):
                    flipped = flip(
                        [
                            turn[f, l0 + i, j0 : j0 + SUBLANES, half * HALF : (half + 1) * HALF]
                            for i in range(SUBLANES)
                        ]
                    )
                    for k, value in enumerate(flipped):
                        j = j0 + k
                        stage[j, at : at + SUBLANES, :] = value
                        if j in (0, rows - 1):
                            ends[min(j, 1), at : at + SUBLANES, :] = value
                send(at, at // SUBLANES)
    for j in range(rows):
        stage[j, payload:, :] = jnp.broadcast_to(edge_rows[j : j + 1, :], (SUBLANES, HALF))
    send(payload, payload // SUBLANES)
    for copy in copies:
        copy.wait()


def seam_kernel(ends, north, south, tend, out, stage, sems):
    del tend
    chans = south.shape[0]
    levels = chans // 3
    copies = []
    for at, beyond, sign in ((0, south, -1.0), (1, north, 1.0)):
        for half in range(2):
            lanes = slice(half * HALF, (half + 1) * HALF)
            u, v, h = (beyond[f * levels : (f + 1) * levels, lanes] for f in range(3))
            slope = sign * MERIDIONAL
            for f, term in enumerate((VISCOSITY * u, VISCOSITY * v - slope * h, -slope * v)):
                some = slice((2 * f + half) * levels, (2 * f + half + 1) * levels)
                stage[at, some, :] = ends[at, some, :] + term
        row = at * (out.shape[0] - 1)
        copies.append(pltpu.make_async_copy(stage.at[at], out.at[row, pl.ds(0, 2 * chans)], sems.at[at]))
        copies[-1].start()
    for copy in copies:
        copy.wait()


def split2(x):
    hi = x.astype(jnp.bfloat16)
    return hi, (x - hi.astype(jnp.float32)).astype(jnp.bfloat16)


def mix_operand(matrix):
    hi, lo = split2(matrix)
    return jnp.concatenate([hi, hi, lo], axis=1)


def pair_mix_operand(matrix):
    hi, lo = split2(matrix)
    none = jnp.zeros_like(hi)
    return jnp.concatenate(
        [
            jnp.concatenate([hi, hi, none, none], axis=1),
            jnp.concatenate([none, none, hi, hi], axis=1),
            jnp.concatenate([lo, none, none, none], axis=1),
            jnp.concatenate([none, none, lo, none], axis=1),
        ],
        axis=0,
    )


def filter_kernel(
    own_row, half_width, filter_mask, zonal, tend, matrices, out, halves, parts, seam, matrix, stage, matrix_sem, sems
):
    lev_parts, blocks, levels = out.shape[0], out.shape[1], out.shape[4]
    chans = 3 * levels
    payload = 2 * chans
    count = 2 * blocks
    both = lev_parts * chans
    row = own_row[0]
    fetch = pltpu.make_async_copy(matrices.at[row], matrix, matrix_sem)
    fetch.start()
    reach = half_width[row]
    whole = reach == count // 2
    norm = jnp.where(whole, count * HALF, 2 * HALF * reach + 1).astype(jnp.float32)
    filtered = filter_mask[row] == 1
    edge_gain = jnp.where(whole, 0.0, 1.0).astype(jnp.float32)

    for b in range(blocks):
        for part in range(lev_parts):
            at = b * lev_parts + part
            seam[at : at + 1, :] = tend[part, b, payload : payload + 1, :]
    columns = seam[...].T
    zon = zonal[row]
    u, v, h = (columns[f * levels : (f + 1) * levels] for f in range(3))
    from_east = jnp.concatenate([VISCOSITY * u - zon * h, VISCOSITY * v, -zon * u], axis=0)
    u, v, h = (columns[chans + f * levels : chans + (f + 1) * levels] for f in range(3))
    from_west = jnp.concatenate([VISCOSITY * u + zon * h, VISCOSITY * v, zon * u], axis=0)
    lane_id = lax.broadcasted_iota(jnp.int32, (levels, HALF), 1)
    window = jnp.zeros((both, HALF), jnp.float32)
    for g in range(count):
        b, half = divmod(g, 2)
        beyond = (b + 1) % blocks if half else (b + blocks - 1) % blocks
        terms, lane = (from_east, HALF - 1) if half else (from_west, 0)
        pieces = []
        for part in range(lev_parts):
            source = beyond * lev_parts + part
            for f in range(3):
                here = tend[part, b, (2 * f + half) * levels : (2 * f + half + 1) * levels, :]
                term = terms[f * levels : (f + 1) * levels, source : source + 1]
                pieces.append(here + jnp.where(lane_id == lane, term, 0.0))
        value = jnp.concatenate(pieces, axis=0)
        halves[g] = value
        inside = lax.rem(g + reach, count) < 2 * reach
        window = window + jnp.where(inside, 1.0, 0.0).astype(jnp.float32) * value

    src = lax.broadcasted_iota(jnp.int32, (2 * HALF, 2 * HALF), 0)
    dst = lax.broadcasted_iota(jnp.int32, (2 * HALF, 2 * HALF), 1)
    sums = jnp.where((src & (HALF - 1)) <= dst, 1.0, 0.0).astype(jnp.bfloat16)
    fetch.wait()
    mixer = pair_mix_operand(matrix[...])
    scale = TIME_STEP / norm
    total = jnp.dot(
        jnp.concatenate(split2(window), axis=1), sums, preferred_element_type=jnp.float32
    )[:, HALF:]

    def split_group(g0):
        for g in range(g0, g0 + GROUP):
            ahead = halves[lax.rem(g + reach, count)]
            behind = halves[lax.rem(g + count - reach, count)]
            hi, lo = split2(ahead - behind)
            parts[g * both : (g + 1) * both, :HALF] = hi
            parts[g * both : (g + 1) * both, HALF:] = lo

    copies = []

    def finish_group(g0, total):
        box = jnp.dot(parts[g0 * both : (g0 + GROUP) * both, :], sums, preferred_element_type=jnp.float32)
        for pair in range(GROUP // 2):
            b = g0 // 2 + pair
            steps = []
            for half in range(2):
                g = 2 * b + half
                at = (g - g0) * both
                behind = halves[lax.rem(g + count - reach, count)]
                smooth = (box[at : at + both, :HALF] + total + edge_gain * behind) * scale
                total = total + box[at : at + both, HALF:]
                step = jnp.where(filtered, smooth, TIME_STEP * halves[g])
                for p in range(lev_parts):
                    stage[p, b, 2, half] = step[p * chans + 2 * levels : (p + 1) * chans]
                steps.append(step)
            step = jnp.concatenate(steps, axis=1)
            winds = []
            for f in range(2):
                winds += split2(
                    jnp.concatenate(
                        [step[p * chans + f * levels : p * chans + (f + 1) * levels] for p in range(lev_parts)],
                        axis=0,
                    )
                )
            mixed = jnp.dot(mixer, jnp.concatenate(winds, axis=0), preferred_element_type=jnp.float32)
            mixed = mixed[: 2 * lev_parts * levels] + mixed[2 * lev_parts * levels :]
            for f in range(2):
                for p in range(lev_parts):
                    at = (f * lev_parts + p) * levels
                    for half in range(2):
                        stage[p, b, f, half] = mixed[at : at + levels, half * HALF : (half + 1) * HALF]
            copies.append(pltpu.make_async_copy(stage.at[:, b], out.at[:, b], sems.at[b]))
            copies[-1].start()
        return total

    split_group(0)
    for g0 in range(0, count, GROUP):
        if g0 + GROUP < count:
            split_group(g0 + GROUP)
        total = finish_group(g0, total)
    for copy in copies:
        copy.wait()


def base_kernel(own_part, own, other, matrix, out):
    _, levels, rows, width = own.shape
    lower = own_part[0] == 0

    def by_row(ref, f, j0):
        flipped = [
            flip([ref[f, l0 + i, j0 : j0 + SUBLANES, :] for i in range(SUBLANES)])
            for l0 in range(0, levels, SUBLANES)
        ]
        return [jnp.concatenate([part[k] for part in flipped], axis=0) for k in range(SUBLANES)]

    for j0 in range(0, rows, SUBLANES):
        mine = [by_row(own, f, j0) for f in range(3)]
        theirs = [by_row(other, f, j0) for f in range(2)]
        for k in range(SUBLANES):
            j = j0 + k
            winds = []
            for f in range(2):
                a, b = mine[f][k], theirs[f][k]
                winds.append(jnp.concatenate([jnp.where(lower, a, b), jnp.where(lower, b, a)], axis=0))
            wind_hi, wind_lo = split2(jnp.concatenate(winds, axis=1))
            mixed = jnp.dot(
                mix_operand(matrix[j]),
                jnp.concatenate([wind_hi, wind_lo, wind_hi], axis=0),
                preferred_element_type=jnp.float32,
            )
            kept = jnp.where(lower, mixed[:levels], mixed[levels:])
            for f in range(2):
                out[j, f, 0] = kept[:, f * width : (f + 1) * width]
            out[j, 2, 0] = mine[2][k]


def finish_kernel(step, base, out, added, stage, in_sems, out_sems):
    fields, levels, rows, _ = out.shape
    blocks = levels // SUBLANES
    loads, copies = [], []
    for f in range(fields):
        for n in range(blocks):
            some = pl.ds(n * SUBLANES, SUBLANES)
            loads.append(
                pltpu.make_async_copy(base.at[:, f, :, some], added.at[:, f, :, some], in_sems.at[f * blocks + n])
            )
            loads[-1].start()
    for f in range(fields):
        for n in range(blocks):
            loads[f * blocks + n].wait()
            l0 = n * SUBLANES
            some = slice(l0, l0 + SUBLANES)
            for half in range(2):
                for j0 in range(0, rows, SUBLANES):
                    flipped = flip(
                        [step[j0 + k, f, half, some, :] + added[j0 + k, f, half, some, :] for k in range(SUBLANES)]
                    )
                    for i, value in enumerate(flipped):
                        stage[f, l0 + i, j0 : j0 + SUBLANES, half * HALF : (half + 1) * HALF] = value
            some = pl.ds(l0, SUBLANES)
            copies.append(
                pltpu.make_async_copy(stage.at[f, some], out.at[f, some], out_sems.at[f * blocks + n])
            )
            copies[-1].start()
    for copy in copies:
        copy.wait()


def per_device(prognostic, half_width, filter_mask, column_inverse):
    fields, levels, rows, width = prognostic.shape
    lon_devices, lat_devices, lev_devices = (lax.axis_size(a) for a in ("lon", "lat", "lev"))
    lon_index, lat_index, lev_index = (lax.axis_index(a) for a in ("lon", "lat", "lev"))
    chans = fields * levels
    halves = width // HALF
    params = pltpu.CompilerParams(vmem_limit_bytes=VMEM_LIMIT)
    hbm = pl.BlockSpec(memory_space=pltpu.HBM)
    vmem = pl.BlockSpec(memory_space=pltpu.VMEM)

    def in_hbm(x):
        return pltpu.with_memory_space_constraint(x, pltpu.HBM)

    def in_vmem(x):
        return pltpu.with_memory_space_constraint(x, pltpu.VMEM)


    with jax.named_scope("fetch"):
        tile, first, last = pl.pallas_call(
            fetch_kernel,
            out_shape=(
                pltpu.VMEM(prognostic.shape, jnp.float32),
                pltpu.VMEM((chans, width), jnp.float32),
                pltpu.VMEM((chans, width), jnp.float32),
            ),
            in_specs=[hbm],
            out_specs=(vmem, vmem, vmem),
            scratch_shapes=[pltpu.SemaphoreType.DMA((fields, LOADS))],
            compiler_params=params,
        )(in_hbm(prognostic))
    north = lax.ppermute(first, "lat", [(i + 1, i) for i in range(lat_devices - 1)])
    south = lax.ppermute(last, "lat", [(i, i + 1) for i in range(lat_devices - 1)])
    other = lax.ppermute(prognostic[:2], "lev", [(0, 1), (1, 0)])

    global_rows = (lat_index * rows + jnp.arange(rows)).astype(jnp.float32)
    cosine, sine = latitudes(global_rows, rows * lat_devices)
    zonal = 0.25 / (cosine + 0.05)
    zonal_field = jnp.broadcast_to(zonal[:, None], (rows, width))
    coriolis_field = jnp.broadcast_to((0.5 * sine)[:, None], (rows, width))

    sent_rows = halves * chans + SUBLANES
    with jax.named_scope("tendencies"):
        tend, ends = pl.pallas_call(
            tendency_kernel,
            out_shape=(
                pltpu.HBM((rows, sent_rows, HALF), jnp.float32),
                pltpu.VMEM((2, halves * chans, HALF), jnp.float32),
            ),
            in_specs=[vmem, vmem, vmem],
            out_specs=(hbm, vmem),
            scratch_shapes=[
                pltpu.VMEM(prognostic.shape, jnp.float32),
                pltpu.VMEM((rows, sent_rows, HALF), jnp.float32),
                pltpu.SemaphoreType.DMA((sent_rows // SUBLANES,)),
            ],
            compiler_params=params,
        )(in_vmem(tile), in_vmem(zonal_field), in_vmem(coriolis_field))

    with jax.named_scope("seam_rows"):
        tend = pl.pallas_call(
            seam_kernel,
            out_shape=pltpu.HBM(tend.shape, jnp.float32),
            in_specs=[vmem, vmem, vmem, hbm],
            out_specs=hbm,
            input_output_aliases={3: 0},
            scratch_shapes=[pltpu.VMEM(ends.shape, jnp.float32), pltpu.SemaphoreType.DMA((2,))],
            compiler_params=params,
        )(in_vmem(ends), in_vmem(north), in_vmem(south), in_hbm(tend))

    whole_rows = lax.all_to_all(tend, ("lev", "lon"), 0, 0, tiled=True)

    own_row = (lev_index * lon_devices + lon_index).astype(jnp.int32).reshape(1)
    stepped_shape = (lev_devices, lon_devices, fields, halves, levels, HALF)
    count = halves * lon_devices
    both = lev_devices * chans
    with jax.named_scope("row_filter"):
        stepped = pl.pallas_call(
            filter_kernel,
            out_shape=pltpu.HBM(stepped_shape, jnp.float32),
            grid_spec=pltpu.PrefetchScalarGridSpec(
                num_scalar_prefetch=4,
                grid=(1,),
                in_specs=[vmem, hbm],
                out_specs=hbm,
                scratch_shapes=[
                    pltpu.VMEM((count, both, HALF), jnp.float32),
                    pltpu.VMEM((count * both, 2 * HALF), jnp.bfloat16),
                    pltpu.VMEM((HALF, HALF), jnp.float32),
                    pltpu.VMEM(column_inverse.shape[1:], jnp.float32),
                    pltpu.VMEM(stepped_shape, jnp.float32),
                    pltpu.SemaphoreType.DMA,
                    pltpu.SemaphoreType.DMA((lon_devices,)),
                ],
            ),
            compiler_params=params,
        )(
            own_row,
            half_width,
            filter_mask,
            zonal,
            in_vmem(whole_rows.reshape(lev_devices, lon_devices, sent_rows, HALF)),
            in_hbm(column_inverse),
        )

    returned = lax.all_to_all(
        stepped.reshape((rows,) + stepped_shape[2:]), ("lev", "lon"), 0, 0, tiled=True
    )

    with jax.named_scope("base"):
        base = pl.pallas_call(
            base_kernel,
            out_shape=pltpu.HBM(returned.shape, jnp.float32),
            grid_spec=pltpu.PrefetchScalarGridSpec(
                num_scalar_prefetch=1,
                grid=(halves,),
                in_specs=[
                    pl.BlockSpec((fields, levels, rows, HALF), lambda i, *_: (0, 0, 0, i)),
                    pl.BlockSpec((2, levels, rows, HALF), lambda i, *_: (0, 0, 0, i)),
                    pl.BlockSpec(column_inverse.shape, lambda i, *_: (0, 0, 0)),
                ],
                out_specs=pl.BlockSpec((rows, fields, 1, levels, HALF), lambda i, *_: (0, 0, i, 0, 0)),
            ),
            compiler_params=params,
        )(lev_index.astype(jnp.int32).reshape(1), prognostic, other, column_inverse)

    with jax.named_scope("finish"):
        return pl.pallas_call(
            finish_kernel,
            out_shape=jax.ShapeDtypeStruct(prognostic.shape, jnp.float32),
            in_specs=[vmem, hbm],
            out_specs=hbm,
            scratch_shapes=[
                pltpu.VMEM(returned.shape, jnp.float32),
                pltpu.VMEM(prognostic.shape, jnp.float32),
                pltpu.SemaphoreType.DMA((fields * levels // SUBLANES,)),
                pltpu.SemaphoreType.DMA((fields * levels // SUBLANES,)),
            ],
            compiler_params=params,
        )(in_vmem(returned), in_hbm(base))


def solution(mesh):
    placed = (P(None, "lev", "lat", "lon"), P("lat"), P("lat"), P("lat", None, None))
    return jax.shard_map(
        per_device,
        mesh=mesh,
        in_specs=placed,
        out_specs=P(None, "lev", "lat", "lon"),
        check_vma=False,
    )
```

```python
import jax
import jax.numpy as jnp
from jax import lax
from jax.experimental import pallas as pl
from jax.experimental.pallas import tpu as pltpu
from jax.sharding import PartitionSpec as P

TIME_STEP = 0.5
VISCOSITY = 0.05
MERIDIONAL = 0.25
HALF = 128
SUBLANES = 8
VMEM_LIMIT = 32 * 1024 * 1024
GROUP = 4
LOADS = 4


def latitudes(global_rows, row_total):
    latitude_angle = -0.5 * jnp.pi + (global_rows + 0.5) * jnp.pi / row_total
    return (jnp.cos(latitude_angle), jnp.sin(latitude_angle))


def flip(tiles):
    row = lax.broadcasted_iota(jnp.int32, tiles[0].shape, 0)
    for d in (4, 2, 1):
        keep = (row & d) == 0
        turned = list(tiles)
        for i in range(SUBLANES):
            if not i & d:
                a, b = tiles[i], tiles[i + d]
                turned[i] = jnp.where(keep, a, pltpu.roll(b, d, 0))
                turned[i + d] = jnp.where(keep, pltpu.roll(a, SUBLANES - d, 0), b)
        tiles = turned
    return tiles


def fetch_kernel(prog, tile, first, last, sems):
    fields, levels, rows, _ = prog.shape
    per_load = levels // LOADS
    loads = []
    for f in range(fields):
        for load in range(LOADS):
            some = pl.ds(load * per_load, per_load)
            loads.append(pltpu.make_async_copy(prog.at[f, some], tile.at[f, some], sems.at[f, load]))
            loads[-1].start()
    for f in range(fields):
        for l in range(levels):
            if l % per_load == 0:
                loads[f * LOADS + l // per_load].wait()
            c = f * levels + l
            last[c : c + 1, :] = tile[f, l, rows - 1 : rows, :]
            first[c : c + 1, :] = tile[f, l, 0:1, :]


def tendency_kernel(tile, zonal, coriolis, out, ends, stage, sems):
    _, levels, rows, width = tile.shape
    chans = 3 * levels
    payload = 2 * chans
    row_id = lax.broadcasted_iota(jnp.int32, (SUBLANES, width), 0)
    col_id = lax.broadcasted_iota(jnp.int32, (SUBLANES, width), 1)
    lane_id = lax.broadcasted_iota(jnp.int32, (SUBLANES, HALF), 1)
    first_row, last_row = row_id == 0, row_id == SUBLANES - 1
    first_col, last_col = col_id == 0, col_id == width - 1
    copies = []
    for j0 in range(0, rows, SUBLANES):
        j1 = j0 + SUBLANES
        zon, cor = zonal[j0:j1, :], coriolis[j0:j1, :]
        edge_rows = jnp.zeros((SUBLANES, HALF), jnp.float32)
        for l0 in range(0, levels, SUBLANES):
            tends = [[], [], []]
            for l in range(l0, l0 + SUBLANES):
                centre, dx, dy, sx = [], [], [], []
                for f in range(3):
                    c = f * levels + l
                    here = tile[f, l, j0:j1, :]
                    after = tile[f, l, j1 : j1 + 1, :] if j1 < rows else 0.0
                    before = tile[f, l, j0 - 1 : j0, :] if j0 else 0.0
                    e = jnp.where(last_col, 0.0, pltpu.roll(here, width - 1, 1))
                    w = jnp.where(first_col, 0.0, pltpu.roll(here, 1, 1))
                    n = jnp.where(last_row, after, pltpu.roll(here, SUBLANES - 1, 0))
                    s = jnp.where(first_row, before, pltpu.roll(here, 1, 0))
                    centre.append(here)
                    dx.append(e - w)
                    dy.append(n - s)
                    sx.append(e + w + n + s - 4.0 * here)
                    first = here[:, :HALF]
                    last = here[:, width - HALF :]
                    if c:
                        first = pltpu.roll(first, c, 1)
                    last = pltpu.roll(last, (chans + c + 1) % HALF, 1)
                    edge_rows = jnp.where(lane_id == c, first, jnp.where(lane_id == chans + c, last, edge_rows))
                tends[0].append(-zon * dx[2] + cor * centre[1] + VISCOSITY * sx[0])
                tends[1].append(-MERIDIONAL * dy[2] - cor * centre[0] + VISCOSITY * sx[1])
                tends[2].append(-zon * dx[0] - MERIDIONAL * dy[1])
            for f in range(3):
                for half in range(2):
                    at = (2 * f + half) * levels + l0
                    flipped = flip([value[:, half * HALF : (half + 1) * HALF] for value in tends[f]])
                    for k, value in enumerate(flipped):
                        j = j0 + k
                        stage[j, at : at + SUBLANES, :] = value
                        if j in (0, rows - 1):
                            ends[min(j, 1), at : at + SUBLANES, :] = value
        for k in range(SUBLANES):
            stage[j0 + k, payload:, :] = jnp.broadcast_to(edge_rows[k : k + 1, :], (SUBLANES, HALF))
        some = pl.ds(j0, SUBLANES)
        copies.append(pltpu.make_async_copy(stage.at[some], out.at[some], sems.at[j0 // SUBLANES]))
        copies[-1].start()
    for copy in copies:
        copy.wait()


def seam_kernel(ends, north, south, tend, out, stage, sems):
    del tend
    chans = south.shape[0]
    levels = chans // 3
    copies = []
    for at, beyond, sign in ((0, south, -1.0), (1, north, 1.0)):
        for half in range(2):
            lanes = slice(half * HALF, (half + 1) * HALF)
            u, v, h = (beyond[f * levels : (f + 1) * levels, lanes] for f in range(3))
            slope = sign * MERIDIONAL
            for f, term in enumerate((VISCOSITY * u, VISCOSITY * v - slope * h, -slope * v)):
                some = slice((2 * f + half) * levels, (2 * f + half + 1) * levels)
                stage[at, some, :] = ends[at, some, :] + term
        row = at * (out.shape[0] - 1)
        copies.append(pltpu.make_async_copy(stage.at[at], out.at[row, pl.ds(0, 2 * chans)], sems.at[at]))
        copies[-1].start()
    for copy in copies:
        copy.wait()


def split2(x):
    hi = x.astype(jnp.bfloat16)
    return hi, (x - hi.astype(jnp.float32)).astype(jnp.bfloat16)


def mix_operand(matrix):
    hi, lo = split2(matrix)
    return jnp.concatenate([hi, hi, lo], axis=1)


def pair_mix_operand(matrix):
    hi, lo = split2(matrix)
    none = jnp.zeros_like(hi)
    return jnp.concatenate(
        [
            jnp.concatenate([hi, hi, none, none], axis=1),
            jnp.concatenate([none, none, hi, hi], axis=1),
            jnp.concatenate([lo, none, none, none], axis=1),
            jnp.concatenate([none, none, lo, none], axis=1),
        ],
        axis=0,
    )


def filter_kernel(
    own_row, half_width, filter_mask, zonal, tend, matrices, out, halves, parts, seam, matrix, stage, matrix_sem, sems
):
    lev_parts, blocks, levels = out.shape[0], out.shape[1], out.shape[4]
    chans = 3 * levels
    payload = 2 * chans
    count = 2 * blocks
    both = lev_parts * chans
    row = own_row[0]
    fetch = pltpu.make_async_copy(matrices.at[row], matrix, matrix_sem)
    fetch.start()
    reach = half_width[row]
    whole = reach == count // 2
    norm = jnp.where(whole, count * HALF, 2 * HALF * reach + 1).astype(jnp.float32)
    filtered = filter_mask[row] == 1
    edge_gain = jnp.where(whole, 0.0, 1.0).astype(jnp.float32)

    for b in range(blocks):
        for part in range(lev_parts):
            at = b * lev_parts + part
            seam[at : at + 1, :] = tend[part, b, payload : payload + 1, :]
    columns = seam[...].T
    zon = zonal[row]
    u, v, h = (columns[f * levels : (f + 1) * levels] for f in range(3))
    from_east = jnp.concatenate([VISCOSITY * u - zon * h, VISCOSITY * v, -zon * u], axis=0)
    u, v, h = (columns[chans + f * levels : chans + (f + 1) * levels] for f in range(3))
    from_west = jnp.concatenate([VISCOSITY * u + zon * h, VISCOSITY * v, zon * u], axis=0)
    lane_id = lax.broadcasted_iota(jnp.int32, (levels, HALF), 1)
    window = jnp.zeros((both, HALF), jnp.float32)
    for g in range(count):
        b, half = divmod(g, 2)
        beyond = (b + 1) % blocks if half else (b + blocks - 1) % blocks
        terms, lane = (from_east, HALF - 1) if half else (from_west, 0)
        pieces = []
        for part in range(lev_parts):
            source = beyond * lev_parts + part
            for f in range(3):
                here = tend[part, b, (2 * f + half) * levels : (2 * f + half + 1) * levels, :]
                term = terms[f * levels : (f + 1) * levels, source : source + 1]
                pieces.append(here + jnp.where(lane_id == lane, term, 0.0))
        value = jnp.concatenate(pieces, axis=0)
        halves[g] = value
        inside = lax.rem(g + reach, count) < 2 * reach
        window = window + jnp.where(inside, 1.0, 0.0).astype(jnp.float32) * value

    src = lax.broadcasted_iota(jnp.int32, (2 * HALF, 2 * HALF), 0)
    dst = lax.broadcasted_iota(jnp.int32, (2 * HALF, 2 * HALF), 1)
    sums = jnp.where((src & (HALF - 1)) <= dst, 1.0, 0.0).astype(jnp.bfloat16)
    fetch.wait()
    mixer = pair_mix_operand(matrix[...])
    scale = TIME_STEP / norm
    total = jnp.dot(
        jnp.concatenate(split2(window), axis=1), sums, preferred_element_type=jnp.float32
    )[:, HALF:]

    def split_group(g0):
        for g in range(g0, g0 + GROUP):
            ahead = halves[lax.rem(g + reach, count)]
            behind = halves[lax.rem(g + count - reach, count)]
            hi, lo = split2(ahead - behind)
            parts[g * both : (g + 1) * both, :HALF] = hi
            parts[g * both : (g + 1) * both, HALF:] = lo

    def emit(b, steps):
        for half, step in enumerate(steps):
            for p in range(lev_parts):
                stage[p, b, 2, half] = step[p * chans + 2 * levels : (p + 1) * chans]
        step = jnp.concatenate(steps, axis=1)
        winds = []
        for f in range(2):
            winds += split2(
                jnp.concatenate(
                    [step[p * chans + f * levels : p * chans + (f + 1) * levels] for p in range(lev_parts)],
                    axis=0,
                )
            )
        mixed = jnp.dot(mixer, jnp.concatenate(winds, axis=0), preferred_element_type=jnp.float32)
        mixed = mixed[: 2 * lev_parts * levels] + mixed[2 * lev_parts * levels :]
        for f in range(2):
            for p in range(lev_parts):
                at = (f * lev_parts + p) * levels
                for half in range(2):
                    stage[p, b, f, half] = mixed[at : at + levels, half * HALF : (half + 1) * HALF]
        copy = pltpu.make_async_copy(stage.at[:, b], out.at[:, b], sems.at[b])
        copy.start()
        return copy

    @pl.when(filtered)
    def _():
        copies = []
        running = total
        split_group(0)
        for g0 in range(0, count, GROUP):
            if g0 + GROUP < count:
                split_group(g0 + GROUP)
            box = jnp.dot(parts[g0 * both : (g0 + GROUP) * both, :], sums, preferred_element_type=jnp.float32)
            for b in range(g0 // 2, (g0 + GROUP) // 2):
                steps = []
                for g in (2 * b, 2 * b + 1):
                    at = (g - g0) * both
                    behind = halves[lax.rem(g + count - reach, count)]
                    steps.append((box[at : at + both, :HALF] + running + edge_gain * behind) * scale)
                    running = running + box[at : at + both, HALF:]
                copies.append(emit(b, steps))
        for copy in copies:
            copy.wait()

    @pl.when(jnp.logical_not(filtered))
    def _():
        copies = [emit(b, [TIME_STEP * halves[2 * b], TIME_STEP * halves[2 * b + 1]]) for b in range(blocks)]
        for copy in copies:
            copy.wait()


def base_kernel(own_part, own, other, matrix, out):
    _, levels, rows, width = own.shape
    lower = own_part[0] == 0

    def by_row(ref, f, j0):
        flipped = [
            flip([ref[f, l0 + i, j0 : j0 + SUBLANES, :] for i in range(SUBLANES)])
            for l0 in range(0, levels, SUBLANES)
        ]
        return [jnp.concatenate([part[k] for part in flipped], axis=0) for k in range(SUBLANES)]

    for j0 in range(0, rows, SUBLANES):
        mine = [by_row(own, f, j0) for f in range(3)]
        theirs = [by_row(other, f, j0) for f in range(2)]
        for k in range(SUBLANES):
            j = j0 + k
            winds = []
            for f in range(2):
                a, b = mine[f][k], theirs[f][k]
                winds.append(jnp.concatenate([jnp.where(lower, a, b), jnp.where(lower, b, a)], axis=0))
            wind_hi, wind_lo = split2(jnp.concatenate(winds, axis=1))
            mixed = jnp.dot(
                mix_operand(matrix[j]),
                jnp.concatenate([wind_hi, wind_lo, wind_hi], axis=0),
                preferred_element_type=jnp.float32,
            )
            kept = jnp.where(lower, mixed[:levels], mixed[levels:])
            for f in range(2):
                out[j, f, 0] = kept[:, f * width : (f + 1) * width]
            out[j, 2, 0] = mine[2][k]


def finish_kernel(step, base, out, added, stage, in_sems, out_sems):
    fields, levels, rows, _ = out.shape
    blocks = levels // SUBLANES
    loads, copies = [], []
    for f in range(fields):
        for n in range(blocks):
            some = pl.ds(n * SUBLANES, SUBLANES)
            loads.append(
                pltpu.make_async_copy(base.at[:, f, :, some], added.at[:, f, :, some], in_sems.at[f * blocks + n])
            )
            loads[-1].start()
    for f in range(fields):
        for n in range(blocks):
            loads[f * blocks + n].wait()
            l0 = n * SUBLANES
            some = slice(l0, l0 + SUBLANES)
            for half in range(2):
                for j0 in range(0, rows, SUBLANES):
                    flipped = flip(
                        [step[j0 + k, f, half, some, :] + added[j0 + k, f, half, some, :] for k in range(SUBLANES)]
                    )
                    for i, value in enumerate(flipped):
                        stage[f, l0 + i, j0 : j0 + SUBLANES, half * HALF : (half + 1) * HALF] = value
            some = pl.ds(l0, SUBLANES)
            copies.append(
                pltpu.make_async_copy(stage.at[f, some], out.at[f, some], out_sems.at[f * blocks + n])
            )
            copies[-1].start()
    for copy in copies:
        copy.wait()


def per_device(prognostic, half_width, filter_mask, column_inverse):
    fields, levels, rows, width = prognostic.shape
    lon_devices, lat_devices, lev_devices = (lax.axis_size(a) for a in ("lon", "lat", "lev"))
    lon_index, lat_index, lev_index = (lax.axis_index(a) for a in ("lon", "lat", "lev"))
    chans = fields * levels
    halves = width // HALF
    params = pltpu.CompilerParams(vmem_limit_bytes=VMEM_LIMIT)
    hbm = pl.BlockSpec(memory_space=pltpu.HBM)
    vmem = pl.BlockSpec(memory_space=pltpu.VMEM)

    def in_hbm(x):
        return pltpu.with_memory_space_constraint(x, pltpu.HBM)

    def in_vmem(x):
        return pltpu.with_memory_space_constraint(x, pltpu.VMEM)


    with jax.named_scope("fetch"):
        tile, first, last = pl.pallas_call(
            fetch_kernel,
            out_shape=(
                pltpu.VMEM(prognostic.shape, jnp.float32),
                pltpu.VMEM((chans, width), jnp.float32),
                pltpu.VMEM((chans, width), jnp.float32),
            ),
            in_specs=[hbm],
            out_specs=(vmem, vmem, vmem),
            scratch_shapes=[pltpu.SemaphoreType.DMA((fields, LOADS))],
            compiler_params=params,
        )(in_hbm(prognostic))
    north = lax.ppermute(first, "lat", [(i + 1, i) for i in range(lat_devices - 1)])
    south = lax.ppermute(last, "lat", [(i, i + 1) for i in range(lat_devices - 1)])
    other = lax.ppermute(prognostic[:2], "lev", [(0, 1), (1, 0)])

    global_rows = (lat_index * rows + jnp.arange(rows)).astype(jnp.float32)
    cosine, sine = latitudes(global_rows, rows * lat_devices)
    zonal = 0.25 / (cosine + 0.05)
    zonal_field = jnp.broadcast_to(zonal[:, None], (rows, width))
    coriolis_field = jnp.broadcast_to((0.5 * sine)[:, None], (rows, width))

    sent_rows = halves * chans + SUBLANES
    with jax.named_scope("tendencies"):
        tend, ends = pl.pallas_call(
            tendency_kernel,
            out_shape=(
                pltpu.HBM((rows, sent_rows, HALF), jnp.float32),
                pltpu.VMEM((2, halves * chans, HALF), jnp.float32),
            ),
            in_specs=[vmem, vmem, vmem],
            out_specs=(hbm, vmem),
            scratch_shapes=[
                pltpu.VMEM((rows, sent_rows, HALF), jnp.float32),
                pltpu.SemaphoreType.DMA((rows // SUBLANES,)),
            ],
            compiler_params=params,
        )(in_vmem(tile), in_vmem(zonal_field), in_vmem(coriolis_field))

    with jax.named_scope("seam_rows"):
        tend = pl.pallas_call(
            seam_kernel,
            out_shape=pltpu.HBM(tend.shape, jnp.float32),
            in_specs=[vmem, vmem, vmem, hbm],
            out_specs=hbm,
            input_output_aliases={3: 0},
            scratch_shapes=[pltpu.VMEM(ends.shape, jnp.float32), pltpu.SemaphoreType.DMA((2,))],
            compiler_params=params,
        )(in_vmem(ends), in_vmem(north), in_vmem(south), in_hbm(tend))

    whole_rows = lax.all_to_all(tend, ("lev", "lon"), 0, 0, tiled=True)

    own_row = (lev_index * lon_devices + lon_index).astype(jnp.int32).reshape(1)
    stepped_shape = (lev_devices, lon_devices, fields, halves, levels, HALF)
    count = halves * lon_devices
    both = lev_devices * chans
    with jax.named_scope("row_filter"):
        stepped = pl.pallas_call(
            filter_kernel,
            out_shape=pltpu.HBM(stepped_shape, jnp.float32),
            grid_spec=pltpu.PrefetchScalarGridSpec(
                num_scalar_prefetch=4,
                grid=(1,),
                in_specs=[vmem, hbm],
                out_specs=hbm,
                scratch_shapes=[
                    pltpu.VMEM((count, both, HALF), jnp.float32),
                    pltpu.VMEM((count * both, 2 * HALF), jnp.bfloat16),
                    pltpu.VMEM((HALF, HALF), jnp.float32),
                    pltpu.VMEM(column_inverse.shape[1:], jnp.float32),
                    pltpu.VMEM(stepped_shape, jnp.float32),
                    pltpu.SemaphoreType.DMA,
                    pltpu.SemaphoreType.DMA((lon_devices,)),
                ],
            ),
            compiler_params=params,
        )(
            own_row,
            half_width,
            filter_mask,
            zonal,
            in_vmem(whole_rows.reshape(lev_devices, lon_devices, sent_rows, HALF)),
            in_hbm(column_inverse),
        )

    returned = lax.all_to_all(
        stepped.reshape((rows,) + stepped_shape[2:]), ("lev", "lon"), 0, 0, tiled=True
    )

    with jax.named_scope("base"):
        base = pl.pallas_call(
            base_kernel,
            out_shape=pltpu.HBM(returned.shape, jnp.float32),
            grid_spec=pltpu.PrefetchScalarGridSpec(
                num_scalar_prefetch=1,
                grid=(halves,),
                in_specs=[
                    pl.BlockSpec((fields, levels, rows, HALF), lambda i, *_: (0, 0, 0, i)),
                    pl.BlockSpec((2, levels, rows, HALF), lambda i, *_: (0, 0, 0, i)),
                    pl.BlockSpec(column_inverse.shape, lambda i, *_: (0, 0, 0)),
                ],
                out_specs=pl.BlockSpec((rows, fields, 1, levels, HALF), lambda i, *_: (0, 0, i, 0, 0)),
            ),
            compiler_params=params,
        )(lev_index.astype(jnp.int32).reshape(1), prognostic, other, column_inverse)

    with jax.named_scope("finish"):
        return pl.pallas_call(
            finish_kernel,
            out_shape=jax.ShapeDtypeStruct(prognostic.shape, jnp.float32),
            in_specs=[vmem, hbm],
            out_specs=hbm,
            scratch_shapes=[
                pltpu.VMEM(returned.shape, jnp.float32),
                pltpu.VMEM(prognostic.shape, jnp.float32),
                pltpu.SemaphoreType.DMA((fields * levels // SUBLANES,)),
                pltpu.SemaphoreType.DMA((fields * levels // SUBLANES,)),
            ],
            compiler_params=params,
        )(in_vmem(returned), in_hbm(base))


def solution(mesh):
    placed = (P(None, "lev", "lat", "lon"), P("lat"), P("lat"), P("lat", None, None))
    return jax.shard_map(
        per_device,
        mesh=mesh,
        in_specs=placed,
        out_specs=P(None, "lev", "lat", "lon"),
        check_vma=False,
    )
```

```python
import jax
import jax.numpy as jnp
from jax import lax
from jax.experimental import pallas as pl
from jax.experimental.pallas import tpu as pltpu
from jax.sharding import PartitionSpec as P

TIME_STEP = 0.5
VISCOSITY = 0.05
MERIDIONAL = 0.25
HALF = 128
SUBLANES = 8
VMEM_LIMIT = 32 * 1024 * 1024
GROUP = 8
LOADS = 4


def latitudes(global_rows, row_total):
    latitude_angle = -0.5 * jnp.pi + (global_rows + 0.5) * jnp.pi / row_total
    return (jnp.cos(latitude_angle), jnp.sin(latitude_angle))


def flip(tiles):
    row = lax.broadcasted_iota(jnp.int32, tiles[0].shape, 0)
    for d in (4, 2, 1):
        keep = (row & d) == 0
        turned = list(tiles)
        for i in range(SUBLANES):
            if not i & d:
                a, b = tiles[i], tiles[i + d]
                turned[i] = jnp.where(keep, a, pltpu.roll(b, d, 0))
                turned[i + d] = jnp.where(keep, pltpu.roll(a, SUBLANES - d, 0), b)
        tiles = turned
    return tiles


def fetch_kernel(prog, tile, first, last, sems):
    fields, levels, rows, _ = prog.shape
    per_load = levels // LOADS
    loads = []
    for f in range(fields):
        for load in range(LOADS):
            some = pl.ds(load * per_load, per_load)
            loads.append(pltpu.make_async_copy(prog.at[f, some], tile.at[f, some], sems.at[f, load]))
            loads[-1].start()
    for f in range(fields):
        for l in range(levels):
            if l % per_load == 0:
                loads[f * LOADS + l // per_load].wait()
            c = f * levels + l
            last[c : c + 1, :] = tile[f, l, rows - 1 : rows, :]
            first[c : c + 1, :] = tile[f, l, 0:1, :]


def tendency_kernel(tile, zonal, coriolis, out, ends, stage, sems):
    _, levels, rows, width = tile.shape
    chans = 3 * levels
    payload = 2 * chans
    row_id = lax.broadcasted_iota(jnp.int32, (SUBLANES, width), 0)
    col_id = lax.broadcasted_iota(jnp.int32, (SUBLANES, width), 1)
    lane_id = lax.broadcasted_iota(jnp.int32, (SUBLANES, HALF), 1)
    first_row, last_row = row_id == 0, row_id == SUBLANES - 1
    first_col, last_col = col_id == 0, col_id == width - 1
    copies = []
    for j0 in range(0, rows, SUBLANES):
        j1 = j0 + SUBLANES
        zon, cor = zonal[j0:j1, :], coriolis[j0:j1, :]
        edge_rows = jnp.zeros((SUBLANES, HALF), jnp.float32)
        for l0 in range(0, levels, SUBLANES):
            tends = [[], [], []]
            for l in range(l0, l0 + SUBLANES):
                centre, dx, dy, sx = [], [], [], []
                for f in range(3):
                    c = f * levels + l
                    here = tile[f, l, j0:j1, :]
                    after = tile[f, l, j1 : j1 + 1, :] if j1 < rows else 0.0
                    before = tile[f, l, j0 - 1 : j0, :] if j0 else 0.0
                    e = jnp.where(last_col, 0.0, pltpu.roll(here, width - 1, 1))
                    w = jnp.where(first_col, 0.0, pltpu.roll(here, 1, 1))
                    n = jnp.where(last_row, after, pltpu.roll(here, SUBLANES - 1, 0))
                    s = jnp.where(first_row, before, pltpu.roll(here, 1, 0))
                    centre.append(here)
                    dx.append(e - w)
                    dy.append(n - s)
                    sx.append(e + w + n + s - 4.0 * here)
                    first = here[:, :HALF]
                    last = here[:, width - HALF :]
                    if c:
                        first = pltpu.roll(first, c, 1)
                    last = pltpu.roll(last, (chans + c + 1) % HALF, 1)
                    edge_rows = jnp.where(lane_id == c, first, jnp.where(lane_id == chans + c, last, edge_rows))
                tends[0].append(-zon * dx[2] + cor * centre[1] + VISCOSITY * sx[0])
                tends[1].append(-MERIDIONAL * dy[2] - cor * centre[0] + VISCOSITY * sx[1])
                tends[2].append(-zon * dx[0] - MERIDIONAL * dy[1])
            for f in range(3):
                for half in range(2):
                    at = (2 * f + half) * levels + l0
                    flipped = flip([value[:, half * HALF : (half + 1) * HALF] for value in tends[f]])
                    for k, value in enumerate(flipped):
                        j = j0 + k
                        stage[j, at : at + SUBLANES, :] = value
                        if j in (0, rows - 1):
                            ends[min(j, 1), at : at + SUBLANES, :] = value
        for k in range(SUBLANES):
            stage[j0 + k, payload:, :] = jnp.broadcast_to(edge_rows[k : k + 1, :], (SUBLANES, HALF))
        some = pl.ds(j0, SUBLANES)
        copies.append(pltpu.make_async_copy(stage.at[some], out.at[some], sems.at[j0 // SUBLANES]))
        copies[-1].start()
    for copy in copies:
        copy.wait()


def seam_kernel(ends, north, south, tend, out, stage, sems):
    del tend
    chans = south.shape[0]
    levels = chans // 3
    copies = []
    for at, beyond, sign in ((0, south, -1.0), (1, north, 1.0)):
        for half in range(2):
            lanes = slice(half * HALF, (half + 1) * HALF)
            u, v, h = (beyond[f * levels : (f + 1) * levels, lanes] for f in range(3))
            slope = sign * MERIDIONAL
            for f, term in enumerate((VISCOSITY * u, VISCOSITY * v - slope * h, -slope * v)):
                some = slice((2 * f + half) * levels, (2 * f + half + 1) * levels)
                stage[at, some, :] = ends[at, some, :] + term
        row = at * (out.shape[0] - 1)
        copies.append(pltpu.make_async_copy(stage.at[at], out.at[row, pl.ds(0, 2 * chans)], sems.at[at]))
        copies[-1].start()
    for copy in copies:
        copy.wait()


def split2(x):
    hi = x.astype(jnp.bfloat16)
    return hi, (x - hi.astype(jnp.float32)).astype(jnp.bfloat16)


def mix_operand(matrix):
    hi, lo = split2(matrix)
    return jnp.concatenate([hi, hi, lo], axis=1)


def pair_mix_operand(matrix):
    hi, lo = split2(matrix)
    none = jnp.zeros_like(hi)
    return jnp.concatenate(
        [
            jnp.concatenate([hi, hi, none, none], axis=1),
            jnp.concatenate([none, none, hi, hi], axis=1),
            jnp.concatenate([lo, none, none, none], axis=1),
            jnp.concatenate([none, none, lo, none], axis=1),
        ],
        axis=0,
    )


def filter_kernel(
    own_row, half_width, filter_mask, zonal, tend, matrices, out, halves, parts, seam, matrix, stage, matrix_sem, sems
):
    lev_parts, blocks, levels = out.shape[0], out.shape[1], out.shape[4]
    chans = 3 * levels
    payload = 2 * chans
    count = 2 * blocks
    both = lev_parts * chans
    row = own_row[0]
    fetch = pltpu.make_async_copy(matrices.at[row], matrix, matrix_sem)
    fetch.start()
    reach = half_width[row]
    whole = reach == count // 2
    norm = jnp.where(whole, count * HALF, 2 * HALF * reach + 1).astype(jnp.float32)
    filtered = filter_mask[row] == 1
    edge_gain = jnp.where(whole, 0.0, 1.0).astype(jnp.float32)

    for b in range(blocks):
        for part in range(lev_parts):
            at = b * lev_parts + part
            seam[at : at + 1, :] = tend[part, b, payload : payload + 1, :]
    columns = seam[...].T
    zon = zonal[row]
    u, v, h = (columns[f * levels : (f + 1) * levels] for f in range(3))
    from_east = jnp.concatenate([VISCOSITY * u - zon * h, VISCOSITY * v, -zon * u], axis=0)
    u, v, h = (columns[chans + f * levels : chans + (f + 1) * levels] for f in range(3))
    from_west = jnp.concatenate([VISCOSITY * u + zon * h, VISCOSITY * v, zon * u], axis=0)
    lane_id = lax.broadcasted_iota(jnp.int32, (levels, HALF), 1)
    window = jnp.zeros((both, HALF), jnp.float32)
    for g in range(count):
        b, half = divmod(g, 2)
        beyond = (b + 1) % blocks if half else (b + blocks - 1) % blocks
        terms, lane = (from_east, HALF - 1) if half else (from_west, 0)
        pieces = []
        for part in range(lev_parts):
            source = beyond * lev_parts + part
            for f in range(3):
                here = tend[part, b, (2 * f + half) * levels : (2 * f + half + 1) * levels, :]
                term = terms[f * levels : (f + 1) * levels, source : source + 1]
                pieces.append(here + jnp.where(lane_id == lane, term, 0.0))
        value = jnp.concatenate(pieces, axis=0)
        halves[g] = value
        inside = lax.rem(g + reach, count) < 2 * reach
        window = window + jnp.where(inside, 1.0, 0.0).astype(jnp.float32) * value

    src = lax.broadcasted_iota(jnp.int32, (2 * HALF, 2 * HALF), 0)
    dst = lax.broadcasted_iota(jnp.int32, (2 * HALF, 2 * HALF), 1)
    sums = jnp.where((src & (HALF - 1)) <= dst, 1.0, 0.0).astype(jnp.bfloat16)
    fetch.wait()
    mixer = pair_mix_operand(matrix[...])
    scale = TIME_STEP / norm
    total = jnp.dot(
        jnp.concatenate(split2(window), axis=1), sums, preferred_element_type=jnp.float32
    )[:, HALF:]

    def split_group(g0):
        for g in range(g0, g0 + GROUP):
            ahead = halves[lax.rem(g + reach, count)]
            behind = halves[lax.rem(g + count - reach, count)]
            hi, lo = split2(ahead - behind)
            parts[g * both : (g + 1) * both, :HALF] = hi
            parts[g * both : (g + 1) * both, HALF:] = lo

    def emit(b, steps):
        for half, step in enumerate(steps):
            for p in range(lev_parts):
                stage[p, b, 2, half] = step[p * chans + 2 * levels : (p + 1) * chans]
        step = jnp.concatenate(steps, axis=1)
        winds = []
        for f in range(2):
            winds += split2(
                jnp.concatenate(
                    [step[p * chans + f * levels : p * chans + (f + 1) * levels] for p in range(lev_parts)],
                    axis=0,
                )
            )
        mixed = jnp.dot(mixer, jnp.concatenate(winds, axis=0), preferred_element_type=jnp.float32)
        mixed = mixed[: 2 * lev_parts * levels] + mixed[2 * lev_parts * levels :]
        for f in range(2):
            for p in range(lev_parts):
                at = (f * lev_parts + p) * levels
                for half in range(2):
                    stage[p, b, f, half] = mixed[at : at + levels, half * HALF : (half + 1) * HALF]
        copy = pltpu.make_async_copy(stage.at[:, b], out.at[:, b], sems.at[b])
        copy.start()
        return copy

    @pl.when(filtered)
    def _():
        copies = []
        running = total
        split_group(0)
        for g0 in range(0, count, GROUP):
            if g0 + GROUP < count:
                split_group(g0 + GROUP)
            box = jnp.dot(parts[g0 * both : (g0 + GROUP) * both, :], sums, preferred_element_type=jnp.float32)
            for b in range(g0 // 2, (g0 + GROUP) // 2):
                steps = []
                for g in (2 * b, 2 * b + 1):
                    at = (g - g0) * both
                    behind = halves[lax.rem(g + count - reach, count)]
                    steps.append((box[at : at + both, :HALF] + running + edge_gain * behind) * scale)
                    running = running + box[at : at + both, HALF:]
                copies.append(emit(b, steps))
        for copy in copies:
            copy.wait()

    @pl.when(jnp.logical_not(filtered))
    def _():
        copies = [emit(b, [TIME_STEP * halves[2 * b], TIME_STEP * halves[2 * b + 1]]) for b in range(blocks)]
        for copy in copies:
            copy.wait()


def base_kernel(own_part, own, other, matrix, out):
    _, levels, rows, width = own.shape
    lower = own_part[0] == 0

    def by_row(ref, f, j0):
        flipped = [
            flip([ref[f, l0 + i, j0 : j0 + SUBLANES, :] for i in range(SUBLANES)])
            for l0 in range(0, levels, SUBLANES)
        ]
        return [jnp.concatenate([part[k] for part in flipped], axis=0) for k in range(SUBLANES)]

    for j0 in range(0, rows, SUBLANES):
        mine = [by_row(own, f, j0) for f in range(3)]
        theirs = [by_row(other, f, j0) for f in range(2)]
        for k in range(SUBLANES):
            j = j0 + k
            winds = []
            for f in range(2):
                a, b = mine[f][k], theirs[f][k]
                winds.append(jnp.concatenate([jnp.where(lower, a, b), jnp.where(lower, b, a)], axis=0))
            wind_hi, wind_lo = split2(jnp.concatenate(winds, axis=1))
            mixed = jnp.dot(
                mix_operand(matrix[j]),
                jnp.concatenate([wind_hi, wind_lo, wind_hi], axis=0),
                preferred_element_type=jnp.float32,
            )
            kept = jnp.where(lower, mixed[:levels], mixed[levels:])
            for f in range(2):
                out[j, f, 0] = kept[:, f * width : (f + 1) * width]
            out[j, 2, 0] = mine[2][k]


def finish_kernel(step, base, out, added, stage, in_sems, out_sems):
    fields, levels, rows, _ = out.shape
    pieces = [(f, l0) for f in range(fields) for l0 in range(0, levels, SUBLANES)]
    loads, copies = {}, []
    for n, (f, l0) in enumerate(pieces):
        some = pl.ds(l0, SUBLANES)
        for half in range(2):
            loads[f, l0, half] = pltpu.make_async_copy(
                base.at[:, f, half, some], added.at[:, f, half, some], in_sems.at[2 * n + half]
            )
            loads[f, l0, half].start()
    for n, (f, l0) in enumerate(pieces):
        some = slice(l0, l0 + SUBLANES)
        for half in range(2):
            loads[f, l0, half].wait()
            for j0 in range(0, rows, SUBLANES):
                flipped = flip(
                    [step[j0 + k, f, half, some, :] + added[j0 + k, f, half, some, :] for k in range(SUBLANES)]
                )
                for i, value in enumerate(flipped):
                    stage[f, l0 + i, j0 : j0 + SUBLANES, half * HALF : (half + 1) * HALF] = value
        some = pl.ds(l0, SUBLANES)
        copies.append(pltpu.make_async_copy(stage.at[f, some], out.at[f, some], out_sems.at[n]))
        copies[-1].start()
    for copy in copies:
        copy.wait()


def per_device(prognostic, half_width, filter_mask, column_inverse):
    fields, levels, rows, width = prognostic.shape
    lon_devices, lat_devices, lev_devices = (lax.axis_size(a) for a in ("lon", "lat", "lev"))
    lon_index, lat_index, lev_index = (lax.axis_index(a) for a in ("lon", "lat", "lev"))
    chans = fields * levels
    halves = width // HALF
    params = pltpu.CompilerParams(vmem_limit_bytes=VMEM_LIMIT)
    hbm = pl.BlockSpec(memory_space=pltpu.HBM)
    vmem = pl.BlockSpec(memory_space=pltpu.VMEM)

    def in_hbm(x):
        return pltpu.with_memory_space_constraint(x, pltpu.HBM)

    def in_vmem(x):
        return pltpu.with_memory_space_constraint(x, pltpu.VMEM)


    with jax.named_scope("fetch"):
        tile, first, last = pl.pallas_call(
            fetch_kernel,
            out_shape=(
                pltpu.VMEM(prognostic.shape, jnp.float32),
                pltpu.VMEM((chans, width), jnp.float32),
                pltpu.VMEM((chans, width), jnp.float32),
            ),
            in_specs=[hbm],
            out_specs=(vmem, vmem, vmem),
            scratch_shapes=[pltpu.SemaphoreType.DMA((fields, LOADS))],
            compiler_params=params,
        )(in_hbm(prognostic))
    north = lax.ppermute(first, "lat", [(i + 1, i) for i in range(lat_devices - 1)])
    south = lax.ppermute(last, "lat", [(i, i + 1) for i in range(lat_devices - 1)])
    other = lax.ppermute(prognostic[:2], "lev", [(0, 1), (1, 0)])

    global_rows = (lat_index * rows + jnp.arange(rows)).astype(jnp.float32)
    cosine, sine = latitudes(global_rows, rows * lat_devices)
    zonal = 0.25 / (cosine + 0.05)
    zonal_field = jnp.broadcast_to(zonal[:, None], (rows, width))
    coriolis_field = jnp.broadcast_to((0.5 * sine)[:, None], (rows, width))

    sent_rows = halves * chans + SUBLANES
    with jax.named_scope("tendencies"):
        tend, ends = pl.pallas_call(
            tendency_kernel,
            out_shape=(
                pltpu.HBM((rows, sent_rows, HALF), jnp.float32),
                pltpu.VMEM((2, halves * chans, HALF), jnp.float32),
            ),
            in_specs=[vmem, vmem, vmem],
            out_specs=(hbm, vmem),
            scratch_shapes=[
                pltpu.VMEM((rows, sent_rows, HALF), jnp.float32),
                pltpu.SemaphoreType.DMA((rows // SUBLANES,)),
            ],
            compiler_params=params,
        )(in_vmem(tile), in_vmem(zonal_field), in_vmem(coriolis_field))

    with jax.named_scope("seam_rows"):
        tend = pl.pallas_call(
            seam_kernel,
            out_shape=pltpu.HBM(tend.shape, jnp.float32),
            in_specs=[vmem, vmem, vmem, hbm],
            out_specs=hbm,
            input_output_aliases={3: 0},
            scratch_shapes=[pltpu.VMEM(ends.shape, jnp.float32), pltpu.SemaphoreType.DMA((2,))],
            compiler_params=params,
        )(in_vmem(ends), in_vmem(north), in_vmem(south), in_hbm(tend))

    whole_rows = lax.all_to_all(tend, ("lev", "lon"), 0, 0, tiled=True)

    own_row = (lev_index * lon_devices + lon_index).astype(jnp.int32).reshape(1)
    stepped_shape = (lev_devices, lon_devices, fields, halves, levels, HALF)
    count = halves * lon_devices
    both = lev_devices * chans
    with jax.named_scope("row_filter"):
        stepped = pl.pallas_call(
            filter_kernel,
            out_shape=pltpu.HBM(stepped_shape, jnp.float32),
            grid_spec=pltpu.PrefetchScalarGridSpec(
                num_scalar_prefetch=4,
                grid=(1,),
                in_specs=[vmem, hbm],
                out_specs=hbm,
                scratch_shapes=[
                    pltpu.VMEM((count, both, HALF), jnp.float32),
                    pltpu.VMEM((count * both, 2 * HALF), jnp.bfloat16),
                    pltpu.VMEM((HALF, HALF), jnp.float32),
                    pltpu.VMEM(column_inverse.shape[1:], jnp.float32),
                    pltpu.VMEM(stepped_shape, jnp.float32),
                    pltpu.SemaphoreType.DMA,
                    pltpu.SemaphoreType.DMA((lon_devices,)),
                ],
            ),
            compiler_params=params,
        )(
            own_row,
            half_width,
            filter_mask,
            zonal,
            in_vmem(whole_rows.reshape(lev_devices, lon_devices, sent_rows, HALF)),
            in_hbm(column_inverse),
        )

    returned = lax.all_to_all(
        stepped.reshape((rows,) + stepped_shape[2:]), ("lev", "lon"), 0, 0, tiled=True
    )

    with jax.named_scope("base"):
        base = pl.pallas_call(
            base_kernel,
            out_shape=pltpu.HBM(returned.shape, jnp.float32),
            grid_spec=pltpu.PrefetchScalarGridSpec(
                num_scalar_prefetch=1,
                grid=(halves,),
                in_specs=[
                    pl.BlockSpec((fields, levels, rows, HALF), lambda i, *_: (0, 0, 0, i)),
                    pl.BlockSpec((2, levels, rows, HALF), lambda i, *_: (0, 0, 0, i)),
                    pl.BlockSpec(column_inverse.shape, lambda i, *_: (0, 0, 0)),
                ],
                out_specs=pl.BlockSpec((rows, fields, 1, levels, HALF), lambda i, *_: (0, 0, i, 0, 0)),
            ),
            compiler_params=params,
        )(lev_index.astype(jnp.int32).reshape(1), prognostic, other, column_inverse)

    with jax.named_scope("finish"):
        return pl.pallas_call(
            finish_kernel,
            out_shape=jax.ShapeDtypeStruct(prognostic.shape, jnp.float32),
            in_specs=[vmem, hbm],
            out_specs=hbm,
            scratch_shapes=[
                pltpu.VMEM(returned.shape, jnp.float32),
                pltpu.VMEM(prognostic.shape, jnp.float32),
                pltpu.SemaphoreType.DMA((fields * halves * levels // SUBLANES,)),
                pltpu.SemaphoreType.DMA((fields * levels // SUBLANES,)),
            ],
            compiler_params=params,
        )(in_vmem(returned), in_hbm(base))


def solution(mesh):
    placed = (P(None, "lev", "lat", "lon"), P("lat"), P("lat"), P("lat", None, None))
    return jax.shard_map(
        per_device,
        mesh=mesh,
        in_specs=placed,
        out_specs=P(None, "lev", "lat", "lon"),
        check_vma=False,
    )
```

```python
import jax
import jax.numpy as jnp
from jax import lax
from jax.experimental import pallas as pl
from jax.experimental.pallas import tpu as pltpu
from jax.sharding import PartitionSpec as P

TIME_STEP = 0.5
VISCOSITY = 0.05
MERIDIONAL = 0.25
HALF = 128
SUBLANES = 8
VMEM_LIMIT = 32 * 1024 * 1024
GROUP = 16
LOADS = 4


def latitudes(global_rows, row_total):
    latitude_angle = -0.5 * jnp.pi + (global_rows + 0.5) * jnp.pi / row_total
    return (jnp.cos(latitude_angle), jnp.sin(latitude_angle))


def flip(tiles):
    row = lax.broadcasted_iota(jnp.int32, tiles[0].shape, 0)
    for d in (4, 2, 1):
        keep = (row & d) == 0
        turned = list(tiles)
        for i in range(SUBLANES):
            if not i & d:
                a, b = tiles[i], tiles[i + d]
                turned[i] = jnp.where(keep, a, pltpu.roll(b, d, 0))
                turned[i + d] = jnp.where(keep, pltpu.roll(a, SUBLANES - d, 0), b)
        tiles = turned
    return tiles


def fetch_kernel(prog, tile, first, last, sems):
    fields, levels, rows, _ = prog.shape
    per_load = levels // LOADS
    loads = []
    for f in range(fields):
        for load in range(LOADS):
            some = pl.ds(load * per_load, per_load)
            loads.append(pltpu.make_async_copy(prog.at[f, some], tile.at[f, some], sems.at[f, load]))
            loads[-1].start()
    for f in range(fields):
        for l in range(levels):
            if l % per_load == 0:
                loads[f * LOADS + l // per_load].wait()
            c = f * levels + l
            last[c : c + 1, :] = tile[f, l, rows - 1 : rows, :]
            first[c : c + 1, :] = tile[f, l, 0:1, :]


def tendency_kernel(tile, zonal, coriolis, out, ends, stage, sems):
    _, levels, rows, width = tile.shape
    chans = 3 * levels
    payload = 2 * chans
    row_id = lax.broadcasted_iota(jnp.int32, (SUBLANES, width), 0)
    col_id = lax.broadcasted_iota(jnp.int32, (SUBLANES, width), 1)
    lane_id = lax.broadcasted_iota(jnp.int32, (SUBLANES, HALF), 1)
    first_row, last_row = row_id == 0, row_id == SUBLANES - 1
    first_col, last_col = col_id == 0, col_id == width - 1
    copies = []
    for j0 in range(0, rows, SUBLANES):
        j1 = j0 + SUBLANES
        zon, cor = zonal[j0:j1, :], coriolis[j0:j1, :]
        edge_rows = jnp.zeros((SUBLANES, HALF), jnp.float32)
        for l0 in range(0, levels, SUBLANES):
            tends = [[], [], []]
            for l in range(l0, l0 + SUBLANES):
                centre, dx, dy, sx = [], [], [], []
                for f in range(3):
                    c = f * levels + l
                    here = tile[f, l, j0:j1, :]
                    after = tile[f, l, j1 : j1 + 1, :] if j1 < rows else 0.0
                    before = tile[f, l, j0 - 1 : j0, :] if j0 else 0.0
                    e = jnp.where(last_col, 0.0, pltpu.roll(here, width - 1, 1))
                    w = jnp.where(first_col, 0.0, pltpu.roll(here, 1, 1))
                    n = jnp.where(last_row, after, pltpu.roll(here, SUBLANES - 1, 0))
                    s = jnp.where(first_row, before, pltpu.roll(here, 1, 0))
                    centre.append(here)
                    dx.append(e - w)
                    dy.append(n - s)
                    sx.append(e + w + n + s - 4.0 * here)
                    first = here[:, :HALF]
                    last = here[:, width - HALF :]
                    if c:
                        first = pltpu.roll(first, c, 1)
                    last = pltpu.roll(last, (chans + c + 1) % HALF, 1)
                    edge_rows = jnp.where(lane_id == c, first, jnp.where(lane_id == chans + c, last, edge_rows))
                tends[0].append(-zon * dx[2] + cor * centre[1] + VISCOSITY * sx[0])
                tends[1].append(-MERIDIONAL * dy[2] - cor * centre[0] + VISCOSITY * sx[1])
                tends[2].append(-zon * dx[0] - MERIDIONAL * dy[1])
            for f in range(3):
                for half in range(2):
                    at = (2 * f + half) * levels + l0
                    flipped = flip([value[:, half * HALF : (half + 1) * HALF] for value in tends[f]])
                    for k, value in enumerate(flipped):
                        j = j0 + k
                        stage[j, at : at + SUBLANES, :] = value
                        if j in (0, rows - 1):
                            ends[min(j, 1), at : at + SUBLANES, :] = value
        for k in range(SUBLANES):
            stage[j0 + k, payload:, :] = jnp.broadcast_to(edge_rows[k : k + 1, :], (SUBLANES, HALF))
        some = pl.ds(j0, SUBLANES)
        copies.append(pltpu.make_async_copy(stage.at[some], out.at[some], sems.at[j0 // SUBLANES]))
        copies[-1].start()
    for copy in copies:
        copy.wait()


def seam_kernel(ends, north, south, tend, out, stage, sems):
    del tend
    chans = south.shape[0]
    levels = chans // 3
    copies = []
    for at, beyond, sign in ((0, south, -1.0), (1, north, 1.0)):
        for half in range(2):
            lanes = slice(half * HALF, (half + 1) * HALF)
            u, v, h = (beyond[f * levels : (f + 1) * levels, lanes] for f in range(3))
            slope = sign * MERIDIONAL
            for f, term in enumerate((VISCOSITY * u, VISCOSITY * v - slope * h, -slope * v)):
                some = slice((2 * f + half) * levels, (2 * f + half + 1) * levels)
                stage[at, some, :] = ends[at, some, :] + term
        row = at * (out.shape[0] - 1)
        copies.append(pltpu.make_async_copy(stage.at[at], out.at[row, pl.ds(0, 2 * chans)], sems.at[at]))
        copies[-1].start()
    for copy in copies:
        copy.wait()


def split2(x):
    hi = x.astype(jnp.bfloat16)
    return hi, (x - hi.astype(jnp.float32)).astype(jnp.bfloat16)


def mix_operand(matrix):
    hi, lo = split2(matrix)
    return jnp.concatenate([hi, hi, lo], axis=1)


def pair_mix_operand(matrix):
    hi, lo = split2(matrix)
    none = jnp.zeros_like(hi)
    return jnp.concatenate(
        [
            jnp.concatenate([hi, hi, none, none], axis=1),
            jnp.concatenate([none, none, hi, hi], axis=1),
            jnp.concatenate([lo, none, none, none], axis=1),
            jnp.concatenate([none, none, lo, none], axis=1),
        ],
        axis=0,
    )


def filter_kernel(
    own_row, half_width, filter_mask, zonal, tend, matrices, out, halves, parts, seam, matrix, stage, matrix_sem, sems
):
    lev_parts, blocks, levels = out.shape[0], out.shape[1], out.shape[4]
    chans = 3 * levels
    payload = 2 * chans
    count = 2 * blocks
    both = lev_parts * chans
    row = own_row[0]
    fetch = pltpu.make_async_copy(matrices.at[row], matrix, matrix_sem)
    fetch.start()
    reach = half_width[row]
    whole = reach == count // 2
    norm = jnp.where(whole, count * HALF, 2 * HALF * reach + 1).astype(jnp.float32)
    filtered = filter_mask[row] == 1
    edge_gain = jnp.where(whole, 0.0, 1.0).astype(jnp.float32)

    for b in range(blocks):
        for part in range(lev_parts):
            at = b * lev_parts + part
            seam[at : at + 1, :] = tend[part, b, payload : payload + 1, :]
    columns = seam[...].T
    zon = zonal[row]
    u, v, h = (columns[f * levels : (f + 1) * levels] for f in range(3))
    from_east = jnp.concatenate([VISCOSITY * u - zon * h, VISCOSITY * v, -zon * u], axis=0)
    u, v, h = (columns[chans + f * levels : chans + (f + 1) * levels] for f in range(3))
    from_west = jnp.concatenate([VISCOSITY * u + zon * h, VISCOSITY * v, zon * u], axis=0)
    lane_id = lax.broadcasted_iota(jnp.int32, (levels, HALF), 1)
    window = jnp.zeros((both, HALF), jnp.float32)
    for g in range(count):
        b, half = divmod(g, 2)
        beyond = (b + 1) % blocks if half else (b + blocks - 1) % blocks
        terms, lane = (from_east, HALF - 1) if half else (from_west, 0)
        pieces = []
        for part in range(lev_parts):
            source = beyond * lev_parts + part
            for f in range(3):
                here = tend[part, b, (2 * f + half) * levels : (2 * f + half + 1) * levels, :]
                term = terms[f * levels : (f + 1) * levels, source : source + 1]
                pieces.append(here + jnp.where(lane_id == lane, term, 0.0))
        value = jnp.concatenate(pieces, axis=0)
        halves[g] = value
        inside = lax.rem(g + reach, count) < 2 * reach
        window = window + jnp.where(inside, 1.0, 0.0).astype(jnp.float32) * value

    src = lax.broadcasted_iota(jnp.int32, (2 * HALF, 2 * HALF), 0)
    dst = lax.broadcasted_iota(jnp.int32, (2 * HALF, 2 * HALF), 1)
    sums = jnp.where((src & (HALF - 1)) <= dst, 1.0, 0.0).astype(jnp.bfloat16)
    fetch.wait()
    mixer = pair_mix_operand(matrix[...])
    scale = TIME_STEP / norm
    total = jnp.dot(
        jnp.concatenate(split2(window), axis=1), sums, preferred_element_type=jnp.float32
    )[:, HALF:]

    def split_group(g0):
        for g in range(g0, g0 + GROUP):
            ahead = halves[lax.rem(g + reach, count)]
            behind = halves[lax.rem(g + count - reach, count)]
            hi, lo = split2(ahead - behind)
            parts[g * both : (g + 1) * both, :HALF] = hi
            parts[g * both : (g + 1) * both, HALF:] = lo

    def emit(b, steps):
        for half, step in enumerate(steps):
            for p in range(lev_parts):
                stage[p, b, 2, half] = step[p * chans + 2 * levels : (p + 1) * chans]
        step = jnp.concatenate(steps, axis=1)
        winds = []
        for f in range(2):
            winds += split2(
                jnp.concatenate(
                    [step[p * chans + f * levels : p * chans + (f + 1) * levels] for p in range(lev_parts)],
                    axis=0,
                )
            )
        mixed = jnp.dot(mixer, jnp.concatenate(winds, axis=0), preferred_element_type=jnp.float32)
        mixed = mixed[: 2 * lev_parts * levels] + mixed[2 * lev_parts * levels :]
        for f in range(2):
            for p in range(lev_parts):
                at = (f * lev_parts + p) * levels
                for half in range(2):
                    stage[p, b, f, half] = mixed[at : at + levels, half * HALF : (half + 1) * HALF]
        copy = pltpu.make_async_copy(stage.at[:, b], out.at[:, b], sems.at[b])
        copy.start()
        return copy

    @pl.when(filtered)
    def _():
        copies = []
        running = total
        split_group(0)
        for g0 in range(0, count, GROUP):
            if g0 + GROUP < count:
                split_group(g0 + GROUP)
            box = jnp.dot(parts[g0 * both : (g0 + GROUP) * both, :], sums, preferred_element_type=jnp.float32)
            for b in range(g0 // 2, (g0 + GROUP) // 2):
                steps = []
                for g in (2 * b, 2 * b + 1):
                    at = (g - g0) * both
                    behind = halves[lax.rem(g + count - reach, count)]
                    steps.append((box[at : at + both, :HALF] + running + edge_gain * behind) * scale)
                    running = running + box[at : at + both, HALF:]
                copies.append(emit(b, steps))
        for copy in copies:
            copy.wait()

    @pl.when(jnp.logical_not(filtered))
    def _():
        copies = [emit(b, [TIME_STEP * halves[2 * b], TIME_STEP * halves[2 * b + 1]]) for b in range(blocks)]
        for copy in copies:
            copy.wait()


def base_kernel(own_part, own, other, matrix, out):
    _, levels, rows, width = own.shape
    lower = own_part[0] == 0

    def by_row(ref, f, j0):
        flipped = [
            flip([ref[f, l0 + i, j0 : j0 + SUBLANES, :] for i in range(SUBLANES)])
            for l0 in range(0, levels, SUBLANES)
        ]
        return [jnp.concatenate([part[k] for part in flipped], axis=0) for k in range(SUBLANES)]

    for j0 in range(0, rows, SUBLANES):
        mine = [by_row(own, f, j0) for f in range(3)]
        theirs = [by_row(other, f, j0) for f in range(2)]
        for k in range(SUBLANES):
            j = j0 + k
            winds = []
            for f in range(2):
                a, b = mine[f][k], theirs[f][k]
                winds.append(jnp.concatenate([jnp.where(lower, a, b), jnp.where(lower, b, a)], axis=0))
            wind_hi, wind_lo = split2(jnp.concatenate(winds, axis=1))
            mixed = jnp.dot(
                mix_operand(matrix[j]),
                jnp.concatenate([wind_hi, wind_lo, wind_hi], axis=0),
                preferred_element_type=jnp.float32,
            )
            kept = jnp.where(lower, mixed[:levels], mixed[levels:])
            for f in range(2):
                out[j, f, 0] = kept[:, f * width : (f + 1) * width]
            out[j, 2, 0] = mine[2][k]


def finish_kernel(step, base, out, added, stage, in_sems, out_sems):
    fields, levels, rows, _ = out.shape
    blocks = levels // SUBLANES
    loads, copies = [], []
    for f in range(fields):
        for n in range(blocks):
            some = pl.ds(n * SUBLANES, SUBLANES)
            loads.append(
                pltpu.make_async_copy(base.at[:, f, :, some], added.at[:, f, :, some], in_sems.at[f * blocks + n])
            )
            loads[-1].start()
    for f in range(fields):
        for n in range(blocks):
            loads[f * blocks + n].wait()
            l0 = n * SUBLANES
            some = slice(l0, l0 + SUBLANES)
            for half in range(2):
                for j0 in range(0, rows, SUBLANES):
                    flipped = flip(
                        [step[j0 + k, f, half, some, :] + added[j0 + k, f, half, some, :] for k in range(SUBLANES)]
                    )
                    for i, value in enumerate(flipped):
                        stage[f, l0 + i, j0 : j0 + SUBLANES, half * HALF : (half + 1) * HALF] = value
            some = pl.ds(l0, SUBLANES)
            copies.append(
                pltpu.make_async_copy(stage.at[f, some], out.at[f, some], out_sems.at[f * blocks + n])
            )
            copies[-1].start()
    for copy in copies:
        copy.wait()


def per_device(prognostic, half_width, filter_mask, column_inverse):
    fields, levels, rows, width = prognostic.shape
    lon_devices, lat_devices, lev_devices = (lax.axis_size(a) for a in ("lon", "lat", "lev"))
    lon_index, lat_index, lev_index = (lax.axis_index(a) for a in ("lon", "lat", "lev"))
    chans = fields * levels
    halves = width // HALF
    params = pltpu.CompilerParams(vmem_limit_bytes=VMEM_LIMIT)
    hbm = pl.BlockSpec(memory_space=pltpu.HBM)
    vmem = pl.BlockSpec(memory_space=pltpu.VMEM)

    def in_hbm(x):
        return pltpu.with_memory_space_constraint(x, pltpu.HBM)

    def in_vmem(x):
        return pltpu.with_memory_space_constraint(x, pltpu.VMEM)


    with jax.named_scope("fetch"):
        tile, first, last = pl.pallas_call(
            fetch_kernel,
            out_shape=(
                pltpu.VMEM(prognostic.shape, jnp.float32),
                pltpu.VMEM((chans, width), jnp.float32),
                pltpu.VMEM((chans, width), jnp.float32),
            ),
            in_specs=[hbm],
            out_specs=(vmem, vmem, vmem),
            scratch_shapes=[pltpu.SemaphoreType.DMA((fields, LOADS))],
            compiler_params=params,
        )(in_hbm(prognostic))
    north = lax.ppermute(first, "lat", [(i + 1, i) for i in range(lat_devices - 1)])
    south = lax.ppermute(last, "lat", [(i, i + 1) for i in range(lat_devices - 1)])
    other = lax.ppermute(prognostic[:2], "lev", [(0, 1), (1, 0)])

    global_rows = (lat_index * rows + jnp.arange(rows)).astype(jnp.float32)
    cosine, sine = latitudes(global_rows, rows * lat_devices)
    zonal = 0.25 / (cosine + 0.05)
    zonal_field = jnp.broadcast_to(zonal[:, None], (rows, width))
    coriolis_field = jnp.broadcast_to((0.5 * sine)[:, None], (rows, width))

    sent_rows = halves * chans + SUBLANES
    with jax.named_scope("tendencies"):
        tend, ends = pl.pallas_call(
            tendency_kernel,
            out_shape=(
                pltpu.HBM((rows, sent_rows, HALF), jnp.float32),
                pltpu.VMEM((2, halves * chans, HALF), jnp.float32),
            ),
            in_specs=[vmem, vmem, vmem],
            out_specs=(hbm, vmem),
            scratch_shapes=[
                pltpu.VMEM((rows, sent_rows, HALF), jnp.float32),
                pltpu.SemaphoreType.DMA((rows // SUBLANES,)),
            ],
            compiler_params=params,
        )(in_vmem(tile), in_vmem(zonal_field), in_vmem(coriolis_field))

    with jax.named_scope("seam_rows"):
        tend = pl.pallas_call(
            seam_kernel,
            out_shape=pltpu.HBM(tend.shape, jnp.float32),
            in_specs=[vmem, vmem, vmem, hbm],
            out_specs=hbm,
            input_output_aliases={3: 0},
            scratch_shapes=[pltpu.VMEM(ends.shape, jnp.float32), pltpu.SemaphoreType.DMA((2,))],
            compiler_params=params,
        )(in_vmem(ends), in_vmem(north), in_vmem(south), in_hbm(tend))

    whole_rows = lax.all_to_all(tend, ("lev", "lon"), 0, 0, tiled=True)

    own_row = (lev_index * lon_devices + lon_index).astype(jnp.int32).reshape(1)
    stepped_shape = (lev_devices, lon_devices, fields, halves, levels, HALF)
    count = halves * lon_devices
    both = lev_devices * chans
    with jax.named_scope("row_filter"):
        stepped = pl.pallas_call(
            filter_kernel,
            out_shape=pltpu.HBM(stepped_shape, jnp.float32),
            grid_spec=pltpu.PrefetchScalarGridSpec(
                num_scalar_prefetch=4,
                grid=(1,),
                in_specs=[vmem, hbm],
                out_specs=hbm,
                scratch_shapes=[
                    pltpu.VMEM((count, both, HALF), jnp.float32),
                    pltpu.VMEM((count * both, 2 * HALF), jnp.bfloat16),
                    pltpu.VMEM((HALF, HALF), jnp.float32),
                    pltpu.VMEM(column_inverse.shape[1:], jnp.float32),
                    pltpu.VMEM(stepped_shape, jnp.float32),
                    pltpu.SemaphoreType.DMA,
                    pltpu.SemaphoreType.DMA((lon_devices,)),
                ],
            ),
            compiler_params=params,
        )(
            own_row,
            half_width,
            filter_mask,
            zonal,
            in_vmem(whole_rows.reshape(lev_devices, lon_devices, sent_rows, HALF)),
            in_hbm(column_inverse),
        )

    returned = lax.all_to_all(
        stepped.reshape((rows,) + stepped_shape[2:]), ("lev", "lon"), 0, 0, tiled=True
    )

    with jax.named_scope("base"):
        base = pl.pallas_call(
            base_kernel,
            out_shape=pltpu.HBM(returned.shape, jnp.float32),
            grid_spec=pltpu.PrefetchScalarGridSpec(
                num_scalar_prefetch=1,
                grid=(halves,),
                in_specs=[
                    pl.BlockSpec((fields, levels, rows, HALF), lambda i, *_: (0, 0, 0, i)),
                    pl.BlockSpec((2, levels, rows, HALF), lambda i, *_: (0, 0, 0, i)),
                    pl.BlockSpec(column_inverse.shape, lambda i, *_: (0, 0, 0)),
                ],
                out_specs=pl.BlockSpec((rows, fields, 1, levels, HALF), lambda i, *_: (0, 0, i, 0, 0)),
            ),
            compiler_params=params,
        )(lev_index.astype(jnp.int32).reshape(1), prognostic, other, column_inverse)

    with jax.named_scope("finish"):
        return pl.pallas_call(
            finish_kernel,
            out_shape=jax.ShapeDtypeStruct(prognostic.shape, jnp.float32),
            in_specs=[vmem, hbm],
            out_specs=hbm,
            scratch_shapes=[
                pltpu.VMEM(returned.shape, jnp.float32),
                pltpu.VMEM(prognostic.shape, jnp.float32),
                pltpu.SemaphoreType.DMA((fields * levels // SUBLANES,)),
                pltpu.SemaphoreType.DMA((fields * levels // SUBLANES,)),
            ],
            compiler_params=params,
        )(in_vmem(returned), in_hbm(base))


def solution(mesh):
    placed = (P(None, "lev", "lat", "lon"), P("lat"), P("lat"), P("lat", None, None))
    return jax.shard_map(
        per_device,
        mesh=mesh,
        in_specs=placed,
        out_specs=P(None, "lev", "lat", "lon"),
        check_vma=False,
    )
```

```python
import jax
import jax.numpy as jnp
import numpy as np
from jax import lax
from jax.experimental import pallas as pl
from jax.experimental.pallas import tpu as pltpu
from jax.sharding import PartitionSpec as P

TIME_STEP = 0.5
VISCOSITY = 0.05
MERIDIONAL = 0.25
HALF = 128
SUBLANES = 8
VMEM_LIMIT = 32 * 1024 * 1024
GROUP = 8
LOADS = 4


def latitudes(global_rows, row_total):
    latitude_angle = -0.5 * jnp.pi + (global_rows + 0.5) * jnp.pi / row_total
    return (jnp.cos(latitude_angle), jnp.sin(latitude_angle))


def row_factors(row_total):
    angle = -0.5 * np.pi + (np.arange(row_total) + 0.5) * np.pi / row_total
    both = np.stack([0.25 / (np.cos(angle) + 0.05), 0.5 * np.sin(angle)], axis=1).astype(np.float32)
    return np.repeat(both, HALF, axis=1)


def flip(tiles):
    row = lax.broadcasted_iota(jnp.int32, tiles[0].shape, 0)
    for d in (4, 2, 1):
        keep = (row & d) == 0
        turned = list(tiles)
        for i in range(SUBLANES):
            if not i & d:
                a, b = tiles[i], tiles[i + d]
                turned[i] = jnp.where(keep, a, pltpu.roll(b, d, 0))
                turned[i + d] = jnp.where(keep, pltpu.roll(a, SUBLANES - d, 0), b)
        tiles = turned
    return tiles


def fetch_kernel(prog, table, tile, first, last, factors, sems, table_sem):
    fields, levels, rows, _ = prog.shape
    per_load = levels // LOADS
    own = pl.ds(pl.multiple_of(lax.axis_index("lat") * rows, rows), rows)
    extra = pltpu.make_async_copy(table.at[own], factors, table_sem)
    extra.start()
    loads = []
    for f in range(fields):
        for load in range(LOADS):
            some = pl.ds(load * per_load, per_load)
            loads.append(pltpu.make_async_copy(prog.at[f, some], tile.at[f, some], sems.at[f, load]))
            loads[-1].start()
    for f in range(fields):
        for l in range(levels):
            if l % per_load == 0:
                loads[f * LOADS + l // per_load].wait()
            c = f * levels + l
            last[c : c + 1, :] = tile[f, l, rows - 1 : rows, :]
            first[c : c + 1, :] = tile[f, l, 0:1, :]
    extra.wait()


def tendency_kernel(tile, factors, out, ends, stage, sems):
    _, levels, rows, width = tile.shape
    chans = 3 * levels
    payload = 2 * chans
    row_id = lax.broadcasted_iota(jnp.int32, (SUBLANES, width), 0)
    col_id = lax.broadcasted_iota(jnp.int32, (SUBLANES, width), 1)
    lane_id = lax.broadcasted_iota(jnp.int32, (SUBLANES, HALF), 1)
    first_row, last_row = row_id == 0, row_id == SUBLANES - 1
    first_col, last_col = col_id == 0, col_id == width - 1
    copies = []
    for j0 in range(0, rows, SUBLANES):
        j1 = j0 + SUBLANES
        zon, cor = (
            jnp.concatenate([factors[j0:j1, at : at + HALF]] * 2, axis=1) for at in (0, HALF)
        )
        edge_rows = jnp.zeros((SUBLANES, HALF), jnp.float32)
        for l0 in range(0, levels, SUBLANES):
            tends = [[], [], []]
            for l in range(l0, l0 + SUBLANES):
                centre, dx, dy, sx = [], [], [], []
                for f in range(3):
                    c = f * levels + l
                    here = tile[f, l, j0:j1, :]
                    after = tile[f, l, j1 : j1 + 1, :] if j1 < rows else 0.0
                    before = tile[f, l, j0 - 1 : j0, :] if j0 else 0.0
                    e = jnp.where(last_col, 0.0, pltpu.roll(here, width - 1, 1))
                    w = jnp.where(first_col, 0.0, pltpu.roll(here, 1, 1))
                    n = jnp.where(last_row, after, pltpu.roll(here, SUBLANES - 1, 0))
                    s = jnp.where(first_row, before, pltpu.roll(here, 1, 0))
                    centre.append(here)
                    dx.append(e - w)
                    dy.append(n - s)
                    sx.append(e + w + n + s - 4.0 * here)
                    first = here[:, :HALF]
                    last = here[:, width - HALF :]
                    if c:
                        first = pltpu.roll(first, c, 1)
                    last = pltpu.roll(last, (chans + c + 1) % HALF, 1)
                    edge_rows = jnp.where(lane_id == c, first, jnp.where(lane_id == chans + c, last, edge_rows))
                tends[0].append(-zon * dx[2] + cor * centre[1] + VISCOSITY * sx[0])
                tends[1].append(-MERIDIONAL * dy[2] - cor * centre[0] + VISCOSITY * sx[1])
                tends[2].append(-zon * dx[0] - MERIDIONAL * dy[1])
            for f in range(3):
                for half in range(2):
                    at = (2 * f + half) * levels + l0
                    flipped = flip([value[:, half * HALF : (half + 1) * HALF] for value in tends[f]])
                    for k, value in enumerate(flipped):
                        j = j0 + k
                        stage[j, at : at + SUBLANES, :] = value
                        if j in (0, rows - 1):
                            ends[min(j, 1), at : at + SUBLANES, :] = value
        for k in range(SUBLANES):
            stage[j0 + k, payload:, :] = jnp.broadcast_to(edge_rows[k : k + 1, :], (SUBLANES, HALF))
        some = pl.ds(j0, SUBLANES)
        copies.append(pltpu.make_async_copy(stage.at[some], out.at[some], sems.at[j0 // SUBLANES]))
        copies[-1].start()
    for copy in copies:
        copy.wait()


def seam_kernel(ends, north, south, tend, out, stage, sems):
    del tend
    chans = south.shape[0]
    levels = chans // 3
    copies = []
    for at, beyond, sign in ((0, south, -1.0), (1, north, 1.0)):
        for half in range(2):
            lanes = slice(half * HALF, (half + 1) * HALF)
            u, v, h = (beyond[f * levels : (f + 1) * levels, lanes] for f in range(3))
            slope = sign * MERIDIONAL
            for f, term in enumerate((VISCOSITY * u, VISCOSITY * v - slope * h, -slope * v)):
                some = slice((2 * f + half) * levels, (2 * f + half + 1) * levels)
                stage[at, some, :] = ends[at, some, :] + term
        row = at * (out.shape[0] - 1)
        copies.append(pltpu.make_async_copy(stage.at[at], out.at[row, pl.ds(0, 2 * chans)], sems.at[at]))
        copies[-1].start()
    for copy in copies:
        copy.wait()


def split2(x):
    hi = x.astype(jnp.bfloat16)
    return hi, (x - hi.astype(jnp.float32)).astype(jnp.bfloat16)


def mix_operand(matrix):
    hi, lo = split2(matrix)
    return jnp.concatenate([hi, hi, lo], axis=1)


def pair_mix_operand(matrix):
    hi, lo = split2(matrix)
    none = jnp.zeros_like(hi)
    return jnp.concatenate(
        [
            jnp.concatenate([hi, hi, none, none], axis=1),
            jnp.concatenate([none, none, hi, hi], axis=1),
            jnp.concatenate([lo, none, none, none], axis=1),
            jnp.concatenate([none, none, lo, none], axis=1),
        ],
        axis=0,
    )


def filter_kernel(
    own_row, half_width, filter_mask, zonal, tend, matrices, out, halves, parts, seam, matrix, stage, matrix_sem, sems
):
    lev_parts, blocks, levels = out.shape[0], out.shape[1], out.shape[4]
    chans = 3 * levels
    payload = 2 * chans
    count = 2 * blocks
    both = lev_parts * chans
    row = own_row[0]
    fetch = pltpu.make_async_copy(matrices.at[row], matrix, matrix_sem)
    fetch.start()
    reach = half_width[row]
    whole = reach == count // 2
    norm = jnp.where(whole, count * HALF, 2 * HALF * reach + 1).astype(jnp.float32)
    filtered = filter_mask[row] == 1
    edge_gain = jnp.where(whole, 0.0, 1.0).astype(jnp.float32)

    for b in range(blocks):
        for part in range(lev_parts):
            at = b * lev_parts + part
            seam[at : at + 1, :] = tend[part, b, payload : payload + 1, :]
    columns = seam[...].T
    zon = zonal[row]
    u, v, h = (columns[f * levels : (f + 1) * levels] for f in range(3))
    from_east = jnp.concatenate([VISCOSITY * u - zon * h, VISCOSITY * v, -zon * u], axis=0)
    u, v, h = (columns[chans + f * levels : chans + (f + 1) * levels] for f in range(3))
    from_west = jnp.concatenate([VISCOSITY * u + zon * h, VISCOSITY * v, zon * u], axis=0)
    lane_id = lax.broadcasted_iota(jnp.int32, (levels, HALF), 1)
    window = jnp.zeros((both, HALF), jnp.float32)
    for g in range(count):
        b, half = divmod(g, 2)
        beyond = (b + 1) % blocks if half else (b + blocks - 1) % blocks
        terms, lane = (from_east, HALF - 1) if half else (from_west, 0)
        pieces = []
        for part in range(lev_parts):
            source = beyond * lev_parts + part
            for f in range(3):
                here = tend[part, b, (2 * f + half) * levels : (2 * f + half + 1) * levels, :]
                term = terms[f * levels : (f + 1) * levels, source : source + 1]
                pieces.append(here + jnp.where(lane_id == lane, term, 0.0))
        value = jnp.concatenate(pieces, axis=0)
        halves[g] = value
        inside = lax.rem(g + reach, count) < 2 * reach
        window = window + jnp.where(inside, 1.0, 0.0).astype(jnp.float32) * value

    src = lax.broadcasted_iota(jnp.int32, (2 * HALF, 2 * HALF), 0)
    dst = lax.broadcasted_iota(jnp.int32, (2 * HALF, 2 * HALF), 1)
    sums = jnp.where((src & (HALF - 1)) <= dst, 1.0, 0.0).astype(jnp.bfloat16)
    fetch.wait()
    mixer = pair_mix_operand(matrix[...])
    scale = TIME_STEP / norm
    total = jnp.dot(
        jnp.concatenate(split2(window), axis=1), sums, preferred_element_type=jnp.float32
    )[:, HALF:]

    def split_group(g0):
        for g in range(g0, g0 + GROUP):
            ahead = halves[lax.rem(g + reach, count)]
            behind = halves[lax.rem(g + count - reach, count)]
            hi, lo = split2(ahead - behind)
            parts[g * both : (g + 1) * both, :HALF] = hi
            parts[g * both : (g + 1) * both, HALF:] = lo

    def emit(b, steps):
        for half, step in enumerate(steps):
            for p in range(lev_parts):
                stage[p, b, 2, half] = step[p * chans + 2 * levels : (p + 1) * chans]
        step = jnp.concatenate(steps, axis=1)
        winds = []
        for f in range(2):
            winds += split2(
                jnp.concatenate(
                    [step[p * chans + f * levels : p * chans + (f + 1) * levels] for p in range(lev_parts)],
                    axis=0,
                )
            )
        mixed = jnp.dot(mixer, jnp.concatenate(winds, axis=0), preferred_element_type=jnp.float32)
        mixed = mixed[: 2 * lev_parts * levels] + mixed[2 * lev_parts * levels :]
        for f in range(2):
            for p in range(lev_parts):
                at = (f * lev_parts + p) * levels
                for half in range(2):
                    stage[p, b, f, half] = mixed[at : at + levels, half * HALF : (half + 1) * HALF]
        copy = pltpu.make_async_copy(stage.at[:, b], out.at[:, b], sems.at[b])
        copy.start()
        return copy

    @pl.when(filtered)
    def _():
        copies = []
        running = total
        split_group(0)
        for g0 in range(0, count, GROUP):
            if g0 + GROUP < count:
                split_group(g0 + GROUP)
            box = jnp.dot(parts[g0 * both : (g0 + GROUP) * both, :], sums, preferred_element_type=jnp.float32)
            for b in range(g0 // 2, (g0 + GROUP) // 2):
                steps = []
                for g in (2 * b, 2 * b + 1):
                    at = (g - g0) * both
                    behind = halves[lax.rem(g + count - reach, count)]
                    steps.append((box[at : at + both, :HALF] + running + edge_gain * behind) * scale)
                    running = running + box[at : at + both, HALF:]
                copies.append(emit(b, steps))
        for copy in copies:
            copy.wait()

    @pl.when(jnp.logical_not(filtered))
    def _():
        copies = [emit(b, [TIME_STEP * halves[2 * b], TIME_STEP * halves[2 * b + 1]]) for b in range(blocks)]
        for copy in copies:
            copy.wait()


def base_kernel(own_part, own, other, matrix, out):
    _, levels, rows, width = own.shape
    lower = own_part[0] == 0

    def by_row(ref, f, j0):
        flipped = [
            flip([ref[f, l0 + i, j0 : j0 + SUBLANES, :] for i in range(SUBLANES)])
            for l0 in range(0, levels, SUBLANES)
        ]
        return [jnp.concatenate([part[k] for part in flipped], axis=0) for k in range(SUBLANES)]

    for j0 in range(0, rows, SUBLANES):
        mine = [by_row(own, f, j0) for f in range(3)]
        theirs = [by_row(other, f, j0) for f in range(2)]
        for k in range(SUBLANES):
            j = j0 + k
            winds = []
            for f in range(2):
                a, b = mine[f][k], theirs[f][k]
                winds.append(jnp.concatenate([jnp.where(lower, a, b), jnp.where(lower, b, a)], axis=0))
            wind_hi, wind_lo = split2(jnp.concatenate(winds, axis=1))
            mixed = jnp.dot(
                mix_operand(matrix[j]),
                jnp.concatenate([wind_hi, wind_lo, wind_hi], axis=0),
                preferred_element_type=jnp.float32,
            )
            kept = jnp.where(lower, mixed[:levels], mixed[levels:])
            for f in range(2):
                out[j, f, 0] = kept[:, f * width : (f + 1) * width]
            out[j, 2, 0] = mine[2][k]


def finish_kernel(step, base, out, added, stage, in_sems, out_sems):
    fields, levels, rows, _ = out.shape
    blocks = levels // SUBLANES
    loads, copies = [], []
    for f in range(fields):
        for n in range(blocks):
            some = pl.ds(n * SUBLANES, SUBLANES)
            loads.append(
                pltpu.make_async_copy(base.at[:, f, :, some], added.at[:, f, :, some], in_sems.at[f * blocks + n])
            )
            loads[-1].start()
    for f in range(fields):
        for n in range(blocks):
            loads[f * blocks + n].wait()
            l0 = n * SUBLANES
            some = slice(l0, l0 + SUBLANES)
            for half in range(2):
                for j0 in range(0, rows, SUBLANES):
                    flipped = flip(
                        [step[j0 + k, f, half, some, :] + added[j0 + k, f, half, some, :] for k in range(SUBLANES)]
                    )
                    for i, value in enumerate(flipped):
                        stage[f, l0 + i, j0 : j0 + SUBLANES, half * HALF : (half + 1) * HALF] = value
            some = pl.ds(l0, SUBLANES)
            copies.append(
                pltpu.make_async_copy(stage.at[f, some], out.at[f, some], out_sems.at[f * blocks + n])
            )
            copies[-1].start()
    for copy in copies:
        copy.wait()


def per_device(prognostic, half_width, filter_mask, column_inverse):
    fields, levels, rows, width = prognostic.shape
    lon_devices, lat_devices, lev_devices = (lax.axis_size(a) for a in ("lon", "lat", "lev"))
    lon_index, lat_index, lev_index = (lax.axis_index(a) for a in ("lon", "lat", "lev"))
    chans = fields * levels
    halves = width // HALF
    params = pltpu.CompilerParams(vmem_limit_bytes=VMEM_LIMIT)
    hbm = pl.BlockSpec(memory_space=pltpu.HBM)
    vmem = pl.BlockSpec(memory_space=pltpu.VMEM)

    def in_hbm(x):
        return pltpu.with_memory_space_constraint(x, pltpu.HBM)

    def in_vmem(x):
        return pltpu.with_memory_space_constraint(x, pltpu.VMEM)


    with jax.named_scope("fetch"):
        tile, first, last, factors = pl.pallas_call(
            fetch_kernel,
            out_shape=(
                pltpu.VMEM(prognostic.shape, jnp.float32),
                pltpu.VMEM((chans, width), jnp.float32),
                pltpu.VMEM((chans, width), jnp.float32),
                pltpu.VMEM((rows, 2 * HALF), jnp.float32),
            ),
            in_specs=[hbm, hbm],
            out_specs=(vmem,) * 4,
            scratch_shapes=[pltpu.SemaphoreType.DMA((fields, LOADS)), pltpu.SemaphoreType.DMA],
            compiler_params=params,
        )(in_hbm(prognostic), in_hbm(jnp.asarray(row_factors(rows * lat_devices))))
    north = lax.ppermute(first, "lat", [(i + 1, i) for i in range(lat_devices - 1)])
    south = lax.ppermute(last, "lat", [(i, i + 1) for i in range(lat_devices - 1)])
    other = lax.ppermute(prognostic[:2], "lev", [(0, 1), (1, 0)])

    global_rows = (lat_index * rows + jnp.arange(rows)).astype(jnp.float32)
    cosine, _ = latitudes(global_rows, rows * lat_devices)
    zonal = 0.25 / (cosine + 0.05)

    sent_rows = halves * chans + SUBLANES
    with jax.named_scope("tendencies"):
        tend, ends = pl.pallas_call(
            tendency_kernel,
            out_shape=(
                pltpu.HBM((rows, sent_rows, HALF), jnp.float32),
                pltpu.VMEM((2, halves * chans, HALF), jnp.float32),
            ),
            in_specs=[vmem, vmem],
            out_specs=(hbm, vmem),
            scratch_shapes=[
                pltpu.VMEM((rows, sent_rows, HALF), jnp.float32),
                pltpu.SemaphoreType.DMA((rows // SUBLANES,)),
            ],
            compiler_params=params,
        )(in_vmem(tile), in_vmem(factors))

    with jax.named_scope("seam_rows"):
        tend = pl.pallas_call(
            seam_kernel,
            out_shape=pltpu.HBM(tend.shape, jnp.float32),
            in_specs=[vmem, vmem, vmem, hbm],
            out_specs=hbm,
            input_output_aliases={3: 0},
            scratch_shapes=[pltpu.VMEM(ends.shape, jnp.float32), pltpu.SemaphoreType.DMA((2,))],
            compiler_params=params,
        )(in_vmem(ends), in_vmem(north), in_vmem(south), in_hbm(tend))

    whole_rows = lax.all_to_all(tend, ("lev", "lon"), 0, 0, tiled=True)

    own_row = (lev_index * lon_devices + lon_index).astype(jnp.int32).reshape(1)
    stepped_shape = (lev_devices, lon_devices, fields, halves, levels, HALF)
    count = halves * lon_devices
    both = lev_devices * chans
    with jax.named_scope("row_filter"):
        stepped = pl.pallas_call(
            filter_kernel,
            out_shape=pltpu.HBM(stepped_shape, jnp.float32),
            grid_spec=pltpu.PrefetchScalarGridSpec(
                num_scalar_prefetch=4,
                grid=(1,),
                in_specs=[vmem, hbm],
                out_specs=hbm,
                scratch_shapes=[
                    pltpu.VMEM((count, both, HALF), jnp.float32),
                    pltpu.VMEM((count * both, 2 * HALF), jnp.bfloat16),
                    pltpu.VMEM((HALF, HALF), jnp.float32),
                    pltpu.VMEM(column_inverse.shape[1:], jnp.float32),
                    pltpu.VMEM(stepped_shape, jnp.float32),
                    pltpu.SemaphoreType.DMA,
                    pltpu.SemaphoreType.DMA((lon_devices,)),
                ],
            ),
            compiler_params=params,
        )(
            own_row,
            half_width,
            filter_mask,
            zonal,
            in_vmem(whole_rows.reshape(lev_devices, lon_devices, sent_rows, HALF)),
            in_hbm(column_inverse),
        )

    returned = lax.all_to_all(
        stepped.reshape((rows,) + stepped_shape[2:]), ("lev", "lon"), 0, 0, tiled=True
    )

    with jax.named_scope("base"):
        base = pl.pallas_call(
            base_kernel,
            out_shape=pltpu.HBM(returned.shape, jnp.float32),
            grid_spec=pltpu.PrefetchScalarGridSpec(
                num_scalar_prefetch=1,
                grid=(halves,),
                in_specs=[
                    pl.BlockSpec((fields, levels, rows, HALF), lambda i, *_: (0, 0, 0, i)),
                    pl.BlockSpec((2, levels, rows, HALF), lambda i, *_: (0, 0, 0, i)),
                    pl.BlockSpec(column_inverse.shape, lambda i, *_: (0, 0, 0)),
                ],
                out_specs=pl.BlockSpec((rows, fields, 1, levels, HALF), lambda i, *_: (0, 0, i, 0, 0)),
            ),
            compiler_params=params,
        )(lev_index.astype(jnp.int32).reshape(1), prognostic, other, column_inverse)

    with jax.named_scope("finish"):
        return pl.pallas_call(
            finish_kernel,
            out_shape=jax.ShapeDtypeStruct(prognostic.shape, jnp.float32),
            in_specs=[vmem, hbm],
            out_specs=hbm,
            scratch_shapes=[
                pltpu.VMEM(returned.shape, jnp.float32),
                pltpu.VMEM(prognostic.shape, jnp.float32),
                pltpu.SemaphoreType.DMA((fields * levels // SUBLANES,)),
                pltpu.SemaphoreType.DMA((fields * levels // SUBLANES,)),
            ],
            compiler_params=params,
        )(in_vmem(returned), in_hbm(base))


def solution(mesh):
    placed = (P(None, "lev", "lat", "lon"), P("lat"), P("lat"), P("lat", None, None))
    return jax.shard_map(
        per_device,
        mesh=mesh,
        in_specs=placed,
        out_specs=P(None, "lev", "lat", "lon"),
        check_vma=False,
    )
```

```python
import jax
import jax.numpy as jnp
from jax import lax
from jax.experimental import pallas as pl
from jax.experimental.pallas import tpu as pltpu
from jax.sharding import PartitionSpec as P

TIME_STEP = 0.5
VISCOSITY = 0.05
MERIDIONAL = 0.25
HALF = 128
SUBLANES = 8
VMEM_LIMIT = 32 * 1024 * 1024
GROUP = 8
LOADS = 1


def latitudes(global_rows, row_total):
    latitude_angle = -0.5 * jnp.pi + (global_rows + 0.5) * jnp.pi / row_total
    return (jnp.cos(latitude_angle), jnp.sin(latitude_angle))


def flip(tiles):
    row = lax.broadcasted_iota(jnp.int32, tiles[0].shape, 0)
    for d in (4, 2, 1):
        keep = (row & d) == 0
        turned = list(tiles)
        for i in range(SUBLANES):
            if not i & d:
                a, b = tiles[i], tiles[i + d]
                turned[i] = jnp.where(keep, a, pltpu.roll(b, d, 0))
                turned[i + d] = jnp.where(keep, pltpu.roll(a, SUBLANES - d, 0), b)
        tiles = turned
    return tiles


def fetch_kernel(prog, tile, first, last, sems):
    fields, levels, rows, _ = prog.shape
    per_load = levels // LOADS
    loads = []
    for f in range(fields):
        for load in range(LOADS):
            some = pl.ds(load * per_load, per_load)
            loads.append(pltpu.make_async_copy(prog.at[f, some], tile.at[f, some], sems.at[f, load]))
            loads[-1].start()
    for f in range(fields):
        for l in range(levels):
            if l % per_load == 0:
                loads[f * LOADS + l // per_load].wait()
            c = f * levels + l
            last[c : c + 1, :] = tile[f, l, rows - 1 : rows, :]
            first[c : c + 1, :] = tile[f, l, 0:1, :]


def tendency_kernel(tile, zonal, coriolis, out, ends, stage, sems):
    _, levels, rows, width = tile.shape
    chans = 3 * levels
    payload = 2 * chans
    row_id = lax.broadcasted_iota(jnp.int32, (SUBLANES, width), 0)
    col_id = lax.broadcasted_iota(jnp.int32, (SUBLANES, width), 1)
    lane_id = lax.broadcasted_iota(jnp.int32, (SUBLANES, HALF), 1)
    first_row, last_row = row_id == 0, row_id == SUBLANES - 1
    first_col, last_col = col_id == 0, col_id == width - 1
    copies = []
    for j0 in range(0, rows, SUBLANES):
        j1 = j0 + SUBLANES
        zon, cor = zonal[j0:j1, :], coriolis[j0:j1, :]
        edge_rows = jnp.zeros((SUBLANES, HALF), jnp.float32)
        for l0 in range(0, levels, SUBLANES):
            tends = [[], [], []]
            for l in range(l0, l0 + SUBLANES):
                centre, dx, dy, sx = [], [], [], []
                for f in range(3):
                    c = f * levels + l
                    here = tile[f, l, j0:j1, :]
                    after = tile[f, l, j1 : j1 + 1, :] if j1 < rows else 0.0
                    before = tile[f, l, j0 - 1 : j0, :] if j0 else 0.0
                    e = jnp.where(last_col, 0.0, pltpu.roll(here, width - 1, 1))
                    w = jnp.where(first_col, 0.0, pltpu.roll(here, 1, 1))
                    n = jnp.where(last_row, after, pltpu.roll(here, SUBLANES - 1, 0))
                    s = jnp.where(first_row, before, pltpu.roll(here, 1, 0))
                    centre.append(here)
                    dx.append(e - w)
                    dy.append(n - s)
                    sx.append(e + w + n + s - 4.0 * here)
                    first = here[:, :HALF]
                    last = here[:, width - HALF :]
                    if c:
                        first = pltpu.roll(first, c, 1)
                    last = pltpu.roll(last, (chans + c + 1) % HALF, 1)
                    edge_rows = jnp.where(lane_id == c, first, jnp.where(lane_id == chans + c, last, edge_rows))
                tends[0].append(-zon * dx[2] + cor * centre[1] + VISCOSITY * sx[0])
                tends[1].append(-MERIDIONAL * dy[2] - cor * centre[0] + VISCOSITY * sx[1])
                tends[2].append(-zon * dx[0] - MERIDIONAL * dy[1])
            for f in range(3):
                for half in range(2):
                    at = (2 * f + half) * levels + l0
                    flipped = flip([value[:, half * HALF : (half + 1) * HALF] for value in tends[f]])
                    for k, value in enumerate(flipped):
                        j = j0 + k
                        stage[j, at : at + SUBLANES, :] = value
                        if j in (0, rows - 1):
                            ends[min(j, 1), at : at + SUBLANES, :] = value
        for k in range(SUBLANES):
            stage[j0 + k, payload:, :] = jnp.broadcast_to(edge_rows[k : k + 1, :], (SUBLANES, HALF))
        some = pl.ds(j0, SUBLANES)
        copies.append(pltpu.make_async_copy(stage.at[some], out.at[some], sems.at[j0 // SUBLANES]))
        copies[-1].start()
    for copy in copies:
        copy.wait()


def seam_kernel(ends, north, south, tend, out, stage, sems):
    del tend
    chans = south.shape[0]
    levels = chans // 3
    copies = []
    for at, beyond, sign in ((0, south, -1.0), (1, north, 1.0)):
        for half in range(2):
            lanes = slice(half * HALF, (half + 1) * HALF)
            u, v, h = (beyond[f * levels : (f + 1) * levels, lanes] for f in range(3))
            slope = sign * MERIDIONAL
            for f, term in enumerate((VISCOSITY * u, VISCOSITY * v - slope * h, -slope * v)):
                some = slice((2 * f + half) * levels, (2 * f + half + 1) * levels)
                stage[at, some, :] = ends[at, some, :] + term
        row = at * (out.shape[0] - 1)
        copies.append(pltpu.make_async_copy(stage.at[at], out.at[row, pl.ds(0, 2 * chans)], sems.at[at]))
        copies[-1].start()
    for copy in copies:
        copy.wait()


def split2(x):
    hi = x.astype(jnp.bfloat16)
    return hi, (x - hi.astype(jnp.float32)).astype(jnp.bfloat16)


def mix_operand(matrix):
    hi, lo = split2(matrix)
    return jnp.concatenate([hi, hi, lo], axis=1)


def pair_mix_operand(matrix):
    hi, lo = split2(matrix)
    none = jnp.zeros_like(hi)
    return jnp.concatenate(
        [
            jnp.concatenate([hi, hi, none, none], axis=1),
            jnp.concatenate([none, none, hi, hi], axis=1),
            jnp.concatenate([lo, none, none, none], axis=1),
            jnp.concatenate([none, none, lo, none], axis=1),
        ],
        axis=0,
    )


def filter_kernel(
    own_row, half_width, filter_mask, zonal, tend, matrices, out, halves, parts, seam, matrix, stage, matrix_sem, sems
):
    lev_parts, blocks, levels = out.shape[0], out.shape[1], out.shape[4]
    chans = 3 * levels
    payload = 2 * chans
    count = 2 * blocks
    both = lev_parts * chans
    row = own_row[0]
    fetch = pltpu.make_async_copy(matrices.at[row], matrix, matrix_sem)
    fetch.start()
    reach = half_width[row]
    whole = reach == count // 2
    norm = jnp.where(whole, count * HALF, 2 * HALF * reach + 1).astype(jnp.float32)
    filtered = filter_mask[row] == 1
    edge_gain = jnp.where(whole, 0.0, 1.0).astype(jnp.float32)

    for b in range(blocks):
        for part in range(lev_parts):
            at = b * lev_parts + part
            seam[at : at + 1, :] = tend[part, b, payload : payload + 1, :]
    columns = seam[...].T
    zon = zonal[row]
    u, v, h = (columns[f * levels : (f + 1) * levels] for f in range(3))
    from_east = jnp.concatenate([VISCOSITY * u - zon * h, VISCOSITY * v, -zon * u], axis=0)
    u, v, h = (columns[chans + f * levels : chans + (f + 1) * levels] for f in range(3))
    from_west = jnp.concatenate([VISCOSITY * u + zon * h, VISCOSITY * v, zon * u], axis=0)
    lane_id = lax.broadcasted_iota(jnp.int32, (levels, HALF), 1)
    window = jnp.zeros((both, HALF), jnp.float32)
    for g in range(count):
        b, half = divmod(g, 2)
        beyond = (b + 1) % blocks if half else (b + blocks - 1) % blocks
        terms, lane = (from_east, HALF - 1) if half else (from_west, 0)
        pieces = []
        for part in range(lev_parts):
            source = beyond * lev_parts + part
            for f in range(3):
                here = tend[part, b, (2 * f + half) * levels : (2 * f + half + 1) * levels, :]
                term = terms[f * levels : (f + 1) * levels, source : source + 1]
                pieces.append(here + jnp.where(lane_id == lane, term, 0.0))
        value = jnp.concatenate(pieces, axis=0)
        halves[g] = value
        inside = lax.rem(g + reach, count) < 2 * reach
        window = window + jnp.where(inside, 1.0, 0.0).astype(jnp.float32) * value

    src = lax.broadcasted_iota(jnp.int32, (2 * HALF, 2 * HALF), 0)
    dst = lax.broadcasted_iota(jnp.int32, (2 * HALF, 2 * HALF), 1)
    sums = jnp.where((src & (HALF - 1)) <= dst, 1.0, 0.0).astype(jnp.bfloat16)
    fetch.wait()
    mixer = pair_mix_operand(matrix[...])
    scale = TIME_STEP / norm
    total = jnp.dot(
        jnp.concatenate(split2(window), axis=1), sums, preferred_element_type=jnp.float32
    )[:, HALF:]

    def split_group(g0):
        for g in range(g0, g0 + GROUP):
            ahead = halves[lax.rem(g + reach, count)]
            behind = halves[lax.rem(g + count - reach, count)]
            hi, lo = split2(ahead - behind)
            parts[g * both : (g + 1) * both, :HALF] = hi
            parts[g * both : (g + 1) * both, HALF:] = lo

    def emit(b, steps):
        for half, step in enumerate(steps):
            for p in range(lev_parts):
                stage[p, b, 2, half] = step[p * chans + 2 * levels : (p + 1) * chans]
        step = jnp.concatenate(steps, axis=1)
        winds = []
        for f in range(2):
            winds += split2(
                jnp.concatenate(
                    [step[p * chans + f * levels : p * chans + (f + 1) * levels] for p in range(lev_parts)],
                    axis=0,
                )
            )
        mixed = jnp.dot(mixer, jnp.concatenate(winds, axis=0), preferred_element_type=jnp.float32)
        mixed = mixed[: 2 * lev_parts * levels] + mixed[2 * lev_parts * levels :]
        for f in range(2):
            for p in range(lev_parts):
                at = (f * lev_parts + p) * levels
                for half in range(2):
                    stage[p, b, f, half] = mixed[at : at + levels, half * HALF : (half + 1) * HALF]
        copy = pltpu.make_async_copy(stage.at[:, b], out.at[:, b], sems.at[b])
        copy.start()
        return copy

    @pl.when(filtered)
    def _():
        copies = []
        running = total
        split_group(0)
        for g0 in range(0, count, GROUP):
            if g0 + GROUP < count:
                split_group(g0 + GROUP)
            box = jnp.dot(parts[g0 * both : (g0 + GROUP) * both, :], sums, preferred_element_type=jnp.float32)
            for b in range(g0 // 2, (g0 + GROUP) // 2):
                steps = []
                for g in (2 * b, 2 * b + 1):
                    at = (g - g0) * both
                    behind = halves[lax.rem(g + count - reach, count)]
                    steps.append((box[at : at + both, :HALF] + running + edge_gain * behind) * scale)
                    running = running + box[at : at + both, HALF:]
                copies.append(emit(b, steps))
        for copy in copies:
            copy.wait()

    @pl.when(jnp.logical_not(filtered))
    def _():
        copies = [emit(b, [TIME_STEP * halves[2 * b], TIME_STEP * halves[2 * b + 1]]) for b in range(blocks)]
        for copy in copies:
            copy.wait()


def base_kernel(own_part, own, other, matrix, out):
    _, levels, rows, width = own.shape
    lower = own_part[0] == 0

    def by_row(ref, f, j0):
        flipped = [
            flip([ref[f, l0 + i, j0 : j0 + SUBLANES, :] for i in range(SUBLANES)])
            for l0 in range(0, levels, SUBLANES)
        ]
        return [jnp.concatenate([part[k] for part in flipped], axis=0) for k in range(SUBLANES)]

    for j0 in range(0, rows, SUBLANES):
        mine = [by_row(own, f, j0) for f in range(3)]
        theirs = [by_row(other, f, j0) for f in range(2)]
        for k in range(SUBLANES):
            j = j0 + k
            winds = []
            for f in range(2):
                a, b = mine[f][k], theirs[f][k]
                winds.append(jnp.concatenate([jnp.where(lower, a, b), jnp.where(lower, b, a)], axis=0))
            wind_hi, wind_lo = split2(jnp.concatenate(winds, axis=1))
            mixed = jnp.dot(
                mix_operand(matrix[j]),
                jnp.concatenate([wind_hi, wind_lo, wind_hi], axis=0),
                preferred_element_type=jnp.float32,
            )
            kept = jnp.where(lower, mixed[:levels], mixed[levels:])
            for f in range(2):
                out[j, f, 0] = kept[:, f * width : (f + 1) * width]
            out[j, 2, 0] = mine[2][k]


def finish_kernel(step, base, out, added, stage, in_sems, out_sems):
    fields, levels, rows, _ = out.shape
    pieces = [(f, l0) for f in range(fields) for l0 in range(0, levels, SUBLANES)]
    loads, copies = {}, []
    for n, (f, l0) in enumerate(pieces):
        some = pl.ds(l0, SUBLANES)
        for half in range(2):
            loads[f, l0, half] = pltpu.make_async_copy(
                base.at[:, f, half, some], added.at[:, f, half, some], in_sems.at[2 * n + half]
            )
            loads[f, l0, half].start()
    for n, (f, l0) in enumerate(pieces):
        some = slice(l0, l0 + SUBLANES)
        for half in range(2):
            loads[f, l0, half].wait()
            for j0 in range(0, rows, SUBLANES):
                flipped = flip(
                    [step[j0 + k, f, half, some, :] + added[j0 + k, f, half, some, :] for k in range(SUBLANES)]
                )
                for i, value in enumerate(flipped):
                    stage[f, l0 + i, j0 : j0 + SUBLANES, half * HALF : (half + 1) * HALF] = value
        some = pl.ds(l0, SUBLANES)
        copies.append(pltpu.make_async_copy(stage.at[f, some], out.at[f, some], out_sems.at[n]))
        copies[-1].start()
    for copy in copies:
        copy.wait()


def per_device(prognostic, half_width, filter_mask, column_inverse):
    fields, levels, rows, width = prognostic.shape
    lon_devices, lat_devices, lev_devices = (lax.axis_size(a) for a in ("lon", "lat", "lev"))
    lon_index, lat_index, lev_index = (lax.axis_index(a) for a in ("lon", "lat", "lev"))
    chans = fields * levels
    halves = width // HALF
    params = pltpu.CompilerParams(vmem_limit_bytes=VMEM_LIMIT)
    hbm = pl.BlockSpec(memory_space=pltpu.HBM)
    vmem = pl.BlockSpec(memory_space=pltpu.VMEM)

    def in_hbm(x):
        return pltpu.with_memory_space_constraint(x, pltpu.HBM)

    def in_vmem(x):
        return pltpu.with_memory_space_constraint(x, pltpu.VMEM)


    with jax.named_scope("fetch"):
        tile, first, last = pl.pallas_call(
            fetch_kernel,
            out_shape=(
                pltpu.VMEM(prognostic.shape, jnp.float32),
                pltpu.VMEM((chans, width), jnp.float32),
                pltpu.VMEM((chans, width), jnp.float32),
            ),
            in_specs=[hbm],
            out_specs=(vmem, vmem, vmem),
            scratch_shapes=[pltpu.SemaphoreType.DMA((fields, LOADS))],
            compiler_params=params,
        )(in_hbm(prognostic))
    north = lax.ppermute(first, "lat", [(i + 1, i) for i in range(lat_devices - 1)])
    south = lax.ppermute(last, "lat", [(i, i + 1) for i in range(lat_devices - 1)])
    other = lax.ppermute(prognostic[:2], "lev", [(0, 1), (1, 0)])

    global_rows = (lat_index * rows + jnp.arange(rows)).astype(jnp.float32)
    cosine, sine = latitudes(global_rows, rows * lat_devices)
    zonal = 0.25 / (cosine + 0.05)
    zonal_field = jnp.broadcast_to(zonal[:, None], (rows, width))
    coriolis_field = jnp.broadcast_to((0.5 * sine)[:, None], (rows, width))

    sent_rows = halves * chans + SUBLANES
    with jax.named_scope("tendencies"):
        tend, ends = pl.pallas_call(
            tendency_kernel,
            out_shape=(
                pltpu.HBM((rows, sent_rows, HALF), jnp.float32),
                pltpu.VMEM((2, halves * chans, HALF), jnp.float32),
            ),
            in_specs=[vmem, vmem, vmem],
            out_specs=(hbm, vmem),
            scratch_shapes=[
                pltpu.VMEM((rows, sent_rows, HALF), jnp.float32),
                pltpu.SemaphoreType.DMA((rows // SUBLANES,)),
            ],
            compiler_params=params,
        )(in_vmem(tile), in_vmem(zonal_field), in_vmem(coriolis_field))

    with jax.named_scope("seam_rows"):
        tend = pl.pallas_call(
            seam_kernel,
            out_shape=pltpu.HBM(tend.shape, jnp.float32),
            in_specs=[vmem, vmem, vmem, hbm],
            out_specs=hbm,
            input_output_aliases={3: 0},
            scratch_shapes=[pltpu.VMEM(ends.shape, jnp.float32), pltpu.SemaphoreType.DMA((2,))],
            compiler_params=params,
        )(in_vmem(ends), in_vmem(north), in_vmem(south), in_hbm(tend))

    whole_rows = lax.all_to_all(tend, ("lev", "lon"), 0, 0, tiled=True)

    own_row = (lev_index * lon_devices + lon_index).astype(jnp.int32).reshape(1)
    stepped_shape = (lev_devices, lon_devices, fields, halves, levels, HALF)
    count = halves * lon_devices
    both = lev_devices * chans
    with jax.named_scope("row_filter"):
        stepped = pl.pallas_call(
            filter_kernel,
            out_shape=pltpu.HBM(stepped_shape, jnp.float32),
            grid_spec=pltpu.PrefetchScalarGridSpec(
                num_scalar_prefetch=4,
                grid=(1,),
                in_specs=[vmem, hbm],
                out_specs=hbm,
                scratch_shapes=[
                    pltpu.VMEM((count, both, HALF), jnp.float32),
                    pltpu.VMEM((count * both, 2 * HALF), jnp.bfloat16),
                    pltpu.VMEM((HALF, HALF), jnp.float32),
                    pltpu.VMEM(column_inverse.shape[1:], jnp.float32),
                    pltpu.VMEM(stepped_shape, jnp.float32),
                    pltpu.SemaphoreType.DMA,
                    pltpu.SemaphoreType.DMA((lon_devices,)),
                ],
            ),
            compiler_params=params,
        )(
            own_row,
            half_width,
            filter_mask,
            zonal,
            in_vmem(whole_rows.reshape(lev_devices, lon_devices, sent_rows, HALF)),
            in_hbm(column_inverse),
        )

    returned = lax.all_to_all(
        stepped.reshape((rows,) + stepped_shape[2:]), ("lev", "lon"), 0, 0, tiled=True
    )

    with jax.named_scope("base"):
        base = pl.pallas_call(
            base_kernel,
            out_shape=pltpu.HBM(returned.shape, jnp.float32),
            grid_spec=pltpu.PrefetchScalarGridSpec(
                num_scalar_prefetch=1,
                grid=(halves,),
                in_specs=[
                    pl.BlockSpec((fields, levels, rows, HALF), lambda i, *_: (0, 0, 0, i)),
                    pl.BlockSpec((2, levels, rows, HALF), lambda i, *_: (0, 0, 0, i)),
                    pl.BlockSpec(column_inverse.shape, lambda i, *_: (0, 0, 0)),
                ],
                out_specs=pl.BlockSpec((rows, fields, 1, levels, HALF), lambda i, *_: (0, 0, i, 0, 0)),
            ),
            compiler_params=params,
        )(lev_index.astype(jnp.int32).reshape(1), prognostic, other, column_inverse)

    with jax.named_scope("finish"):
        return pl.pallas_call(
            finish_kernel,
            out_shape=jax.ShapeDtypeStruct(prognostic.shape, jnp.float32),
            in_specs=[vmem, hbm],
            out_specs=hbm,
            scratch_shapes=[
                pltpu.VMEM(returned.shape, jnp.float32),
                pltpu.VMEM(prognostic.shape, jnp.float32),
                pltpu.SemaphoreType.DMA((fields * halves * levels // SUBLANES,)),
                pltpu.SemaphoreType.DMA((fields * levels // SUBLANES,)),
            ],
            compiler_params=params,
        )(in_vmem(returned), in_hbm(base))


def solution(mesh):
    placed = (P(None, "lev", "lat", "lon"), P("lat"), P("lat"), P("lat", None, None))
    return jax.shard_map(
        per_device,
        mesh=mesh,
        in_specs=placed,
        out_specs=P(None, "lev", "lat", "lon"),
        check_vma=False,
    )
```
